32 devices in a mesh: groups: 2 (over x), weight: 16 (over z, y, core).
Axes of the slice: x: 2, y: 2, z: 4, core: 2. Of those that a mesh axis runs over, the one named last changes fastest.
Arguments:
- hidden: bfloat16 [128, 8192], P(('groups', 'weight')), parts along dimension 0, may hold values from -6 to 6
- norm_gain: float32 [8192], replicated, may hold values from 0.1 to 1.9
- in_weight: bfloat16 [8192, 2, 8192], P(None, None, 'weight'), may hold values from -0.0625 to 0.0625
- conv_weight: float32 [4, 8192], P(None, 'weight'), may hold values from -0.6 to 0.6
- conv_offset: float32 [8192], P('weight'), may hold values from -0.5 to 0.5
- coef_weight: bfloat16 [8192, 544], P('weight'), may hold values from -0.0625 to 0.0625
- step_weight: bfloat16 [512, 8192], P(None, 'weight'), may hold values from -0.25 to 0.25
- step_bias: float32 [8192], P('weight'), may hold values from -3 to 0.5
- log_rates: float32 [16, 8192], P(None, 'weight'), may hold values from 0 to 2.77
- skip_gain: float32 [8192], P('weight'), may hold values from 0.5 to 1.5
- out_weight: bfloat16 [8192, 8192], P('weight'), may hold values from -0.0625 to 0.0625
- ssm_state: bfloat16 [128, 16, 8192], P('groups', None, 'weight'), parts along dimension 0, may hold values from -6 to 6
- conv_state: bfloat16 [128, 3, 8192], P('groups', None, 'weight'), parts along dimension 0, may hold values from -6 to 6
- live_counts: int32 [32], P('groups'), parts along dimension 0, may hold values from 1 to 3, as said below
Outputs:
- mixed: bfloat16 [128, 8192], P(('groups', 'weight')), parts along dimension 0
- new_state: bfloat16 [128, 16, 8192], P('groups', None, 'weight'), parts along dimension 0
- new_conv: bfloat16 [128, 3, 8192], P('groups', None, 'weight'), parts along dimension 0
The draws below stay inside these ranges and needn't reach their ends.
There are 2 independent parts, one for each index of `groups`. The reference program is written for one: setup_inputs(seed, part) draws one part's arguments, and reference() takes and returns one part's arrays. A program takes and returns all parts, laid end to end along the dimension named above; an argument that names none is the same for every part. Nothing has to cross between parts.
Inputs may be any that keep to these rules, and one draw needn't show every extreme that they name: The live rows of a microbatch are its first live_counts rows; the most, 3, is reached by some microbatch.
All inputs are finite; a program needn't handle non-finite values.
Results may differ from the reference program's by a relative error of at most 0.0039.
Values may be sent and summed in bfloat16 or wider, within the bound.
No kernel may reach another device: no remote copies, remote signals or barrier semaphores. Data moves between devices by JAX's collectives and lax.ppermute only.
A program may use at most 64 MiB of HBM per device.

```python
import jax
import jax.numpy as jnp
from jax import lax

D = 8192
E = 8192
NSTATE = 16
DTR = 512
ROWS_DEV = 4
LIVE_MAX = 3
MICRO = 16
R = 64


def draw_live_counts(key, part):
    base = jax.random.fold_in(key, 11)
    first_key, second_key = jax.random.split(base)
    counts = jax.random.randint(first_key, (MICRO,), 1, LIVE_MAX + 1)
    chosen = jax.random.randint(second_key, (), 0, MICRO)
    filled = jnp.where(jnp.arange(MICRO) == chosen, LIVE_MAX, counts)
    return filled.astype(jnp.int32)


def block_scale(stream_key, dims, cuts, least, high):
    factor_of, own = 1.0, jax.random.fold_in(stream_key, 6)
    for axis_at, parts in cuts:
        draws = jnp.exp(jax.random.uniform(jax.random.fold_in(own, axis_at), (parts,), jnp.float32, least / len(cuts), high / len(cuts)))
        factor_of = factor_of * jnp.repeat(draws, dims[axis_at] // parts).reshape([-1 if axis == axis_at else 1 for axis in range(len(dims))])
    return factor_of


def centred(rng, shape, scale, limit, cuts=(), kind=jnp.bfloat16):
    result = scale * jax.random.normal(rng, shape, jnp.float32)
    if cuts:
        result = result * block_scale(rng, shape, cuts, -0.22, 0.18)
    return jnp.clip(result, -limit, limit).astype(kind)


def setup_inputs(seed: int = 0, part: int = 0) -> dict:
    arg_keys = jax.random.split(jax.random.key(seed), 15)
    part_keys = jax.random.split(jax.random.fold_in(arg_keys[14], part), 15)
    hidden = centred(part_keys[0], (R, D), 1.0, 6.0, ((0, 16),))
    norm_gain = jnp.clip(1.0 + 0.18 * jax.random.normal(arg_keys[1], (D,), jnp.float32), 0.1, 1.9)
    in_weight = centred(arg_keys[2], (D, 2, E), D ** -0.5, 0.0625, ((2, 16),))
    conv_weight = jnp.clip(jax.random.uniform(arg_keys[3], (4, E), jnp.float32, -0.6, 0.6) * block_scale(arg_keys[3], (4, E), ((1, 16),), -0.4, 0.0), -0.6, 0.6)
    conv_offset = jnp.clip(jax.random.uniform(arg_keys[4], (E,), jnp.float32, -0.5, 0.5) * block_scale(arg_keys[4], (E,), ((0, 16),), -0.4, 0.0), -0.5, 0.5)
    coef_weight = centred(arg_keys[5], (E, DTR + 2 * NSTATE), E ** -0.5, 0.0625, ((0, 16),))
    step_weight = centred(arg_keys[6], (DTR, E), DTR ** -0.5, 0.25, ((1, 16),))
    step_bias = jnp.clip(-3.0 + 3.5 * jax.random.uniform(arg_keys[7], (E,), jnp.float32) ** block_scale(arg_keys[7], (E,), ((0, 16),), -0.2, 0.2), -3.0, 0.5)
    log_rates = jnp.clip(2.77 * jax.random.uniform(arg_keys[8], (NSTATE, E), jnp.float32) ** block_scale(arg_keys[8], (NSTATE, E), ((1, 16),), -0.2, 0.2), 0.0, 2.77)
    skip_gain = jnp.clip(0.5 + 1.0 * jax.random.uniform(arg_keys[9], (E,), jnp.float32) ** block_scale(arg_keys[9], (E,), ((0, 16),), -0.2, 0.2), 0.5, 1.5)
    out_weight = centred(arg_keys[10], (E, D), E ** -0.5, 0.0625, ((0, 16),))
    ssm_state = centred(part_keys[11], (R, NSTATE, E), 1.0, 6.0, ((2, 16),))
    conv_state = centred(part_keys[12], (R, 3, E), 1.0, 6.0, ((2, 16),))
    live_counts = draw_live_counts(jax.random.fold_in(jax.random.fold_in(arg_keys[14], part), 71), part)
    return {"hidden": hidden, "norm_gain": norm_gain, "in_weight": in_weight, "conv_weight": conv_weight, "conv_offset": conv_offset, "coef_weight": coef_weight, "step_weight": step_weight, "step_bias": step_bias, "log_rates": log_rates, "skip_gain": skip_gain, "out_weight": out_weight, "ssm_state": ssm_state, "conv_state": conv_state, "live_counts": live_counts}


def rms_normed(hidden, norm_gain):
    wide = hidden.astype(jnp.float32)
    factor = lax.rsqrt(lax.optimization_barrier(jnp.mean(wide * wide, axis=-1, keepdims=True)) + 1e-05)
    return (wide * factor * norm_gain).astype(jnp.bfloat16)

def reference(hidden, norm_gain, in_weight, conv_weight, conv_offset, coef_weight, step_weight, step_bias, log_rates, skip_gain, out_weight, ssm_state, conv_state, live_counts):
    total_rows = hidden.shape[0]
    row_ids = jnp.arange(total_rows, dtype=jnp.int32)
    per_row = jnp.repeat(live_counts, ROWS_DEV, total_repeat_length=total_rows)
    alive = row_ids % ROWS_DEV < per_row
    normed = rms_normed(hidden, norm_gain)
    conv_input = jnp.dot(normed, in_weight[:, 0, :], preferred_element_type=jnp.float32).astype(jnp.bfloat16)
    gate_branch = jnp.dot(normed, in_weight[:, 1, :], preferred_element_type=jnp.float32)
    window = jnp.concatenate([conv_state, conv_input[:, None, :]], axis=1)
    convolved = lax.optimization_barrier(jnp.sum(window.astype(jnp.float32) * conv_weight[None], axis=1)) + conv_offset
    mixed_x = jax.nn.silu(convolved).astype(jnp.bfloat16)
    low_rank = jnp.dot(mixed_x, coef_weight, preferred_element_type=jnp.float32)
    step_low = low_rank[:, :DTR].astype(jnp.bfloat16)
    in_coef = low_rank[:, DTR:DTR + NSTATE]
    out_coef = low_rank[:, DTR + NSTATE:]
    step_size = jax.nn.softplus(jnp.dot(step_low, step_weight, preferred_element_type=jnp.float32) + step_bias)
    x_wide = mixed_x.astype(jnp.float32)
    decays = jnp.exp(-step_size[:, None, :] * jnp.exp(log_rates)[None])
    old_state = ssm_state.astype(jnp.float32)
    updated = decays * old_state + step_size[:, None, :] * in_coef[:, :, None] * x_wide[:, None, :]
    readout = lax.optimization_barrier(jnp.sum(out_coef[:, :, None] * updated, axis=1)) + skip_gain * x_wide
    gated_out = jnp.where(alive[:, None], readout * jax.nn.silu(gate_branch), 0.0).astype(jnp.bfloat16)
    mixer_term = jnp.dot(gated_out, out_weight, preferred_element_type=jnp.float32)
    mixed = (hidden.astype(jnp.float32) + mixer_term).astype(jnp.bfloat16)
    new_state = jnp.where(alive[:, None, None], updated, old_state).astype(jnp.bfloat16)
    new_conv = jnp.where(alive[:, None, None], window[:, 1:], conv_state)
    return (mixed, new_state, new_conv)
```

```python
import jax
import jax.numpy as jnp
from jax import lax
from jax.experimental import pallas as pl
from jax.experimental.pallas import tpu as pltpu
from jax.sharding import PartitionSpec as P

NSTATE = 16
DTR = 512
LIVE_MAX = 3
TAPS = 4
BF16 = jnp.bfloat16
F32 = jnp.float32


def gather_phases(devices):
    phases, high = [], devices
    while high > 2:
        if high >= 8:
            step = high // 4
            phases.append((step, 2 * step, 3 * step))
            high //= 4
        else:
            phases.append((high // 2,))
            high //= 2
    phases.append((1,))
    return phases


def sum_phases(devices):
    phases, step = [], 2
    while step < devices:
        if 4 * step <= devices:
            phases.append((step, 2 * step, 3 * step))
            step *= 4
        else:
            phases.append((step,))
            step *= 2
    return phases


def swap(value, shift, devices):
    return lax.ppermute(value, "weight", [(i, i ^ shift) for i in range(devices)])


def rms_normed(hidden, norm_gain):
    wide = hidden.astype(F32)
    factor = lax.rsqrt(jnp.mean(wide * wide, axis=-1, keepdims=True) + 1e-05)
    return (wide * factor * norm_gain).astype(BF16)


def silu(v):
    return v / (1.0 + jnp.exp(-v))


def softplus(v):
    return jnp.maximum(v, 0.0) + jnp.log1p(jnp.exp(-jnp.abs(v)))


def conv_kernel(
    core_ref,
    both_ref,
    place_ref,
    alive_ref,
    conv_ref,
    taps_ref,
    offset_ref,
    coef_ref,
    keep_ref,
    send_ref,
    mixed_ref,
    gate_ref,
    new_conv_ref,
    low_ref,
):
    place = place_ref[...]
    fresh = jnp.dot(place, both_ref[0].astype(BF16), preferred_element_type=F32)
    alive = alive_ref[...] > 0.0
    states = [conv_ref[k].astype(F32) for k in range(TAPS - 1)] + [fresh]
    total = states[0] * taps_ref[0:1, :]
    for k in range(1, TAPS):
        total = total + states[k] * taps_ref[k : k + 1, :]
    mixed = silu(total + offset_ref[...]).astype(BF16)
    mixed_ref[...] = mixed
    low_ref[...] = lax.dot_general(
        mixed, coef_ref[...], (((1,), (1,)), ((), ())), preferred_element_type=F32
    )
    half = keep_ref.shape[0]
    core = core_ref[0]
    keep_ref[...] = low_ref[pl.ds(pl.multiple_of(core * half, half), half), :]
    send_ref[...] = low_ref[pl.ds(pl.multiple_of((1 - core) * half, half), half), :]
    for k in range(TAPS - 1):
        new_conv_ref[k] = jnp.where(alive, states[k + 1], states[k]).astype(BF16)
    gate_ref[...] = jnp.dot(
        place.astype(F32),
        silu(both_ref[1]),
        precision=lax.Precision.HIGHEST,
        preferred_element_type=F32,
    )


def state_kernel(
    core_ref,
    mine_ref,
    other_ref,
    mixed_ref,
    gate_ref,
    alive_ref,
    step_weight_ref,
    bias_ref,
    rates_ref,
    skip_ref,
    state_ref,
    pick_ref,
    out_weight_ref,
    new_state_ref,
    keep_ref,
    send_ref,
    low_ref,
    read_ref,
    weight_ref,
    sems,
):
    chunks, depth, width = weight_ref.shape
    copies = [
        pltpu.make_async_copy(
            out_weight_ref.at[:, pl.ds(c * width, width)], weight_ref.at[c], sems.at[c]
        )
        for c in range(chunks)
    ]
    for copy in copies:
        copy.start()
    half = mine_ref.shape[0]
    rows = 2 * half
    core = core_ref[0]
    low_ref[pl.ds(pl.multiple_of(core * half, half), half), :] = mine_ref[...]
    low_ref[pl.ds(pl.multiple_of((1 - core) * half, half), half), :] = other_ref[...]
    step_size = softplus(
        jnp.dot(
            low_ref[:, :DTR].astype(BF16), step_weight_ref[...], preferred_element_type=F32
        )
        + bias_ref[...]
    )
    coefs = low_ref[:, DTR:].T
    x_wide = mixed_ref[...].astype(F32)
    driven = step_size * x_wide
    rates = -jnp.exp(rates_ref[...])
    alive = alive_ref[...]
    for r in range(rows):
        old = state_ref[r]
        wide = old.astype(F32)
        updated = (
            jnp.exp(step_size[r : r + 1, :] * rates) * wide
            + coefs[:NSTATE, r : r + 1] * driven[r : r + 1, :]
        )
        read_ref[r : r + 1, :] = jnp.sum(
            coefs[NSTATE:, r : r + 1] * updated, axis=0, keepdims=True
        )
        new_state_ref[r] = jnp.where(alive[r : r + 1, :] > 0.0, updated, wide).astype(BF16)
    readout = read_ref[...] + skip_ref[...] * x_wide
    gated = jnp.where(alive > 0.0, readout * gate_ref[...], 0.0).astype(BF16)
    picked = jnp.dot(pick_ref[...], gated, preferred_element_type=F32).astype(BF16)
    kept = keep_ref.shape[0]
    for c in range(chunks):
        copies[c].wait()
        part = jnp.dot(picked, weight_ref[c], preferred_element_type=F32)
        keep_ref[:, c * width : (c + 1) * width] = part[:kept]
        send_ref[:, c * width : (c + 1) * width] = part[kept:].astype(send_ref.dtype)


def vmem(count):
    return [pl.BlockSpec(memory_space=pltpu.VMEM)] * count


def body(
    hidden,
    norm_gain,
    in_weight,
    conv_weight,
    conv_offset,
    coef_weight,
    step_weight,
    step_bias,
    log_rates,
    skip_gain,
    out_weight,
    ssm_state,
    conv_state,
    live_counts,
):
    devices = lax.axis_size("weight")
    rows_dev, width = hidden.shape
    rows = devices * rows_dev
    kept = devices * LIVE_MAX
    channels = in_weight.shape[2]
    low_width = coef_weight.shape[1]
    index = lax.axis_index("weight")
    core = (index % 2).reshape(1)
    phases = gather_phases(devices)
    order = [0]
    for phase in phases:
        order = order + [o ^ s for s in phase for o in order]

    blocks = jnp.bitwise_xor(index, jnp.array(order, jnp.int32))
    row_of = (blocks[:, None] * rows_dev + jnp.arange(rows_dev)[None]).reshape(-1)
    place = (jnp.arange(rows)[:, None] == row_of[None]).astype(BF16)
    kept_of = (blocks[:, None] * rows_dev + jnp.arange(LIVE_MAX)[None]).reshape(-1)
    pick = (kept_of[:, None] == jnp.arange(rows)[None]).astype(BF16)
    alive = (
        (jnp.arange(rows_dev)[None] < live_counts[:, None]).astype(F32).reshape(rows, 1)
    )

    gathered = rms_normed(hidden, norm_gain)
    for phase in phases:
        gathered = jnp.concatenate(
            [gathered] + [swap(gathered, s, devices) for s in phase], axis=0
        )
    both = jnp.einsum("rd,dbc->brc", gathered, in_weight, preferred_element_type=F32)

    keep, send, mixed_x, gate, new_conv = pl.pallas_call(
        conv_kernel,
        out_shape=(
            jax.ShapeDtypeStruct((rows // 2, low_width), F32),
            jax.ShapeDtypeStruct((rows // 2, low_width), F32),
            jax.ShapeDtypeStruct((rows, channels), BF16),
            jax.ShapeDtypeStruct((rows, channels), F32),
            jax.ShapeDtypeStruct((TAPS - 1, rows, channels), BF16),
        ),
        in_specs=[pl.BlockSpec(memory_space=pltpu.SMEM)] + vmem(7),
        out_specs=tuple(vmem(5)),
        scratch_shapes=[pltpu.VMEM((rows, low_width), F32)],
        compiler_params=pltpu.CompilerParams(vmem_limit_bytes=16 * 1024 * 1024),
    )(
        core,
        both,
        place,
        alive,
        conv_state.transpose(1, 0, 2),
        conv_weight,
        conv_offset.reshape(1, channels),
        coef_weight.T,
    )

    low = keep + swap(send, 1, devices)
    for phase in sum_phases(devices):
        low = low + sum(swap(low, s, devices) for s in phase)
    other = swap(low, 1, devices)

    chunks = 4
    new_state, keep, send = pl.pallas_call(
        state_kernel,
        out_shape=(
            jax.ShapeDtypeStruct(ssm_state.shape, BF16),
            jax.ShapeDtypeStruct((kept // 2, width), F32),
            jax.ShapeDtypeStruct((kept // 2, width), F32),
        ),
        in_specs=[pl.BlockSpec(memory_space=pltpu.SMEM)]
        + vmem(11)
        + [pl.BlockSpec(memory_space=pl.ANY)],
        out_specs=tuple(vmem(3)),
        scratch_shapes=[
            pltpu.VMEM((rows, low_width), F32),
            pltpu.VMEM((rows, channels), F32),
            pltpu.VMEM((chunks, channels, width // chunks), BF16),
            pltpu.SemaphoreType.DMA((chunks,)),
        ],
        compiler_params=pltpu.CompilerParams(vmem_limit_bytes=32 * 1024 * 1024),
    )(
        core,
        low,
        other,
        mixed_x,
        gate,
        alive,
        step_weight,
        step_bias.reshape(1, channels),
        log_rates,
        skip_gain.reshape(1, channels),
        ssm_state,
        pick,
        out_weight,
    )

    total = keep + swap(send, 1, devices)
    for phase in reversed(phases[:-1]):
        parts = jnp.split(total, len(phase) + 1, axis=0)
        total = parts[0]
        for part, s in zip(parts[1:], phase):
            total = total + swap(part.astype(BF16), s, devices).astype(F32)
    own = (hidden[:LIVE_MAX].astype(F32) + total).astype(BF16)
    mixed = jnp.concatenate([own, hidden[LIVE_MAX:]], axis=0)
    return (mixed, new_state, new_conv.transpose(1, 0, 2))


def solution(mesh):
    in_specs = (
        P(("groups", "weight"), None),
        P(),
        P(None, None, "weight"),
        P(None, "weight"),
        P("weight"),
        P("weight", None),
        P(None, "weight"),
        P("weight"),
        P(None, "weight"),
        P("weight"),
        P("weight", None),
        P("groups", None, "weight"),
        P("groups", None, "weight"),
        P("groups"),
    )
    out_specs = (
        P(("groups", "weight"), None),
        P("groups", None, "weight"),
        P("groups", None, "weight"),
    )
    return jax.shard_map(body, mesh=mesh, in_specs=in_specs, out_specs=out_specs, check_vma=False)
```

```python
import functools

import jax
import jax.numpy as jnp
from jax import lax
from jax.experimental import pallas as pl
from jax.experimental.pallas import tpu as pltpu
from jax.sharding import PartitionSpec as P

NSTATE = 16
DTR = 512
LIVE_MAX = 3
TAPS = 4
LANES = 128
MIB = 1024 * 1024
BF16 = jnp.bfloat16
F32 = jnp.float32


def gather_phases(devices):
    phases, high = [], devices
    while high > 2:
        if high >= 8:
            step = high // 4
            phases.append((step, 2 * step, 3 * step))
            high //= 4
        else:
            phases.append((high // 2,))
            high //= 2
    phases.append((1,))
    return phases


def sum_phases(devices):
    phases, step = [], 2
    while step < devices:
        if 4 * step <= devices:
            phases.append((step, 2 * step, 3 * step))
            step *= 4
        else:
            phases.append((step,))
            step *= 2
    return phases


def swap(value, shift, devices):
    return lax.ppermute(value, "weight", [(i, i ^ shift) for i in range(devices)])


def silu(v):
    return v / (1.0 + jnp.exp(-v))


def softplus(v):
    return jnp.maximum(v, 0.0) + jnp.log1p(jnp.exp(-jnp.abs(v)))


def vmem(count):
    return [pl.BlockSpec(memory_space=pltpu.VMEM)] * count


def shape(dims, kind=F32):
    return jax.ShapeDtypeStruct(dims, kind)


def call(kernel, outs, operands, scalars=0, far=0, scratch=(), limit=8):
    many = isinstance(outs, tuple)
    return pl.pallas_call(
        kernel,
        out_shape=outs,
        in_specs=[pl.BlockSpec(memory_space=pltpu.SMEM)] * scalars
        + vmem(len(operands) - scalars - far)
        + [pl.BlockSpec(memory_space=pl.ANY)] * far,
        out_specs=tuple(vmem(len(outs))) if many else vmem(1)[0],
        scratch_shapes=list(scratch),
        compiler_params=pltpu.CompilerParams(vmem_limit_bytes=limit * MIB),
    )(*operands)


def fold(wide, folded_ref):
    rows, pieces = wide.shape[0], wide.shape[1] // LANES
    for c in range(pieces):
        folded_ref[pl.ds(c, rows, stride=pieces), :] = wide[:, c * LANES : (c + 1) * LANES]


def norm_kernel(far_hidden_ref, far_gain_ref, out_ref, fold_ref, hidden_ref, gain_ref, sems):
    copies = [
        pltpu.make_async_copy(far_hidden_ref, hidden_ref, sems.at[0]),
        pltpu.make_async_copy(far_gain_ref, gain_ref, sems.at[1]),
    ]
    for copy in copies:
        copy.start()
    for copy in copies:
        copy.wait()
    wide = hidden_ref[...].astype(F32)[:LIVE_MAX]
    factor = lax.rsqrt(jnp.mean(wide * wide, axis=-1, keepdims=True) + 1e-05)
    fold(wide * factor * gain_ref[...], fold_ref)
    out_ref[...] = fold_ref[...].astype(BF16)


def join_kernel(count, *refs):
    start = 0
    for ref in refs[:count]:
        refs[-1][start : start + ref.shape[0]] = ref[...]
        start += ref.shape[0]


def join(parts, after=()):
    rows = sum(part.shape[0] for part in parts)
    return call(
        functools.partial(join_kernel, len(parts)),
        shape((rows, parts[0].shape[1]), parts[0].dtype),
        (*parts, *after),
        far=len(after),
    )


def unfold_kernel(mine_ref, other_ref, out_ref, fold_ref):
    half = mine_ref.shape[0]
    fold_ref[:half] = mine_ref[...].astype(F32)
    fold_ref[half:] = other_ref[...].astype(F32)
    rows, pieces = out_ref.shape[0], out_ref.shape[1] // LANES
    for c in range(pieces):
        out_ref[:, c * LANES : (c + 1) * LANES] = fold_ref[
            pl.ds(c, rows, stride=pieces), :
        ].astype(BF16)


def load_kernel(far_ref, out_ref, sem):
    copy = pltpu.make_async_copy(far_ref, out_ref, sem)
    copy.start()
    copy.wait()


def load(array, limit):
    return pl.pallas_call(
        load_kernel,
        out_shape=pltpu.VMEM(array.shape, array.dtype),
        in_specs=[pl.BlockSpec(memory_space=pl.ANY)],
        out_specs=vmem(1)[0],
        scratch_shapes=[pltpu.SemaphoreType.DMA],
        compiler_params=pltpu.CompilerParams(vmem_limit_bytes=limit * MIB),
    )(array)


def add_kernel(count, *refs):
    total = refs[0][...]
    for ref in refs[1:count]:
        total = total + ref[...]
    refs[-1][...] = total


def conv_kernel(
    live_ref,
    both_ref,
    spot_ref,
    conv_ref,
    taps_ref,
    offset_ref,
    coef_ref,
    keep_ref,
    send_ref,
    mixed_ref,
    gate_ref,
    new_conv_ref,
    low_ref,
    alive_ref,
):
    index = lax.axis_index("weight")
    blocks = live_ref.shape[0]
    rows = conv_ref.shape[1]
    rows_dev = rows // blocks
    kept = mixed_ref.shape[0]
    block = jnp.bitwise_xor(spot_ref[0:1, :], index)
    turn = spot_ref[1:2, :]

    def places(height, span):
        line = lax.broadcasted_iota(jnp.int32, (height, kept), 0)
        return jnp.where(line == block * span + turn, 1.0, 0.0)

    fresh = jnp.dot(
        places(rows, rows_dev).astype(BF16),
        both_ref[0].astype(BF16),
        preferred_element_type=F32,
    )
    row_iota = lax.broadcasted_iota(jnp.int32, (rows_dev, 128), 0)
    for b in range(blocks):
        alive_ref[b * rows_dev : (b + 1) * rows_dev, :] = jnp.where(
            row_iota < live_ref[b], 1.0, 0.0
        )
    alive = alive_ref[:, 0:1] > 0.0
    states = [conv_ref[k].astype(F32) for k in range(TAPS - 1)] + [fresh]
    total = states[0] * taps_ref[0:1, :]
    for k in range(1, TAPS):
        total = total + states[k] * taps_ref[k : k + 1, :]
    mixed = silu(total + offset_ref[...]).astype(BF16)
    line = lax.broadcasted_iota(jnp.int32, (kept, rows), 0)
    column = lax.broadcasted_iota(jnp.int32, (kept, rows), 1)
    chosen = (line // LIVE_MAX) * rows_dev + line % LIVE_MAX == column
    mixed = jnp.dot(
        jnp.where(chosen, 1.0, 0.0).astype(BF16), mixed, preferred_element_type=F32
    ).astype(BF16)
    mixed_ref[...] = mixed
    low_ref[...] = lax.dot_general(
        mixed, coef_ref[...], (((1,), (1,)), ((), ())), preferred_element_type=F32
    )
    half = keep_ref.shape[0]
    core = index % 2
    keep_ref[...] = low_ref[pl.ds(pl.multiple_of(core * half, 8), half), :]
    send_ref[...] = low_ref[pl.ds(pl.multiple_of((1 - core) * half, 8), half), :]
    for k in range(TAPS - 1):
        new_conv_ref[k] = jnp.where(alive, states[k + 1], states[k]).astype(BF16)
    gate_ref[...] = jnp.dot(
        places(kept, LIVE_MAX),
        silu(both_ref[1]),
        precision=lax.Precision.HIGHEST,
        preferred_element_type=F32,
    )


def state_kernel(
    live_ref,
    mine_ref,
    other_ref,
    spot_ref,
    mixed_ref,
    gate_ref,
    step_weight_ref,
    bias_ref,
    rates_ref,
    skip_ref,
    state_ref,
    out_weight_ref,
    new_state_ref,
    keep_ref,
    send_ref,
    low_ref,
    read_ref,
    alive_ref,
):
    index = lax.axis_index("weight")
    blocks = live_ref.shape[0]
    rows_dev = state_ref.shape[0] // blocks
    kept = mixed_ref.shape[0]
    half = mine_ref.shape[0]
    core = index % 2
    low_ref[pl.ds(pl.multiple_of(core * half, 8), half), :] = mine_ref[...]
    low_ref[pl.ds(pl.multiple_of((1 - core) * half, 8), half), :] = other_ref[...]
    step_size = softplus(
        jnp.dot(
            low_ref[:, :DTR].astype(BF16), step_weight_ref[...], preferred_element_type=F32
        )
        + bias_ref[...]
    )
    coefs = low_ref[:, DTR:].T
    x_wide = mixed_ref[...].astype(F32)
    driven = step_size * x_wide
    rates = -jnp.exp(rates_ref[...])
    for b in range(blocks):
        for t in range(LIVE_MAX):
            r = b * LIVE_MAX + t
            wide = state_ref[b * rows_dev + t].astype(F32)
            updated = (
                jnp.exp(step_size[r : r + 1, :] * rates) * wide
                + coefs[:NSTATE, r : r + 1] * driven[r : r + 1, :]
            )
            read_ref[r : r + 1, :] = jnp.sum(
                coefs[NSTATE:, r : r + 1] * updated, axis=0, keepdims=True
            )
            live = t < live_ref[b]
            alive_ref[r : r + 1, :] = jnp.full((1, 128), jnp.where(live, 1.0, 0.0))
            new_state_ref[b * rows_dev + t] = jnp.where(live, updated, wide).astype(BF16)
        for t in range(LIVE_MAX, rows_dev):
            new_state_ref[b * rows_dev + t] = state_ref[b * rows_dev + t]
    readout = read_ref[...] + skip_ref[...] * x_wide
    gated = jnp.where(alive_ref[:, 0:1] > 0.0, readout * gate_ref[...], 0.0).astype(BF16)
    block = jnp.bitwise_xor(spot_ref[:, 0:1], index)
    column = lax.broadcasted_iota(jnp.int32, (kept, kept), 1)
    pick = jnp.where(column == block * LIVE_MAX + spot_ref[:, 1:2], 1.0, 0.0).astype(BF16)
    picked = jnp.dot(pick, gated, preferred_element_type=F32).astype(BF16)
    width = out_weight_ref.shape[1] // 4
    for c in range(4):
        cols = slice(c * width, (c + 1) * width)
        part = jnp.dot(picked, out_weight_ref[:, cols], preferred_element_type=F32)
        keep_ref[:, cols] = part[: kept // 2]
        send_ref[:, cols] = part[kept // 2 :].astype(send_ref.dtype)


def first_sum_kernel(keep_ref, got_ref, *refs):
    outs, fold_ref = refs[:-1], refs[-1]
    fold(keep_ref[...] + got_ref[...].astype(F32), fold_ref)
    size = outs[0].shape[0]
    for k, out in enumerate(outs):
        out[...] = fold_ref[k * size : (k + 1) * size].astype(out.dtype)


def next_sum_kernel(count, *refs):
    parts, outs = refs[:count], refs[count:]
    size = outs[0].shape[0]
    for k, out in enumerate(outs):
        rows = slice(k * size, (k + 1) * size)
        total = parts[0][rows]
        for part in parts[1:]:
            total = total + part[rows].astype(F32)
        out[...] = total.astype(out.dtype)


def last_sum_kernel(*refs):
    hidden_ref, parts, out_ref, fold_ref = refs[0], refs[1:-2], refs[-2], refs[-1]
    total = parts[0][...]
    for part in parts[1:]:
        total = total + part[...].astype(F32)
    fold_ref[...] = total
    pieces = out_ref.shape[1] // LANES
    for c in range(pieces):
        span = slice(c * LANES, (c + 1) * LANES)
        wide = hidden_ref[:, span].astype(F32)
        own = wide[:LIVE_MAX] + fold_ref[pl.ds(c, LIVE_MAX, stride=pieces), :]
        out_ref[:, span] = jnp.concatenate([own, wide[LIVE_MAX:]], axis=0).astype(BF16)


def body(
    hidden,
    norm_gain,
    in_weight,
    conv_weight,
    conv_offset,
    coef_weight,
    step_weight,
    step_bias,
    log_rates,
    skip_gain,
    out_weight,
    ssm_state,
    conv_state,
    live_counts,
):
    devices = lax.axis_size("weight")
    rows_dev, width = hidden.shape
    rows = devices * rows_dev
    kept = devices * LIVE_MAX
    channels = in_weight.shape[2]
    low_width = coef_weight.shape[1]
    phases = gather_phases(devices)
    order = [0]
    for phase in phases:
        order = order + [o ^ s for s in phase for o in order]
    spots = jnp.array(
        [[o for o in order for _ in range(LIVE_MAX)], list(range(LIVE_MAX)) * devices],
        jnp.int32,
    )
    pieces = width // LANES
    slab = LIVE_MAX * pieces

    gathered = call(
        norm_kernel,
        pltpu.VMEM((slab, LANES), BF16),
        (hidden, norm_gain.reshape(1, width)),
        far=2,
        scratch=[
            pltpu.VMEM((slab, LANES), F32),
            pltpu.VMEM(hidden.shape, BF16),
            pltpu.VMEM((1, width), F32),
            pltpu.SemaphoreType.DMA((2,)),
        ],
        limit=60,
    )
    for k, phase in enumerate(phases[:-1]):
        after = ()
        if k == len(phases) - 2:
            near_weight = load(in_weight, 34)
            after = (near_weight,)
        gathered = join([gathered] + [swap(gathered, s, devices) for s in phase], after)
    normed = call(
        unfold_kernel,
        shape((kept, width), BF16),
        (gathered, swap(gathered, 1, devices)),
        scratch=[pltpu.VMEM((kept * pieces, LANES), F32)],
        limit=12,
    )
    both = jnp.einsum("rd,dbc->brc", normed, near_weight, preferred_element_type=F32)

    keep, send, mixed_x, gate, new_conv = call(
        conv_kernel,
        (
            shape((kept // 2, low_width)),
            shape((kept // 2, low_width)),
            shape((kept, channels), BF16),
            shape((kept, channels)),
            shape((TAPS - 1, rows, channels), BF16),
        ),
        (
            live_counts,
            both,
            spots,
            conv_state.transpose(1, 0, 2),
            conv_weight,
            conv_offset.reshape(1, channels),
            coef_weight.T,
        ),
        scalars=1,
        scratch=[pltpu.VMEM((kept, low_width), F32), pltpu.VMEM((rows, 128), F32)],
        limit=16,
    )

    def add(*parts, after=()):
        return call(
            functools.partial(add_kernel, len(parts)),
            shape(parts[0].shape),
            (*parts, *after),
            far=len(after),
        )

    low = add(keep, swap(send, 1, devices))
    exchanges = sum_phases(devices)
    for k, phase in enumerate(exchanges):
        after = ()
        if k == len(exchanges) - 1:
            near_out = load(out_weight, 50)
            after = (near_out,)
        low = add(low, *[swap(low, s, devices) for s in phase], after=after)
    other = swap(low, 1, devices)

    new_state, keep, send = call(
        state_kernel,
        (
            shape(ssm_state.shape, BF16),
            shape((kept // 2, width)),
            shape((kept // 2, width)),
        ),
        (
            live_counts,
            low,
            other,
            spots.T,
            mixed_x,
            gate,
            step_weight,
            step_bias.reshape(1, channels),
            log_rates,
            skip_gain.reshape(1, channels),
            ssm_state,
            near_out,
        ),
        scalars=1,
        scratch=[
            pltpu.VMEM((kept, low_width), F32),
            pltpu.VMEM((kept, channels), F32),
            pltpu.VMEM((kept, 128), F32),
        ],
        limit=32,
    )

    scatter = list(reversed(phases[:-1]))
    total, kernel = (keep, swap(send, 1, devices)), first_sum_kernel
    size = kept // 2 * pieces
    scratch = [pltpu.VMEM((size, LANES), F32)]
    for phase in scatter:
        size //= len(phase) + 1
        parts = call(
            kernel,
            (shape((size, LANES)),) + (shape((size, LANES), BF16),) * len(phase),
            total,
            scratch=scratch,
        )
        total = (parts[0],) + tuple(swap(p, s, devices) for p, s in zip(parts[1:], phase))
        kernel, scratch = functools.partial(next_sum_kernel, len(total)), ()
    mixed = call(
        last_sum_kernel,
        shape(hidden.shape, BF16),
        (hidden,) + total,
        scratch=[pltpu.VMEM((slab, LANES), F32)],
    )
    return (mixed, new_state, new_conv.transpose(1, 0, 2))


def solution(mesh):
    in_specs = (
        P(("groups", "weight"), None),
        P(),
        P(None, None, "weight"),
        P(None, "weight"),
        P("weight"),
        P("weight", None),
        P(None, "weight"),
        P("weight"),
        P(None, "weight"),
        P("weight"),
        P("weight", None),
        P("groups", None, "weight"),
        P("groups", None, "weight"),
        P("groups"),
    )
    out_specs = (
        P(("groups", "weight"), None),
        P("groups", None, "weight"),
        P("groups", None, "weight"),
    )
    return jax.shard_map(body, mesh=mesh, in_specs=in_specs, out_specs=out_specs, check_vma=False)
```

```python
import functools

import jax
import jax.numpy as jnp
from jax import lax
from jax.experimental import pallas as pl
from jax.experimental.pallas import tpu as pltpu
from jax.sharding import PartitionSpec as P

NSTATE = 16
DTR = 512
LIVE_MAX = 3
TAPS = 4
LANES = 128
MIB = 1024 * 1024
BF16 = jnp.bfloat16
F32 = jnp.float32


def gather_phases(devices):
    phases, high = [], devices
    while high > 2:
        if high >= 8:
            step = high // 4
            phases.append((step, 2 * step, 3 * step))
            high //= 4
        else:
            phases.append((high // 2,))
            high //= 2
    phases.append((1,))
    return phases


def sum_phases(devices):
    phases, step = [], 2
    while step < devices:
        if 4 * step <= devices:
            phases.append((step, 2 * step, 3 * step))
            step *= 4
        else:
            phases.append((step,))
            step *= 2
    return phases


def swap(value, shift, devices):
    return lax.ppermute(value, "weight", [(i, i ^ shift) for i in range(devices)])


def silu(v):
    return v / (1.0 + jnp.exp(-v))


def softplus(v):
    return jnp.maximum(v, 0.0) + jnp.log1p(jnp.exp(-jnp.abs(v)))


def vmem(count):
    return [pl.BlockSpec(memory_space=pltpu.VMEM)] * count


def shape(dims, kind=F32):
    return jax.ShapeDtypeStruct(dims, kind)


def call(kernel, outs, operands, scalars=0, far=0, scratch=(), limit=8):
    many = isinstance(outs, tuple)
    return pl.pallas_call(
        kernel,
        out_shape=outs,
        in_specs=[pl.BlockSpec(memory_space=pltpu.SMEM)] * scalars
        + vmem(len(operands) - scalars - far)
        + [pl.BlockSpec(memory_space=pl.ANY)] * far,
        out_specs=tuple(vmem(len(outs))) if many else vmem(1)[0],
        scratch_shapes=list(scratch),
        compiler_params=pltpu.CompilerParams(vmem_limit_bytes=limit * MIB),
    )(*operands)


def fold(wide, folded_ref):
    rows, pieces = wide.shape[0], wide.shape[1] // LANES
    for c in range(pieces):
        folded_ref[pl.ds(c, rows, stride=pieces), :] = wide[:, c * LANES : (c + 1) * LANES]


def norm_kernel(far_hidden_ref, far_gain_ref, out_ref, fold_ref, hidden_ref, gain_ref, sems):
    copies = [
        pltpu.make_async_copy(far_hidden_ref, hidden_ref, sems.at[0]),
        pltpu.make_async_copy(far_gain_ref, gain_ref, sems.at[1]),
    ]
    for copy in copies:
        copy.start()
    for copy in copies:
        copy.wait()
    wide = hidden_ref[...].astype(F32)[:LIVE_MAX]
    factor = lax.rsqrt(jnp.mean(wide * wide, axis=-1, keepdims=True) + 1e-05)
    fold(wide * factor * gain_ref[...], fold_ref)
    out_ref[...] = fold_ref[...].astype(BF16)


def join_kernel(count, *refs):
    start = 0
    for ref in refs[:count]:
        refs[-1][start : start + ref.shape[0]] = ref[...]
        start += ref.shape[0]


def join(parts, after=()):
    rows = sum(part.shape[0] for part in parts)
    return call(
        functools.partial(join_kernel, len(parts)),
        shape((rows, parts[0].shape[1]), parts[0].dtype),
        (*parts, *after),
        far=len(after),
    )


def half_kernel(mine_ref, out_ref, fold_ref):
    fold_ref[...] = mine_ref[...].astype(F32)
    rows, pieces = out_ref.shape[0], out_ref.shape[1] // LANES
    for c in range(pieces):
        out_ref[:, c * LANES : (c + 1) * LANES] = fold_ref[pl.ds(c, rows, stride=pieces), :]


def unfold_kernel(half_ref, other_ref, out_ref, fold_ref):
    fold_ref[...] = other_ref[...].astype(F32)
    rows, pieces = half_ref.shape[0], out_ref.shape[1] // LANES
    for c in range(pieces):
        span = slice(c * LANES, (c + 1) * LANES)
        other = fold_ref[pl.ds(c, rows, stride=pieces), :]
        out_ref[:, span] = jnp.concatenate([half_ref[:, span], other], axis=0).astype(BF16)


def load_kernel(start, size, far_ref, *refs):
    out_ref, sem = refs[-2:]
    rows = pl.ds(start, size)
    copy = pltpu.make_async_copy(far_ref.at[rows], out_ref.at[rows], sem)
    copy.start()
    copy.wait()


def load(array, limit, step=0, steps=1, so_far=None):
    total = array.shape[0]
    start = total * step // steps
    size = total * (step + 1) // steps - start
    operands = (array,) if so_far is None else (array, so_far)
    return pl.pallas_call(
        functools.partial(load_kernel, start, size),
        out_shape=pltpu.VMEM(array.shape, array.dtype),
        in_specs=[pl.BlockSpec(memory_space=pl.ANY)] * len(operands),
        out_specs=vmem(1)[0],
        input_output_aliases={} if so_far is None else {1: 0},
        scratch_shapes=[pltpu.SemaphoreType.DMA],
        compiler_params=pltpu.CompilerParams(vmem_limit_bytes=limit * MIB),
    )(*operands)


def add_kernel(count, *refs):
    total = refs[0][...]
    for ref in refs[1:count]:
        total = total + ref[...]
    refs[-1][...] = total


def places(block, turn, height, span):
    line = lax.broadcasted_iota(jnp.int32, (height, block.shape[1]), 0)
    return jnp.where(line == block * span + turn, 1.0, 0.0)


def fresh_input(both_ref, block, turn, rows, rows_dev):
    return jnp.dot(
        places(block, turn, rows, rows_dev).astype(BF16),
        both_ref[0].astype(BF16),
        preferred_element_type=F32,
    )


def conv_kernel(
    rows_dev,
    both_ref,
    spot_ref,
    conv_ref,
    taps_ref,
    offset_ref,
    coef_ref,
    keep_ref,
    send_ref,
    mixed_ref,
    low_ref,
):
    index = lax.axis_index("weight")
    rows = conv_ref.shape[1]
    kept = mixed_ref.shape[0]
    block = jnp.bitwise_xor(spot_ref[0:1, :], index)
    fresh = fresh_input(both_ref, block, spot_ref[1:2, :], rows, rows_dev)
    states = [conv_ref[k].astype(F32) for k in range(TAPS - 1)] + [fresh]
    total = states[0] * taps_ref[0:1, :]
    for k in range(1, TAPS):
        total = total + states[k] * taps_ref[k : k + 1, :]
    mixed = silu(total + offset_ref[...]).astype(BF16)
    line = lax.broadcasted_iota(jnp.int32, (kept, rows), 0)
    column = lax.broadcasted_iota(jnp.int32, (kept, rows), 1)
    chosen = (line // LIVE_MAX) * rows_dev + line % LIVE_MAX == column
    mixed = jnp.dot(
        jnp.where(chosen, 1.0, 0.0).astype(BF16), mixed, preferred_element_type=F32
    ).astype(BF16)
    mixed_ref[...] = mixed
    low_ref[...] = lax.dot_general(
        mixed, coef_ref[...], (((1,), (1,)), ((), ())), preferred_element_type=F32
    )
    half = keep_ref.shape[0]
    core = index % 2
    keep_ref[...] = low_ref[pl.ds(pl.multiple_of(core * half, 8), half), :]
    send_ref[...] = low_ref[pl.ds(pl.multiple_of((1 - core) * half, 8), half), :]


def gate_kernel(
    live_ref, both_ref, spot_ref, conv_ref, mixed_ref, gate_ref, new_conv_ref, alive_ref
):
    blocks = live_ref.shape[0]
    rows = conv_ref.shape[1]
    rows_dev = rows // blocks
    block = jnp.bitwise_xor(spot_ref[0:1, :], lax.axis_index("weight"))
    turn = spot_ref[1:2, :]
    row_iota = lax.broadcasted_iota(jnp.int32, (rows_dev, 128), 0)
    for b in range(blocks):
        alive_ref[b * rows_dev : (b + 1) * rows_dev, :] = jnp.where(
            row_iota < live_ref[b], 1.0, 0.0
        )
    alive = alive_ref[:, 0:1] > 0.0
    fresh = fresh_input(both_ref, block, turn, rows, rows_dev)
    states = [conv_ref[k].astype(F32) for k in range(TAPS - 1)] + [fresh]
    for k in range(TAPS - 1):
        new_conv_ref[k] = jnp.where(alive, states[k + 1], states[k]).astype(BF16)
    gate_ref[...] = jnp.dot(
        places(block, turn, mixed_ref.shape[0], LIVE_MAX),
        silu(both_ref[1]),
        precision=lax.Precision.HIGHEST,
        preferred_element_type=F32,
    )


def join_low(mine_ref, other_ref, low_ref):
    half = mine_ref.shape[0]
    core = lax.axis_index("weight") % 2
    low_ref[pl.ds(pl.multiple_of(core * half, 8), half), :] = mine_ref[...]
    low_ref[pl.ds(pl.multiple_of((1 - core) * half, 8), half), :] = other_ref[...]


def readout_kernel(
    live_ref,
    mine_ref,
    other_ref,
    spot_ref,
    mixed_ref,
    gate_ref,
    step_weight_ref,
    bias_ref,
    rates_ref,
    skip_ref,
    state_ref,
    out_weight_ref,
    keep_ref,
    send_ref,
    step_ref,
    low_ref,
    read_ref,
    alive_ref,
    fold_ref,
):
    blocks = live_ref.shape[0]
    rows_dev = state_ref.shape[0] // blocks
    kept = mixed_ref.shape[0]
    join_low(mine_ref, other_ref, low_ref)
    step_size = softplus(
        jnp.dot(
            low_ref[:, :DTR].astype(BF16), step_weight_ref[...], preferred_element_type=F32
        )
        + bias_ref[...]
    )
    step_ref[...] = step_size
    coefs = low_ref[:, DTR:]
    both_coefs = jnp.sum(coefs[:, :NSTATE] * coefs[:, NSTATE:], axis=1, keepdims=True)
    out_coefs = coefs[:, NSTATE:].T
    x_wide = mixed_ref[...].astype(F32)
    rates = -jnp.exp(rates_ref[...])
    for b in range(blocks):
        for t in range(LIVE_MAX):
            r = b * LIVE_MAX + t
            wide = state_ref[b * rows_dev + t].astype(F32)
            decayed = jnp.exp(step_size[r : r + 1, :] * rates) * wide
            read_ref[r : r + 1, :] = jnp.sum(
                out_coefs[:, r : r + 1] * decayed, axis=0, keepdims=True
            )
            alive_ref[r : r + 1, :] = jnp.full(
                (1, 128), jnp.where(t < live_ref[b], 1.0, 0.0)
            )
    readout = read_ref[...] + (both_coefs * step_size + skip_ref[...]) * x_wide
    gated = jnp.where(alive_ref[:, 0:1] > 0.0, readout * gate_ref[...], 0.0).astype(BF16)
    block = jnp.bitwise_xor(spot_ref[:, 0:1], lax.axis_index("weight"))
    column = lax.broadcasted_iota(jnp.int32, (kept, kept), 1)
    pick = jnp.where(column == block * LIVE_MAX + spot_ref[:, 1:2], 1.0, 0.0).astype(BF16)
    picked = jnp.dot(pick, gated, preferred_element_type=F32).astype(BF16)
    width = out_weight_ref.shape[1]
    pieces = width // LANES
    group = 4
    for c in range(0, pieces, group):
        part = jnp.dot(
            picked,
            out_weight_ref[:, c * LANES : (c + group) * LANES],
            preferred_element_type=F32,
        )
        for g in range(group):
            piece = part[:, g * LANES : (g + 1) * LANES]
            keep_ref[pl.ds(c + g, kept // 2, stride=pieces), :] = piece[: kept // 2]
            fold_ref[pl.ds(c + g, kept // 2, stride=pieces), :] = piece[kept // 2 :]
    send_ref[...] = fold_ref[...].astype(BF16)


def state_kernel(
    live_ref,
    mine_ref,
    other_ref,
    mixed_ref,
    step_ref,
    rates_ref,
    state_ref,
    new_state_ref,
    low_ref,
):
    blocks = live_ref.shape[0]
    rows_dev = state_ref.shape[0] // blocks
    join_low(mine_ref, other_ref, low_ref)
    in_coefs = low_ref[:, DTR : DTR + NSTATE].T
    step_size = step_ref[...]
    driven = step_size * mixed_ref[...].astype(F32)
    rates = -jnp.exp(rates_ref[...])
    for b in range(blocks):
        for t in range(LIVE_MAX):
            r = b * LIVE_MAX + t
            wide = state_ref[b * rows_dev + t].astype(F32)
            updated = (
                jnp.exp(step_size[r : r + 1, :] * rates) * wide
                + in_coefs[:, r : r + 1] * driven[r : r + 1, :]
            )
            new_state_ref[b * rows_dev + t] = jnp.where(
                t < live_ref[b], updated, wide
            ).astype(BF16)
        for t in range(LIVE_MAX, rows_dev):
            new_state_ref[b * rows_dev + t] = state_ref[b * rows_dev + t]


def sum_kernel(count, *refs):
    parts, outs = refs[:count], refs[count:]
    size = outs[0].shape[0]
    for k, out in enumerate(outs):
        rows = slice(k * size, (k + 1) * size)
        total = parts[0][rows]
        for part in parts[1:]:
            total = total + part[rows].astype(F32)
        out[...] = total.astype(out.dtype)


def last_sum_kernel(*refs):
    hidden_ref, parts, out_ref, fold_ref = refs[0], refs[1:-2], refs[-2], refs[-1]
    total = parts[0][...]
    for part in parts[1:]:
        total = total + part[...].astype(F32)
    fold_ref[...] = total
    pieces = out_ref.shape[1] // LANES
    for c in range(pieces):
        span = slice(c * LANES, (c + 1) * LANES)
        wide = hidden_ref[:, span].astype(F32)
        own = wide[:LIVE_MAX] + fold_ref[pl.ds(c, LIVE_MAX, stride=pieces), :]
        out_ref[:, span] = jnp.concatenate([own, wide[LIVE_MAX:]], axis=0).astype(BF16)


def body(
    hidden,
    norm_gain,
    in_weight,
    conv_weight,
    conv_offset,
    coef_weight,
    step_weight,
    step_bias,
    log_rates,
    skip_gain,
    out_weight,
    ssm_state,
    conv_state,
    live_counts,
):
    devices = lax.axis_size("weight")
    rows_dev, width = hidden.shape
    rows = devices * rows_dev
    kept = devices * LIVE_MAX
    channels = in_weight.shape[2]
    low_width = coef_weight.shape[1]
    phases = gather_phases(devices)
    order = [0]
    for phase in phases:
        order = order + [o ^ s for s in phase for o in order]
    spots = jnp.array(
        [[o for o in order for _ in range(LIVE_MAX)], list(range(LIVE_MAX)) * devices],
        jnp.int32,
    )
    pieces = width // LANES
    slab = LIVE_MAX * pieces

    gathered = call(
        norm_kernel,
        pltpu.VMEM((slab, LANES), BF16),
        (hidden, norm_gain.reshape(1, width)),
        far=2,
        scratch=[
            pltpu.VMEM((slab, LANES), F32),
            pltpu.VMEM(hidden.shape, BF16),
            pltpu.VMEM((1, width), F32),
            pltpu.SemaphoreType.DMA((2,)),
        ],
        limit=60,
    )
    near_weight = None
    for k, phase in enumerate(phases[:-1]):
        near_weight = load(in_weight, 43, k, len(phases) - 1, near_weight)
        gathered = join(
            [gathered] + [swap(gathered, s, devices) for s in phase], (near_weight,)
        )
    folded = [pltpu.VMEM((kept // 2 * pieces, LANES), F32)]
    half = call(half_kernel, shape((kept // 2, width)), (gathered,), scratch=folded, limit=12)
    normed = call(
        unfold_kernel,
        shape((kept, width), BF16),
        (half, swap(gathered, 1, devices)),
        scratch=folded,
        limit=12,
    )
    both = jnp.einsum("rd,dbc->brc", normed, near_weight, preferred_element_type=F32)

    conv_turned = conv_state.transpose(1, 0, 2)
    keep, send, mixed_x = call(
        functools.partial(conv_kernel, rows_dev),
        (
            shape((kept // 2, low_width)),
            shape((kept // 2, low_width)),
            shape((kept, channels), BF16),
        ),
        (
            both,
            spots,
            conv_turned,
            conv_weight,
            conv_offset.reshape(1, channels),
            coef_weight.T,
        ),
        scratch=[pltpu.VMEM((kept, low_width), F32)],
        limit=16,
    )
    gate, new_conv = call(
        gate_kernel,
        (shape((kept, channels)), shape((TAPS - 1, rows, channels), BF16)),
        (live_counts, both, spots, conv_turned, mixed_x),
        scalars=1,
        scratch=[pltpu.VMEM((rows, 128), F32)],
        limit=16,
    )

    def add(*parts, after=()):
        return call(
            functools.partial(add_kernel, len(parts)),
            shape(parts[0].shape),
            (*parts, *after),
            far=len(after),
        )

    low = add(keep, swap(send, 1, devices))
    exchanges = sum_phases(devices)
    for k, phase in enumerate(exchanges):
        after = (gate,)
        if k == len(exchanges) - 1:
            near_out = load(out_weight, 50)
            after = (near_out,)
        low = add(low, *[swap(low, s, devices) for s in phase], after=after)
    other = swap(low, 1, devices)

    size = kept // 2 * pieces
    keep, send, step_size = call(
        readout_kernel,
        (shape((size, LANES)), shape((size, LANES), BF16), shape((kept, channels))),
        (
            live_counts,
            low,
            other,
            spots.T,
            mixed_x,
            gate,
            step_weight,
            step_bias.reshape(1, channels),
            log_rates,
            skip_gain.reshape(1, channels),
            ssm_state,
            near_out,
        ),
        scalars=1,
        scratch=[
            pltpu.VMEM((kept, low_width), F32),
            pltpu.VMEM((kept, channels), F32),
            pltpu.VMEM((kept, 128), F32),
            pltpu.VMEM((size, LANES), F32),
        ],
        limit=32,
    )
    new_state = call(
        state_kernel,
        shape(ssm_state.shape, BF16),
        (live_counts, low, other, mixed_x, step_size, log_rates, ssm_state),
        scalars=1,
        scratch=[pltpu.VMEM((kept, low_width), F32)],
        limit=16,
    )

    total = (keep, swap(send, 1, devices))
    for phase in reversed(phases[:-1]):
        size //= len(phase) + 1
        parts = call(
            functools.partial(sum_kernel, len(total)),
            (shape((size, LANES)),) + (shape((size, LANES), BF16),) * len(phase),
            total,
        )
        total = (parts[0],) + tuple(swap(p, s, devices) for p, s in zip(parts[1:], phase))
    mixed = call(
        last_sum_kernel,
        shape(hidden.shape, BF16),
        (hidden,) + total,
        scratch=[pltpu.VMEM((slab, LANES), F32)],
    )
    return (mixed, new_state, new_conv.transpose(1, 0, 2))


def solution(mesh):
    in_specs = (
        P(("groups", "weight"), None),
        P(),
        P(None, None, "weight"),
        P(None, "weight"),
        P("weight"),
        P("weight", None),
        P(None, "weight"),
        P("weight"),
        P(None, "weight"),
        P("weight"),
        P("weight", None),
        P("groups", None, "weight"),
        P("groups", None, "weight"),
        P("groups"),
    )
    out_specs = (
        P(("groups", "weight"), None),
        P("groups", None, "weight"),
        P("groups", None, "weight"),
    )
    return jax.shard_map(body, mesh=mesh, in_specs=in_specs, out_specs=out_specs, check_vma=False)
```

```python
import functools

import jax
import jax.numpy as jnp
from jax import lax
from jax.experimental import pallas as pl
from jax.experimental.pallas import tpu as pltpu
from jax.sharding import PartitionSpec as P

NSTATE = 16
DTR = 512
LIVE_MAX = 3
TAPS = 4
LANES = 128
MIB = 1024 * 1024
BF16 = jnp.bfloat16
F32 = jnp.float32


def chip_steps(devices):
    steps, high = [], devices
    while high > 2:
        if high >= 8:
            steps.append((high // 4, high // 2))
            high //= 4
        else:
            steps.append((high // 2,))
            high //= 2
    steps = [tuple(step) for step in steps]
    if len(steps[-1]) == 1:
        bits = [bit for step in steps for bit in step]
        bits.sort()
        top = bits.pop()
        steps = [(top,)] + [tuple(bits[k : k + 2]) for k in range(len(bits) - 2, -1, -2)]
    return steps


def gather_phases(devices):
    whole = [step if len(step) == 1 else (sum(step), step[1], step[0]) for step in chip_steps(devices)]
    return whole + [(1,)]


def scatter_phases(devices):
    whole = [step if len(step) == 1 else (step[1], step[0], sum(step)) for step in chip_steps(devices)]
    return whole[::-1]


def sum_phases(devices):
    return [
        (step[0] + 1,) if len(step) == 1 else (step[0] + 1, step[1] + 1, sum(step))
        for step in chip_steps(devices)
    ]


def order_of(phases):
    order = [0]
    for phase in phases:
        order = order + [o ^ s for s in phase for o in order]
    return order


def spots_of(order):
    return jnp.array(
        [[o for o in order for _ in range(LIVE_MAX)], list(range(LIVE_MAX)) * len(order)],
        jnp.int32,
    )


def side(index):
    for shift in (4, 2, 1):
        index = jnp.bitwise_xor(index, lax.shift_right_logical(index, shift))
    return jnp.bitwise_and(index, 1)


def swap(value, shift, devices):
    return lax.ppermute(value, "weight", [(i, i ^ shift) for i in range(devices)])


def silu(v):
    return v / (1.0 + jnp.exp(-v))


def softplus(v):
    return jnp.maximum(v, 0.0) + jnp.log1p(jnp.exp(-jnp.abs(v)))


def vmem(count):
    return [pl.BlockSpec(memory_space=pltpu.VMEM)] * count


def shape(dims, kind=F32):
    return jax.ShapeDtypeStruct(dims, kind)


def call(kernel, outs, operands, scalars=0, far=0, scratch=(), limit=8):
    many = isinstance(outs, tuple)
    return pl.pallas_call(
        kernel,
        out_shape=outs,
        in_specs=[pl.BlockSpec(memory_space=pltpu.SMEM)] * scalars
        + vmem(len(operands) - scalars - far)
        + [pl.BlockSpec(memory_space=pl.ANY)] * far,
        out_specs=tuple(vmem(len(outs))) if many else vmem(1)[0],
        scratch_shapes=list(scratch),
        compiler_params=pltpu.CompilerParams(vmem_limit_bytes=limit * MIB),
    )(*operands)


def fold(wide, folded_ref):
    rows, pieces = wide.shape[0], wide.shape[1] // LANES
    for c in range(pieces):
        folded_ref[pl.ds(c, rows, stride=pieces), :] = wide[:, c * LANES : (c + 1) * LANES]


def norm_kernel(far_hidden_ref, far_gain_ref, out_ref, fold_ref, hidden_ref, gain_ref, sems):
    copies = [
        pltpu.make_async_copy(far_hidden_ref, hidden_ref, sems.at[0]),
        pltpu.make_async_copy(far_gain_ref, gain_ref, sems.at[1]),
    ]
    for copy in copies:
        copy.start()
    for copy in copies:
        copy.wait()
    wide = hidden_ref[...].astype(F32)[:LIVE_MAX]
    factor = lax.rsqrt(jnp.mean(wide * wide, axis=-1, keepdims=True) + 1e-05)
    fold(wide * factor * gain_ref[...], fold_ref)
    out_ref[...] = fold_ref[...].astype(BF16)


def join_kernel(count, *refs):
    start = 0
    for ref in refs[:count]:
        refs[-1][start : start + ref.shape[0]] = ref[...]
        start += ref.shape[0]


def join(parts, after=()):
    rows = sum(part.shape[0] for part in parts)
    return call(
        functools.partial(join_kernel, len(parts)),
        shape((rows, parts[0].shape[1]), parts[0].dtype),
        (*parts, *after),
        far=len(after),
    )


def half_kernel(mine_ref, out_ref, fold_ref):
    fold_ref[...] = mine_ref[...].astype(F32)
    rows, pieces = out_ref.shape[0], out_ref.shape[1] // LANES
    for c in range(pieces):
        out_ref[:, c * LANES : (c + 1) * LANES] = fold_ref[pl.ds(c, rows, stride=pieces), :]


def unfold_kernel(half_ref, other_ref, out_ref, fold_ref):
    fold_ref[...] = other_ref[...].astype(F32)
    rows, pieces = half_ref.shape[0], out_ref.shape[1] // LANES
    for c in range(pieces):
        span = slice(c * LANES, (c + 1) * LANES)
        other = fold_ref[pl.ds(c, rows, stride=pieces), :]
        out_ref[:, span] = jnp.concatenate([half_ref[:, span], other], axis=0).astype(BF16)


def load_kernel(start, size, far_ref, *refs):
    out_ref, sems = refs[-2:]
    count = sems.shape[0]
    copies = []
    for k in range(count):
        rows = pl.ds(start + size * k // count, size // count)
        copies.append(pltpu.make_async_copy(far_ref.at[rows], out_ref.at[rows], sems.at[k]))
    for copy in copies:
        copy.start()
    for copy in copies:
        copy.wait()


def load(array, limit, step=0, steps=1, so_far=None):
    total = array.shape[0]
    start = total * step // steps
    size = total * (step + 1) // steps - start
    operands = (array,) if so_far is None else (array, so_far)
    return pl.pallas_call(
        functools.partial(load_kernel, start, size),
        out_shape=pltpu.VMEM(array.shape, array.dtype),
        in_specs=[pl.BlockSpec(memory_space=pl.ANY)] * len(operands),
        out_specs=vmem(1)[0],
        input_output_aliases={} if so_far is None else {1: 0},
        scratch_shapes=[pltpu.SemaphoreType.DMA((4,))],
        compiler_params=pltpu.CompilerParams(vmem_limit_bytes=limit * MIB),
    )(*operands)


def pack(low):
    coefs = low[:, DTR:]
    high = coefs.astype(BF16)
    rest = (coefs - high.astype(F32)).astype(BF16)
    return jnp.concatenate([low[:, :DTR].astype(BF16), high, rest], axis=1)


def unpack(packed):
    wide = packed.astype(F32)
    count = (wide.shape[1] - DTR) // 2
    coefs = wide[:, DTR : DTR + count] + wide[:, DTR + count :]
    return jnp.concatenate([wide[:, :DTR], coefs], axis=1)


def add_kernel(count, *refs):
    total = refs[0][...]
    for ref in refs[1:count]:
        total = total + (ref[...] if ref.dtype == F32 else unpack(ref[...]))
    refs[-2][...] = total
    refs[-1][...] = pack(total)


def places(block, turn, height, span):
    line = lax.broadcasted_iota(jnp.int32, (height, block.shape[1]), 0)
    return jnp.where(line == block * span + turn, 1.0, 0.0)


def fresh_input(both_ref, block, turn, rows, rows_dev):
    return jnp.dot(
        places(block, turn, rows, rows_dev).astype(BF16),
        both_ref[0].astype(BF16),
        preferred_element_type=F32,
    )


def conv_kernel(
    rows_dev,
    both_ref,
    spot_ref,
    conv_ref,
    taps_ref,
    offset_ref,
    coef_ref,
    keep_ref,
    send_ref,
    mixed_ref,
    low_ref,
):
    index = lax.axis_index("weight")
    rows = conv_ref.shape[1]
    kept = mixed_ref.shape[0]
    block = jnp.bitwise_xor(spot_ref[0:1, :], index)
    fresh = fresh_input(both_ref, block, spot_ref[1:2, :], rows, rows_dev)
    states = [conv_ref[k].astype(F32) for k in range(TAPS - 1)] + [fresh]
    total = states[0] * taps_ref[0:1, :]
    for k in range(1, TAPS):
        total = total + states[k] * taps_ref[k : k + 1, :]
    mixed = silu(total + offset_ref[...]).astype(BF16)
    line = lax.broadcasted_iota(jnp.int32, (kept, rows), 0)
    column = lax.broadcasted_iota(jnp.int32, (kept, rows), 1)
    chosen = (line // LIVE_MAX) * rows_dev + line % LIVE_MAX == column
    mixed = jnp.dot(
        jnp.where(chosen, 1.0, 0.0).astype(BF16), mixed, preferred_element_type=F32
    ).astype(BF16)
    mixed_ref[...] = mixed
    low_ref[...] = lax.dot_general(
        mixed, coef_ref[...], (((1,), (1,)), ((), ())), preferred_element_type=F32
    )
    half = keep_ref.shape[0]
    core = side(index)
    keep_ref[...] = low_ref[pl.ds(pl.multiple_of(core * half, 8), half), :]
    send_ref[...] = low_ref[pl.ds(pl.multiple_of((1 - core) * half, 8), half), :]


def gate_kernel(
    live_ref, both_ref, spot_ref, conv_ref, mixed_ref, gate_ref, new_conv_ref, alive_ref
):
    blocks = live_ref.shape[0]
    rows = conv_ref.shape[1]
    rows_dev = rows // blocks
    block = jnp.bitwise_xor(spot_ref[0:1, :], lax.axis_index("weight"))
    turn = spot_ref[1:2, :]
    row_iota = lax.broadcasted_iota(jnp.int32, (rows_dev, 128), 0)
    for b in range(blocks):
        alive_ref[b * rows_dev : (b + 1) * rows_dev, :] = jnp.where(
            row_iota < live_ref[b], 1.0, 0.0
        )
    alive = alive_ref[:, 0:1] > 0.0
    fresh = fresh_input(both_ref, block, turn, rows, rows_dev)
    states = [conv_ref[k].astype(F32) for k in range(TAPS - 1)] + [fresh]
    for k in range(TAPS - 1):
        new_conv_ref[k] = jnp.where(alive, states[k + 1], states[k]).astype(BF16)
    gate_ref[...] = jnp.dot(
        places(block, turn, mixed_ref.shape[0], LIVE_MAX),
        silu(both_ref[1]),
        precision=lax.Precision.HIGHEST,
        preferred_element_type=F32,
    )


def join_low(mine_ref, other_ref, low_ref):
    half = mine_ref.shape[0]
    core = side(lax.axis_index("weight"))
    low_ref[pl.ds(pl.multiple_of(core * half, 8), half), :] = mine_ref[...]
    low_ref[pl.ds(pl.multiple_of((1 - core) * half, 8), half), :] = unpack(other_ref[...])


def readout_kernel(
    live_ref,
    mine_ref,
    other_ref,
    spot_ref,
    mixed_ref,
    gate_ref,
    step_weight_ref,
    bias_ref,
    rates_ref,
    skip_ref,
    state_ref,
    out_weight_ref,
    keep_ref,
    send_ref,
    step_ref,
    low_ref,
    read_ref,
    alive_ref,
    fold_ref,
):
    blocks = live_ref.shape[0]
    rows_dev = state_ref.shape[0] // blocks
    kept = mixed_ref.shape[0]
    join_low(mine_ref, other_ref, low_ref)
    step_size = softplus(
        jnp.dot(
            low_ref[:, :DTR].astype(BF16), step_weight_ref[...], preferred_element_type=F32
        )
        + bias_ref[...]
    )
    step_ref[...] = step_size
    coefs = low_ref[:, DTR:]
    both_coefs = jnp.sum(coefs[:, :NSTATE] * coefs[:, NSTATE:], axis=1, keepdims=True)
    out_coefs = coefs[:, NSTATE:].T
    x_wide = mixed_ref[...].astype(F32)
    rates = -jnp.exp(rates_ref[...])
    for b in range(blocks):
        for t in range(LIVE_MAX):
            r = b * LIVE_MAX + t
            wide = state_ref[b * rows_dev + t].astype(F32)
            decayed = jnp.exp(step_size[r : r + 1, :] * rates) * wide
            read_ref[r : r + 1, :] = jnp.sum(
                out_coefs[:, r : r + 1] * decayed, axis=0, keepdims=True
            )
            alive_ref[r : r + 1, :] = jnp.full(
                (1, 128), jnp.where(t < live_ref[b], 1.0, 0.0)
            )
    readout = read_ref[...] + (both_coefs * step_size + skip_ref[...]) * x_wide
    gated = jnp.where(alive_ref[:, 0:1] > 0.0, readout * gate_ref[...], 0.0).astype(BF16)
    block = jnp.bitwise_xor(spot_ref[:, 0:1], lax.axis_index("weight"))
    column = lax.broadcasted_iota(jnp.int32, (kept, kept), 1)
    pick = jnp.where(column == block * LIVE_MAX + spot_ref[:, 1:2], 1.0, 0.0).astype(BF16)
    picked = jnp.dot(pick, gated, preferred_element_type=F32).astype(BF16)
    width = out_weight_ref.shape[1]
    pieces = width // LANES
    group = 4
    for c in range(0, pieces, group):
        part = jnp.dot(
            picked,
            out_weight_ref[:, c * LANES : (c + group) * LANES],
            preferred_element_type=F32,
        )
        for g in range(group):
            piece = part[:, g * LANES : (g + 1) * LANES]
            keep_ref[pl.ds(c + g, kept // 2, stride=pieces), :] = piece[: kept // 2]
            fold_ref[pl.ds(c + g, kept // 2, stride=pieces), :] = piece[kept // 2 :]
    send_ref[...] = fold_ref[...].astype(BF16)


def state_kernel(
    live_ref,
    mine_ref,
    other_ref,
    mixed_ref,
    step_ref,
    rates_ref,
    state_ref,
    new_state_ref,
    low_ref,
):
    blocks = live_ref.shape[0]
    rows_dev = state_ref.shape[0] // blocks
    join_low(mine_ref, other_ref, low_ref)
    in_coefs = low_ref[:, DTR : DTR + NSTATE].T
    step_size = step_ref[...]
    driven = step_size * mixed_ref[...].astype(F32)
    rates = -jnp.exp(rates_ref[...])
    for b in range(blocks):
        for t in range(LIVE_MAX):
            r = b * LIVE_MAX + t
            wide = state_ref[b * rows_dev + t].astype(F32)
            updated = (
                jnp.exp(step_size[r : r + 1, :] * rates) * wide
                + in_coefs[:, r : r + 1] * driven[r : r + 1, :]
            )
            new_state_ref[b * rows_dev + t] = jnp.where(
                t < live_ref[b], updated, wide
            ).astype(BF16)
        for t in range(LIVE_MAX, rows_dev):
            new_state_ref[b * rows_dev + t] = state_ref[b * rows_dev + t]


def sum_kernel(count, *refs):
    parts, outs = refs[:count], refs[count:]
    size = outs[0].shape[0]
    for k, out in enumerate(outs):
        rows = slice(k * size, (k + 1) * size)
        total = parts[0][rows]
        for part in parts[1:]:
            total = total + part[rows].astype(F32)
        out[...] = total.astype(out.dtype)


def last_sum_kernel(*refs):
    hidden_ref, parts, out_ref, fold_ref = refs[0], refs[1:-2], refs[-2], refs[-1]
    total = parts[0][...]
    for part in parts[1:]:
        total = total + part[...].astype(F32)
    fold_ref[...] = total
    pieces = out_ref.shape[1] // LANES
    for c in range(pieces):
        span = slice(c * LANES, (c + 1) * LANES)
        wide = hidden_ref[:, span].astype(F32)
        own = wide[:LIVE_MAX] + fold_ref[pl.ds(c, LIVE_MAX, stride=pieces), :]
        out_ref[:, span] = jnp.concatenate([own, wide[LIVE_MAX:]], axis=0).astype(BF16)


def body(
    hidden,
    norm_gain,
    in_weight,
    conv_weight,
    conv_offset,
    coef_weight,
    step_weight,
    step_bias,
    log_rates,
    skip_gain,
    out_weight,
    ssm_state,
    conv_state,
    live_counts,
):
    devices = lax.axis_size("weight")
    rows_dev, width = hidden.shape
    rows = devices * rows_dev
    kept = devices * LIVE_MAX
    channels = in_weight.shape[2]
    low_width = coef_weight.shape[1]
    phases = gather_phases(devices)
    spots = spots_of(order_of(phases))
    scatter = scatter_phases(devices)
    ends = spots_of(order_of(scatter[::-1] + [(1,)])).T
    pieces = width // LANES
    slab = LIVE_MAX * pieces

    gathered = call(
        norm_kernel,
        pltpu.VMEM((slab, LANES), BF16),
        (hidden, norm_gain.reshape(1, width)),
        far=2,
        scratch=[
            pltpu.VMEM((slab, LANES), F32),
            pltpu.VMEM(hidden.shape, BF16),
            pltpu.VMEM((1, width), F32),
            pltpu.SemaphoreType.DMA((2,)),
        ],
        limit=60,
    )
    near_weight = None
    for k, phase in enumerate(phases[:-1]):
        near_weight = load(in_weight, 43, k, len(phases) - 1, near_weight)
        gathered = join(
            [gathered] + [swap(gathered, s, devices) for s in phase], (near_weight,)
        )
    folded = [pltpu.VMEM((kept // 2 * pieces, LANES), F32)]
    half = call(half_kernel, shape((kept // 2, width)), (gathered,), scratch=folded, limit=12)
    normed = call(
        unfold_kernel,
        shape((kept, width), BF16),
        (half, swap(gathered, 1, devices)),
        scratch=folded,
        limit=12,
    )
    both = jnp.einsum("rd,dbc->brc", normed, near_weight, preferred_element_type=F32)

    conv_turned = conv_state.transpose(1, 0, 2)
    keep, send, mixed_x = call(
        functools.partial(conv_kernel, rows_dev),
        (
            shape((kept // 2, low_width)),
            shape((kept // 2, low_width)),
            shape((kept, channels), BF16),
        ),
        (
            both,
            spots,
            conv_turned,
            conv_weight,
            conv_offset.reshape(1, channels),
            coef_weight.T,
        ),
        scratch=[pltpu.VMEM((kept, low_width), F32)],
        limit=16,
    )
    gate, new_conv = call(
        gate_kernel,
        (shape((kept, channels)), shape((TAPS - 1, rows, channels), BF16)),
        (live_counts, both, spots, conv_turned, mixed_x),
        scalars=1,
        scratch=[pltpu.VMEM((rows, 128), F32)],
        limit=16,
    )

    packed_width = low_width + 2 * NSTATE

    def add(*parts, after=()):
        return call(
            functools.partial(add_kernel, len(parts)),
            (shape(parts[0].shape), shape((kept // 2, packed_width), BF16)),
            (*parts, *after),
            far=len(after),
        )

    low, packed = add(keep, swap(send, 1, devices))
    exchanges = sum_phases(devices)
    for k, phase in enumerate(exchanges):
        after = (gate,)
        if k == len(exchanges) - 1:
            near_out = load(out_weight, 50)
            after = (near_out,)
        low, packed = add(low, *[swap(packed, s, devices) for s in phase], after=after)
    other = swap(packed, 1, devices)

    size = kept // 2 * pieces
    keep, send, step_size = call(
        readout_kernel,
        (shape((size, LANES)), shape((size, LANES), BF16), shape((kept, channels))),
        (
            live_counts,
            low,
            other,
            ends,
            mixed_x,
            gate,
            step_weight,
            step_bias.reshape(1, channels),
            log_rates,
            skip_gain.reshape(1, channels),
            ssm_state,
            near_out,
        ),
        scalars=1,
        scratch=[
            pltpu.VMEM((kept, low_width), F32),
            pltpu.VMEM((kept, channels), F32),
            pltpu.VMEM((kept, 128), F32),
            pltpu.VMEM((size, LANES), F32),
        ],
        limit=32,
    )
    new_state = call(
        state_kernel,
        shape(ssm_state.shape, BF16),
        (live_counts, low, other, mixed_x, step_size, log_rates, ssm_state),
        scalars=1,
        scratch=[pltpu.VMEM((kept, low_width), F32)],
        limit=16,
    )

    total = (keep, swap(send, 1, devices))
    for phase in scatter:
        size //= len(phase) + 1
        parts = call(
            functools.partial(sum_kernel, len(total)),
            (shape((size, LANES)),) + (shape((size, LANES), BF16),) * len(phase),
            total,
        )
        total = (parts[0],) + tuple(swap(p, s, devices) for p, s in zip(parts[1:], phase))
    mixed = call(
        last_sum_kernel,
        shape(hidden.shape, BF16),
        (hidden,) + total,
        scratch=[pltpu.VMEM((slab, LANES), F32)],
    )
    return (mixed, new_state, new_conv.transpose(1, 0, 2))


def solution(mesh):
    in_specs = (
        P(("groups", "weight"), None),
        P(),
        P(None, None, "weight"),
        P(None, "weight"),
        P("weight"),
        P("weight", None),
        P(None, "weight"),
        P("weight"),
        P(None, "weight"),
        P("weight"),
        P("weight", None),
        P("groups", None, "weight"),
        P("groups", None, "weight"),
        P("groups"),
    )
    out_specs = (
        P(("groups", "weight"), None),
        P("groups", None, "weight"),
        P("groups", None, "weight"),
    )
    return jax.shard_map(body, mesh=mesh, in_specs=in_specs, out_specs=out_specs, check_vma=False)
```

```python
import functools

import jax
import jax.numpy as jnp
from jax import lax
from jax.experimental import pallas as pl
from jax.experimental.pallas import tpu as pltpu
from jax.sharding import PartitionSpec as P

NSTATE = 16
DTR = 512
LIVE_MAX = 3
TAPS = 4
LANES = 128
MIB = 1024 * 1024
FIRST_SHARE = 0.4375
FIRST_COLUMNS = 5
BF16 = jnp.bfloat16
F32 = jnp.float32


def chip_steps(devices):
    steps, high = [], devices
    while high > 2:
        if high >= 8:
            steps.append((high // 4, high // 2))
            high //= 4
        else:
            steps.append((high // 2,))
            high //= 2
    steps = [tuple(step) for step in steps]
    if len(steps[-1]) == 1:
        bits = [bit for step in steps for bit in step]
        bits.sort()
        top = bits.pop()
        steps = [(top,)] + [tuple(bits[k : k + 2]) for k in range(len(bits) - 2, -1, -2)]
    return steps


def gather_phases(devices):
    whole = [step if len(step) == 1 else (sum(step), step[1], step[0]) for step in chip_steps(devices)]
    return whole + [(1,)]


def scatter_phases(devices):
    whole = [step if len(step) == 1 else (step[1], step[0], sum(step)) for step in chip_steps(devices)]
    return whole[::-1]


def sum_phases(devices):
    return [
        (step[0] + 1,) if len(step) == 1 else (step[0] + 1, step[1] + 1, sum(step))
        for step in chip_steps(devices)
    ]


def order_of(phases):
    order = [0]
    for phase in phases:
        order = order + [o ^ s for s in phase for o in order]
    return order


def spots_of(order):
    return jnp.array(
        [[o for o in order for _ in range(LIVE_MAX)], list(range(LIVE_MAX)) * len(order)],
        jnp.int32,
    )


def side(index):
    for shift in (4, 2, 1):
        index = jnp.bitwise_xor(index, lax.shift_right_logical(index, shift))
    return jnp.bitwise_and(index, 1)


def swap(value, shift, devices):
    return lax.ppermute(value, "weight", [(i, i ^ shift) for i in range(devices)])


def silu(v):
    return v / (1.0 + jnp.exp(-v))


def softplus(v):
    return jnp.maximum(v, 0.0) + jnp.log1p(jnp.exp(-jnp.abs(v)))


def vmem(count):
    return [pl.BlockSpec(memory_space=pltpu.VMEM)] * count


def shape(dims, kind=F32):
    return jax.ShapeDtypeStruct(dims, kind)


def call(kernel, outs, operands, scalars=0, far=0, scratch=(), limit=8, after=(), aliases=None):
    many = isinstance(outs, tuple)
    return pl.pallas_call(
        kernel,
        out_shape=outs,
        in_specs=[pl.BlockSpec(memory_space=pltpu.SMEM)] * scalars
        + vmem(len(operands) - scalars - far)
        + [pl.BlockSpec(memory_space=pl.ANY)] * (far + len(after)),
        out_specs=tuple(vmem(len(outs))) if many else vmem(1)[0],
        scratch_shapes=list(scratch),
        input_output_aliases=aliases or {},
        compiler_params=pltpu.CompilerParams(vmem_limit_bytes=limit * MIB),
    )(*operands, *after)


def share_copies(far_ref, near_ref, sems, share):
    rows = far_ref.shape[0]
    start, end = (int(rows * part) // 8 * 8 for part in share)
    count = sems.shape[0]
    size = (end - start) // count
    spans = [pl.ds(start + size * k, size) for k in range(count)]
    return [
        pltpu.make_async_copy(far_ref.at[span], near_ref.at[span], sems.at[k])
        for k, span in enumerate(spans)
    ]


def start_all(copies):
    for copy in copies:
        copy.start()


def wait_all(copies):
    for copy in copies:
        copy.wait()


def fold(wide, folded_ref):
    rows, pieces = wide.shape[0], wide.shape[1] // LANES
    for c in range(pieces):
        folded_ref[pl.ds(c, rows, stride=pieces), :] = wide[:, c * LANES : (c + 1) * LANES]


def norm_kernel(far_hidden_ref, far_gain_ref, out_ref, fold_ref, hidden_ref, gain_ref, sems):
    copies = [
        pltpu.make_async_copy(far_hidden_ref, hidden_ref, sems.at[0]),
        pltpu.make_async_copy(far_gain_ref, gain_ref, sems.at[1]),
    ]
    start_all(copies)
    wait_all(copies)
    wide = hidden_ref[...].astype(F32)[:LIVE_MAX]
    factor = lax.rsqrt(jnp.mean(wide * wide, axis=-1, keepdims=True) + 1e-05)
    fold(wide * factor * gain_ref[...], fold_ref)
    out_ref[...] = fold_ref[...].astype(BF16)


def join_kernel(count, *refs):
    start = 0
    for ref in refs[:count]:
        refs[-1][start : start + ref.shape[0]] = ref[...]
        start += ref.shape[0]


def join(parts, after=()):
    rows = sum(part.shape[0] for part in parts)
    return call(
        functools.partial(join_kernel, len(parts)),
        shape((rows, parts[0].shape[1]), parts[0].dtype),
        parts,
        after=after,
    )


def half_kernel(mine_ref, out_ref, fold_ref):
    fold_ref[...] = mine_ref[...].astype(F32)
    rows, pieces = out_ref.shape[0], out_ref.shape[1] // LANES
    for c in range(pieces):
        out_ref[:, c * LANES : (c + 1) * LANES] = fold_ref[pl.ds(c, rows, stride=pieces), :]


def unfold_kernel(half_ref, other_ref, out_ref, fold_ref):
    fold_ref[...] = other_ref[...].astype(F32)
    rows, pieces = half_ref.shape[0], out_ref.shape[1] // LANES
    for c in range(pieces):
        span = slice(c * LANES, (c + 1) * LANES)
        other = fold_ref[pl.ds(c, rows, stride=pieces), :]
        out_ref[:, span] = jnp.concatenate([half_ref[:, span], other], axis=0).astype(BF16)


def columns_kernel(start, far_ref, near_ref, sems):
    columns = pl.ds(start, near_ref.shape[1])
    loads = share_copies(far_ref.at[:, columns], near_ref, sems, (0, 1))
    start_all(loads)
    wait_all(loads)


def load_kernel(share, far_ref, *refs):
    near_ref, sems = refs[-2:]
    loads = share_copies(far_ref, near_ref, sems, share)
    start_all(loads)
    wait_all(loads)


def pack(low):
    coefs = low[:, DTR:]
    high = coefs.astype(BF16)
    rest = (coefs - high.astype(F32)).astype(BF16)
    return jnp.concatenate([low[:, :DTR].astype(BF16), high, rest], axis=1)


def unpack(packed):
    wide = packed.astype(F32)
    count = (wide.shape[1] - DTR) // 2
    coefs = wide[:, DTR : DTR + count] + wide[:, DTR + count :]
    return jnp.concatenate([wide[:, :DTR], coefs], axis=1)


def add_kernel(count, *refs):
    total = refs[0][...]
    for ref in refs[1:count]:
        total = total + (ref[...] if ref.dtype == F32 else unpack(ref[...]))
    refs[-2][...] = total
    refs[-1][...] = pack(total)


def places(block, turn, height, span):
    line = lax.broadcasted_iota(jnp.int32, (height, block.shape[1]), 0)
    return jnp.where(line == block * span + turn, 1.0, 0.0)


def fresh_input(both_ref, block, turn, rows, rows_dev):
    return jnp.dot(
        places(block, turn, rows, rows_dev).astype(BF16),
        both_ref[0].astype(BF16),
        preferred_element_type=F32,
    )


def conv_kernel(
    rows_dev,
    both_ref,
    spot_ref,
    conv_ref,
    taps_ref,
    offset_ref,
    coef_ref,
    keep_ref,
    send_ref,
    mixed_ref,
    low_ref,
):
    index = lax.axis_index("weight")
    rows = conv_ref.shape[1]
    kept = mixed_ref.shape[0]
    block = jnp.bitwise_xor(spot_ref[0:1, :], index)
    fresh = fresh_input(both_ref, block, spot_ref[1:2, :], rows, rows_dev)
    states = [conv_ref[k].astype(F32) for k in range(TAPS - 1)] + [fresh]
    total = states[0] * taps_ref[0:1, :]
    for k in range(1, TAPS):
        total = total + states[k] * taps_ref[k : k + 1, :]
    mixed = silu(total + offset_ref[...]).astype(BF16)
    line = lax.broadcasted_iota(jnp.int32, (kept, rows), 0)
    column = lax.broadcasted_iota(jnp.int32, (kept, rows), 1)
    chosen = (line // LIVE_MAX) * rows_dev + line % LIVE_MAX == column
    mixed = jnp.dot(
        jnp.where(chosen, 1.0, 0.0).astype(BF16), mixed, preferred_element_type=F32
    ).astype(BF16)
    mixed_ref[...] = mixed
    low_ref[...] = lax.dot_general(
        mixed, coef_ref[...], (((1,), (1,)), ((), ())), preferred_element_type=F32
    )
    half = keep_ref.shape[0]
    core = side(index)
    keep_ref[...] = low_ref[pl.ds(pl.multiple_of(core * half, 8), half), :]
    send_ref[...] = low_ref[pl.ds(pl.multiple_of((1 - core) * half, 8), half), :]


def gate_kernel(both_ref, spot_ref, gate_ref):
    block = jnp.bitwise_xor(spot_ref[0:1, :], lax.axis_index("weight"))
    gate_ref[...] = jnp.dot(
        places(block, spot_ref[1:2, :], gate_ref.shape[0], LIVE_MAX),
        silu(both_ref[1]),
        precision=lax.Precision.HIGHEST,
        preferred_element_type=F32,
    )


def taps_kernel(live_ref, both_ref, spot_ref, conv_ref, new_conv_ref, alive_ref):
    blocks = live_ref.shape[0]
    rows = conv_ref.shape[1]
    rows_dev = rows // blocks
    block = jnp.bitwise_xor(spot_ref[0:1, :], lax.axis_index("weight"))
    row_iota = lax.broadcasted_iota(jnp.int32, (rows_dev, LANES), 0)
    for b in range(blocks):
        alive_ref[b * rows_dev : (b + 1) * rows_dev, :] = jnp.where(
            row_iota < live_ref[b], 1.0, 0.0
        )
    alive = alive_ref[:, 0:1] > 0.0
    fresh = fresh_input(both_ref, block, spot_ref[1:2, :], rows, rows_dev)
    states = [conv_ref[k].astype(F32) for k in range(TAPS - 1)] + [fresh]
    for k in range(TAPS - 1):
        new_conv_ref[k] = jnp.where(alive, states[k + 1], states[k]).astype(BF16)


def join_low(mine_ref, other_ref, low_ref):
    half = mine_ref.shape[0]
    core = side(lax.axis_index("weight"))
    low_ref[pl.ds(pl.multiple_of(core * half, 8), half), :] = mine_ref[...]
    low_ref[pl.ds(pl.multiple_of((1 - core) * half, 8), half), :] = unpack(other_ref[...])


def readout_kernel(
    live_ref,
    mine_ref,
    other_ref,
    spot_ref,
    mixed_ref,
    gate_ref,
    step_weight_ref,
    bias_ref,
    rates_ref,
    skip_ref,
    state_ref,
    first_ref,
    last_ref,
    keep_ref,
    send_ref,
    step_ref,
    low_ref,
    read_ref,
    alive_ref,
    fold_ref,
):
    blocks = live_ref.shape[0]
    rows_dev = state_ref.shape[0] // blocks
    kept = mixed_ref.shape[0]
    join_low(mine_ref, other_ref, low_ref)
    step_size = softplus(
        jnp.dot(
            low_ref[:, :DTR].astype(BF16), step_weight_ref[...], preferred_element_type=F32
        )
        + bias_ref[...]
    )
    step_ref[...] = step_size
    coefs = low_ref[:, DTR:]
    both_coefs = jnp.sum(coefs[:, :NSTATE] * coefs[:, NSTATE:], axis=1, keepdims=True)
    out_coefs = coefs[:, NSTATE:].T
    x_wide = mixed_ref[...].astype(F32)
    rates = -jnp.exp(rates_ref[...])
    for b in range(blocks):
        for t in range(LIVE_MAX):
            r = b * LIVE_MAX + t
            wide = state_ref[b * rows_dev + t].astype(F32)
            decayed = jnp.exp(step_size[r : r + 1, :] * rates) * wide
            read_ref[r : r + 1, :] = jnp.sum(
                out_coefs[:, r : r + 1] * decayed, axis=0, keepdims=True
            )
            alive_ref[r : r + 1, :] = jnp.full(
                (1, 128), jnp.where(t < live_ref[b], 1.0, 0.0)
            )
    readout = read_ref[...] + (both_coefs * step_size + skip_ref[...]) * x_wide
    gated = jnp.where(alive_ref[:, 0:1] > 0.0, readout * gate_ref[...], 0.0).astype(BF16)
    block = jnp.bitwise_xor(spot_ref[:, 0:1], lax.axis_index("weight"))
    column = lax.broadcasted_iota(jnp.int32, (kept, kept), 1)
    pick = jnp.where(column == block * LIVE_MAX + spot_ref[:, 1:2], 1.0, 0.0).astype(BF16)
    picked = jnp.dot(pick, gated, preferred_element_type=F32).astype(BF16)
    half = kept // 2
    near = first_ref.shape[1]
    pieces = (near + last_ref.shape[1]) // LANES
    group = 4
    for c in range(0, pieces, group):
        start = c * LANES
        if start < near:
            weight = first_ref[:, start : start + group * LANES]
        else:
            weight = last_ref[:, start - near : start - near + group * LANES]
        part = jnp.dot(picked, weight, preferred_element_type=F32)
        for g in range(group):
            piece = part[:, g * LANES : (g + 1) * LANES]
            fold_ref[pl.ds(c + g, kept, stride=pieces + 1), :] = piece
    for r in range(half):
        rows = slice(r * pieces, (r + 1) * pieces)
        start = r * (pieces + 1)
        keep_ref[rows] = fold_ref[start : start + pieces]
        start = (half + r) * (pieces + 1)
        send_ref[rows] = fold_ref[start : start + pieces].astype(BF16)


def state_kernel(
    live_ref,
    mine_ref,
    other_ref,
    mixed_ref,
    step_ref,
    rates_ref,
    state_ref,
    new_state_ref,
    token_ref,
    low_ref,
):
    token_ref[...] = jnp.zeros_like(token_ref)
    blocks = live_ref.shape[0]
    rows_dev = state_ref.shape[0] // blocks
    join_low(mine_ref, other_ref, low_ref)
    in_coefs = low_ref[:, DTR : DTR + NSTATE].T
    step_size = step_ref[...]
    driven = step_size * mixed_ref[...].astype(F32)
    rates = -jnp.exp(rates_ref[...])
    for b in range(blocks):
        for t in range(LIVE_MAX):
            r = b * LIVE_MAX + t
            wide = state_ref[b * rows_dev + t].astype(F32)
            updated = (
                jnp.exp(step_size[r : r + 1, :] * rates) * wide
                + in_coefs[:, r : r + 1] * driven[r : r + 1, :]
            )
            new_state_ref[b * rows_dev + t] = jnp.where(
                t < live_ref[b], updated, wide
            ).astype(BF16)
        for t in range(LIVE_MAX, rows_dev):
            new_state_ref[b * rows_dev + t] = state_ref[b * rows_dev + t]


def sum_kernel(count, skipped, *refs):
    parts, outs = refs[:count], refs[count + skipped :]
    size = outs[0].shape[0]
    for k, out in enumerate(outs):
        rows = slice(k * size, (k + 1) * size)
        total = parts[0][rows]
        for part in parts[1:]:
            total = total + part[rows].astype(F32)
        out[...] = total.astype(out.dtype)


def last_sum_kernel(*refs):
    hidden_ref, parts, out_ref, fold_ref = refs[0], refs[1:-2], refs[-2], refs[-1]
    total = parts[0][...]
    for part in parts[1:]:
        total = total + part[...].astype(F32)
    fold_ref[...] = total
    pieces = out_ref.shape[1] // LANES
    for c in range(pieces):
        span = slice(c * LANES, (c + 1) * LANES)
        wide = hidden_ref[:, span].astype(F32)
        own = wide[:LIVE_MAX] + fold_ref[pl.ds(c, LIVE_MAX, stride=pieces), :]
        out_ref[:, span] = jnp.concatenate([own, wide[LIVE_MAX:]], axis=0).astype(BF16)


def body(
    hidden,
    norm_gain,
    in_weight,
    conv_weight,
    conv_offset,
    coef_weight,
    step_weight,
    step_bias,
    log_rates,
    skip_gain,
    out_weight,
    ssm_state,
    conv_state,
    live_counts,
):
    devices = lax.axis_size("weight")
    rows_dev, width = hidden.shape
    rows = devices * rows_dev
    kept = devices * LIVE_MAX
    channels = in_weight.shape[2]
    low_width = coef_weight.shape[1]
    phases = gather_phases(devices)
    spots = spots_of(order_of(phases))
    scatter = scatter_phases(devices)
    ends = spots_of(order_of(scatter[::-1] + [(1,)])).T
    pieces = width // LANES
    slab = LIVE_MAX * pieces

    weight_shape = pltpu.VMEM(in_weight.shape, BF16)

    def load(share, so_far=None):
        return call(
            functools.partial(load_kernel, share),
            weight_shape,
            (in_weight,),
            far=1,
            scratch=[pltpu.SemaphoreType.DMA((4,))],
            limit=43,
            after=() if so_far is None else (so_far,),
            aliases={} if so_far is None else {1: 0},
        )

    gathered = call(
        norm_kernel,
        pltpu.VMEM((slab, LANES), BF16),
        (hidden, norm_gain.reshape(1, width)),
        far=2,
        scratch=[
            pltpu.VMEM((slab, LANES), F32),
            pltpu.VMEM(hidden.shape, BF16),
            pltpu.VMEM((1, width), F32),
            pltpu.SemaphoreType.DMA((2,)),
        ],
        limit=60,
    )
    done, near_weight = 0.0, None
    for k, phase in enumerate(phases[:-1]):
        until = 1.0 if k == len(phases) - 2 else done + (1.0 - done) * FIRST_SHARE
        near_weight = load((done, until), near_weight)
        done = until
        gathered = join(
            [gathered] + [swap(gathered, s, devices) for s in phase], (near_weight,)
        )
    folded = [pltpu.VMEM((kept // 2 * pieces, LANES), F32)]
    half = call(half_kernel, shape((kept // 2, width)), (gathered,), scratch=folded, limit=12)
    normed = call(
        unfold_kernel,
        shape((kept, width), BF16),
        (half, swap(gathered, 1, devices)),
        scratch=folded,
        limit=12,
    )
    both = jnp.einsum("rd,dbc->brc", normed, near_weight, preferred_element_type=F32)

    conv_turned = conv_state.transpose(1, 0, 2)
    keep, send, mixed_x = call(
        functools.partial(conv_kernel, rows_dev),
        (
            shape((kept // 2, low_width)),
            shape((kept // 2, low_width)),
            shape((kept, channels), BF16),
        ),
        (
            both,
            spots,
            conv_turned,
            conv_weight,
            conv_offset.reshape(1, channels),
            coef_weight.T,
        ),
        scratch=[pltpu.VMEM((kept, low_width), F32)],
        limit=16,
    )
    gate = call(gate_kernel, shape((kept, channels)), (both, spots))
    new_conv = call(
        taps_kernel,
        shape((TAPS - 1, rows, channels), BF16),
        (live_counts, both, spots, conv_turned),
        scalars=1,
        scratch=[pltpu.VMEM((rows, LANES), F32)],
    )

    packed_width = low_width + 2 * NSTATE

    def add(*parts, after=()):
        return call(
            functools.partial(add_kernel, len(parts)),
            (shape(parts[0].shape), shape((kept // 2, packed_width), BF16)),
            parts,
            after=after,
        )

    low, packed = add(keep, swap(send, 1, devices), after=(gate,))
    exchanges = sum_phases(devices)
    first_columns = width * FIRST_COLUMNS // 16 if len(exchanges) > 1 else width // 2
    near_out = [
        call(
            functools.partial(columns_kernel, start),
            pltpu.VMEM((channels, count), BF16),
            (out_weight,),
            far=1,
            scratch=[pltpu.SemaphoreType.DMA((4,))],
            limit=50,
        )
        for start, count in ((0, first_columns), (first_columns, width - first_columns))
    ]
    for k, phase in enumerate(exchanges):
        after = (near_out[0],) if k == 0 else (near_out[1],)
        low, packed = add(low, *[swap(packed, s, devices) for s in phase], after=after)
    other = swap(packed, 1, devices)

    size = kept // 2 * pieces
    keep, send, step_size = call(
        readout_kernel,
        (shape((size, LANES)), shape((size, LANES), BF16), shape((kept, channels))),
        (
            live_counts,
            low,
            other,
            ends,
            mixed_x,
            gate,
            step_weight,
            step_bias.reshape(1, channels),
            log_rates,
            skip_gain.reshape(1, channels),
            ssm_state,
            *near_out,
        ),
        scalars=1,
        scratch=[
            pltpu.VMEM((kept, low_width), F32),
            pltpu.VMEM((kept, channels), F32),
            pltpu.VMEM((kept, 128), F32),
            pltpu.VMEM((kept * (pieces + 1), LANES), F32),
        ],
        limit=24,
    )
    new_state, token = call(
        state_kernel,
        (shape(ssm_state.shape, BF16), shape((8, LANES))),
        (live_counts, low, other, mixed_x, step_size, log_rates, ssm_state),
        scalars=1,
        scratch=[pltpu.VMEM((kept, low_width), F32)],
        limit=16,
    )

    total = (keep, swap(send, 1, devices))
    for k, phase in enumerate(scatter):
        size //= len(phase) + 1
        parts = call(
            functools.partial(sum_kernel, len(total), 1 if k == 1 else 0),
            (shape((size, LANES)),) + (shape((size, LANES), BF16),) * len(phase),
            total,
            after=(token,) if k == 1 else (),
        )
        total = (parts[0],) + tuple(swap(p, s, devices) for p, s in zip(parts[1:], phase))
    mixed = call(
        last_sum_kernel,
        shape(hidden.shape, BF16),
        (hidden,) + total,
        scratch=[pltpu.VMEM((slab, LANES), F32)],
    )
    return (mixed, new_state, new_conv.transpose(1, 0, 2))


def solution(mesh):
    in_specs = (
        P(("groups", "weight"), None),
        P(),
        P(None, None, "weight"),
        P(None, "weight"),
        P("weight"),
        P("weight", None),
        P(None, "weight"),
        P("weight"),
        P(None, "weight"),
        P("weight"),
        P("weight", None),
        P("groups", None, "weight"),
        P("groups", None, "weight"),
        P("groups"),
    )
    out_specs = (
        P(("groups", "weight"), None),
        P("groups", None, "weight"),
        P("groups", None, "weight"),
    )
    return jax.shard_map(body, mesh=mesh, in_specs=in_specs, out_specs=out_specs, check_vma=False)
```

```python
import functools

import jax
import jax.numpy as jnp
from jax import lax
from jax.experimental import pallas as pl
from jax.experimental.pallas import tpu as pltpu
from jax.sharding import PartitionSpec as P

NSTATE = 16
DTR = 512
LIVE_MAX = 3
TAPS = 4
LANES = 128
MIB = 1024 * 1024
CORE_SHARE = 0.9375
FIRST_SHARE = 0.4
FIRST_COLUMNS = 5
BF16 = jnp.bfloat16
F32 = jnp.float32


def chip_steps(devices):
    steps, high = [], devices
    while high > 2:
        if high >= 8:
            steps.append((high // 4, high // 2))
            high //= 4
        else:
            steps.append((high // 2,))
            high //= 2
    steps = [tuple(step) for step in steps]
    if len(steps[-1]) == 1:
        bits = [bit for step in steps for bit in step]
        bits.sort()
        top = bits.pop()
        steps = [(top,)] + [tuple(bits[k : k + 2]) for k in range(len(bits) - 2, -1, -2)]
    return steps


def gather_phases(devices):
    whole = [step if len(step) == 1 else (sum(step), step[1], step[0]) for step in chip_steps(devices)]
    return whole + [(1,)]


def scatter_phases(devices):
    whole = [step if len(step) == 1 else (step[1], step[0], sum(step)) for step in chip_steps(devices)]
    return whole[::-1]


def sum_phases(devices):
    return [
        (step[0] + 1,) if len(step) == 1 else (step[0] + 1, step[1] + 1, sum(step))
        for step in chip_steps(devices)
    ]


def order_of(phases):
    order = [0]
    for phase in phases:
        order = order + [o ^ s for s in phase for o in order]
    return order


def spots_of(order):
    return jnp.array(
        [[o for o in order for _ in range(LIVE_MAX)], list(range(LIVE_MAX)) * len(order)],
        jnp.int32,
    )


def side(index):
    for shift in (4, 2, 1):
        index = jnp.bitwise_xor(index, lax.shift_right_logical(index, shift))
    return jnp.bitwise_and(index, 1)


def swap(value, shift, devices):
    return lax.ppermute(value, "weight", [(i, i ^ shift) for i in range(devices)])


def silu(v):
    return v / (1.0 + jnp.exp(-v))


def softplus(v):
    return jnp.maximum(v, 0.0) + jnp.log1p(jnp.exp(-jnp.abs(v)))


def vmem(count):
    return [pl.BlockSpec(memory_space=pltpu.VMEM)] * count


def shape(dims, kind=F32):
    return jax.ShapeDtypeStruct(dims, kind)


def call(kernel, outs, operands, scalars=0, far=0, scratch=(), limit=8, after=(), aliases=None):
    many = isinstance(outs, tuple)
    return pl.pallas_call(
        kernel,
        out_shape=outs,
        in_specs=[pl.BlockSpec(memory_space=pltpu.SMEM)] * scalars
        + vmem(len(operands) - scalars - far)
        + [pl.BlockSpec(memory_space=pl.ANY)] * (far + len(after)),
        out_specs=tuple(vmem(len(outs))) if many else vmem(1)[0],
        scratch_shapes=list(scratch),
        input_output_aliases=aliases or {},
        compiler_params=pltpu.CompilerParams(vmem_limit_bytes=limit * MIB),
    )(*operands, *after)


def share_copies(far_ref, near_ref, sems, share):
    rows = far_ref.shape[0]
    start, end = (int(rows * part) // 8 * 8 for part in share)
    count = sems.shape[0]
    size = (end - start) // count
    spans = [pl.ds(start + size * k, size) for k in range(count)]
    return [
        pltpu.make_async_copy(far_ref.at[span], near_ref.at[span], sems.at[k])
        for k, span in enumerate(spans)
    ]


def start_all(copies):
    for copy in copies:
        copy.start()


def wait_all(copies):
    for copy in copies:
        copy.wait()


def fold(wide, fold_ref, folded_ref):
    rows, pieces = wide.shape[0], wide.shape[1] // LANES
    for c in range(pieces):
        fold_ref[pl.ds(c, rows, stride=pieces + 1), :] = wide[:, c * LANES : (c + 1) * LANES]
    for r in range(rows):
        start = r * (pieces + 1)
        folded_ref[r * pieces : (r + 1) * pieces] = fold_ref[start : start + pieces].astype(
            folded_ref.dtype
        )


def spread(folded, fold_ref):
    rows = fold_ref.shape[0] - folded.shape[0]
    pieces = folded.shape[0] // rows
    for r in range(rows):
        start = r * (pieces + 1)
        fold_ref[start : start + pieces] = folded[r * pieces : (r + 1) * pieces].astype(F32)
    return rows, pieces


def norm_kernel(far_hidden_ref, far_gain_ref, out_ref, fold_ref, hidden_ref, gain_ref, sems):
    copies = [
        pltpu.make_async_copy(far_hidden_ref, hidden_ref, sems.at[0]),
        pltpu.make_async_copy(far_gain_ref, gain_ref, sems.at[1]),
    ]
    start_all(copies)
    wait_all(copies)
    wide = hidden_ref[...].astype(F32)[:LIVE_MAX]
    factor = lax.rsqrt(jnp.mean(wide * wide, axis=-1, keepdims=True) + 1e-05)
    fold(wide * factor * gain_ref[...], fold_ref, out_ref)


def join_kernel(count, *refs):
    start = 0
    for ref in refs[:count]:
        refs[-1][start : start + ref.shape[0]] = ref[...]
        start += ref.shape[0]


def join(parts, after=()):
    rows = sum(part.shape[0] for part in parts)
    return call(
        functools.partial(join_kernel, len(parts)),
        shape((rows, parts[0].shape[1]), parts[0].dtype),
        parts,
        after=after,
    )


def half_kernel(mine_ref, out_ref, fold_ref):
    rows, pieces = spread(mine_ref, fold_ref)
    for c in range(pieces):
        out_ref[:, c * LANES : (c + 1) * LANES] = fold_ref[pl.ds(c, rows, stride=pieces + 1), :]


def unfold_kernel(half_ref, other_ref, _, out_ref, fold_ref):
    rows, pieces = spread(other_ref, fold_ref)
    for c in range(pieces):
        span = slice(c * LANES, (c + 1) * LANES)
        other = fold_ref[pl.ds(c, rows, stride=pieces + 1), :]
        out_ref[:, span] = jnp.concatenate([half_ref[:, span], other], axis=0).astype(BF16)


def columns_kernel(start, far_ref, near_ref, sems):
    columns = pl.ds(start, near_ref.shape[1])
    loads = share_copies(far_ref.at[:, columns], near_ref, sems, (0, 1))
    start_all(loads)
    wait_all(loads)


def load_kernel(share, far_ref, *refs):
    near_ref, sems = refs[-2:]
    loads = share_copies(far_ref, near_ref, sems, share)
    start_all(loads)
    wait_all(loads)


def pack(low):
    coefs = low[:, DTR:]
    high = coefs.astype(BF16)
    rest = (coefs - high.astype(F32)).astype(BF16)
    return jnp.concatenate([low[:, :DTR].astype(BF16), high, rest], axis=1)


def unpack(packed):
    wide = packed.astype(F32)
    count = (wide.shape[1] - DTR) // 2
    coefs = wide[:, DTR : DTR + count] + wide[:, DTR + count :]
    return jnp.concatenate([wide[:, :DTR], coefs], axis=1)


def add_kernel(count, *refs):
    total = refs[0][...]
    for ref in refs[1:count]:
        total = total + (ref[...] if ref.dtype == F32 else unpack(ref[...]))
    refs[-2][...] = total
    refs[-1][...] = pack(total)


def places(block, turn, height, span):
    line = lax.broadcasted_iota(jnp.int32, (height, block.shape[1]), 0)
    return jnp.where(line == block * span + turn, 1.0, 0.0)


def fresh_input(both_ref, block, turn, rows, rows_dev):
    return jnp.dot(
        places(block, turn, rows, rows_dev).astype(BF16),
        both_ref[0].astype(BF16),
        preferred_element_type=F32,
    )


def conv_kernel(
    rows_dev,
    both_ref,
    spot_ref,
    conv_ref,
    taps_ref,
    offset_ref,
    coef_ref,
    keep_ref,
    send_ref,
    mixed_ref,
    low_ref,
):
    index = lax.axis_index("weight")
    rows = conv_ref.shape[1]
    kept = mixed_ref.shape[0]
    block = jnp.bitwise_xor(spot_ref[0:1, :], index)
    fresh = fresh_input(both_ref, block, spot_ref[1:2, :], rows, rows_dev)
    states = [conv_ref[k].astype(F32) for k in range(TAPS - 1)] + [fresh]
    total = states[0] * taps_ref[0:1, :]
    for k in range(1, TAPS):
        total = total + states[k] * taps_ref[k : k + 1, :]
    mixed = silu(total + offset_ref[...]).astype(BF16)
    line = lax.broadcasted_iota(jnp.int32, (kept, rows), 0)
    column = lax.broadcasted_iota(jnp.int32, (kept, rows), 1)
    chosen = (line // LIVE_MAX) * rows_dev + line % LIVE_MAX == column
    mixed = jnp.dot(
        jnp.where(chosen, 1.0, 0.0).astype(BF16), mixed, preferred_element_type=F32
    ).astype(BF16)
    mixed_ref[...] = mixed
    low_ref[...] = lax.dot_general(
        mixed, coef_ref[...], (((1,), (1,)), ((), ())), preferred_element_type=F32
    )
    half = keep_ref.shape[0]
    core = side(index)
    keep_ref[...] = low_ref[pl.ds(pl.multiple_of(core * half, 8), half), :]
    send_ref[...] = low_ref[pl.ds(pl.multiple_of((1 - core) * half, 8), half), :]


def gate_kernel(live_ref, both_ref, spot_ref, gate_ref, alive_ref):
    for b in range(live_ref.shape[0]):
        for t in range(LIVE_MAX):
            r = b * LIVE_MAX + t
            alive_ref[r : r + 1, :] = jnp.full(
                (1, LANES), jnp.where(t < live_ref[b], 1.0, 0.0)
            )
    block = jnp.bitwise_xor(spot_ref[0:1, :], lax.axis_index("weight"))
    gate_ref[...] = jnp.dot(
        places(block, spot_ref[1:2, :], gate_ref.shape[0], LIVE_MAX),
        silu(both_ref[1]),
        precision=lax.Precision.HIGHEST,
        preferred_element_type=F32,
    )


def taps_kernel(live_ref, both_ref, spot_ref, conv_ref, new_conv_ref, alive_ref):
    blocks = live_ref.shape[0]
    rows = conv_ref.shape[1]
    rows_dev = rows // blocks
    block = jnp.bitwise_xor(spot_ref[0:1, :], lax.axis_index("weight"))
    row_iota = lax.broadcasted_iota(jnp.int32, (rows_dev, LANES), 0)
    for b in range(blocks):
        alive_ref[b * rows_dev : (b + 1) * rows_dev, :] = jnp.where(
            row_iota < live_ref[b], 1.0, 0.0
        )
    alive = alive_ref[:, 0:1] > 0.0
    fresh = fresh_input(both_ref, block, spot_ref[1:2, :], rows, rows_dev)
    states = [conv_ref[k].astype(F32) for k in range(TAPS - 1)] + [fresh]
    for k in range(TAPS - 1):
        new_conv_ref[k] = jnp.where(alive, states[k + 1], states[k]).astype(BF16)


def join_low(mine_ref, other_ref, low_ref):
    half = mine_ref.shape[0]
    core = side(lax.axis_index("weight"))
    low_ref[pl.ds(pl.multiple_of(core * half, 8), half), :] = mine_ref[...]
    low_ref[pl.ds(pl.multiple_of((1 - core) * half, 8), half), :] = unpack(other_ref[...])


def readout_kernel(
    mine_ref,
    other_ref,
    spot_ref,
    mixed_ref,
    gate_ref,
    alive_ref,
    step_weight_ref,
    bias_ref,
    rates_ref,
    skip_ref,
    state_ref,
    first_ref,
    last_ref,
    keep_ref,
    send_ref,
    step_ref,
    low_ref,
    read_ref,
    fold_ref,
):
    kept = mixed_ref.shape[0]
    blocks = kept // LIVE_MAX
    rows_dev = state_ref.shape[0] // blocks
    join_low(mine_ref, other_ref, low_ref)
    step_size = softplus(
        jnp.dot(
            low_ref[:, :DTR].astype(BF16), step_weight_ref[...], preferred_element_type=F32
        )
        + bias_ref[...]
    )
    step_ref[...] = step_size
    coefs = low_ref[:, DTR:]
    both_coefs = jnp.sum(coefs[:, :NSTATE] * coefs[:, NSTATE:], axis=1, keepdims=True)
    out_coefs = coefs[:, NSTATE:].T
    x_wide = mixed_ref[...].astype(F32)
    rates = -jnp.exp(rates_ref[...])
    for b in range(blocks):
        for t in range(LIVE_MAX):
            r = b * LIVE_MAX + t
            wide = state_ref[b * rows_dev + t].astype(F32)
            decayed = jnp.exp(step_size[r : r + 1, :] * rates) * wide
            read_ref[r : r + 1, :] = jnp.sum(
                out_coefs[:, r : r + 1] * decayed, axis=0, keepdims=True
            )
    readout = read_ref[...] + (both_coefs * step_size + skip_ref[...]) * x_wide
    gated = jnp.where(alive_ref[:, 0:1] > 0.0, readout * gate_ref[...], 0.0).astype(BF16)
    block = jnp.bitwise_xor(spot_ref[:, 0:1], lax.axis_index("weight"))
    column = lax.broadcasted_iota(jnp.int32, (kept, kept), 1)
    pick = jnp.where(column == block * LIVE_MAX + spot_ref[:, 1:2], 1.0, 0.0).astype(BF16)
    picked = jnp.dot(pick, gated, preferred_element_type=F32).astype(BF16)
    half = kept // 2
    near = first_ref.shape[1]
    pieces = (near + last_ref.shape[1]) // LANES
    group = 4
    for c in range(0, pieces, group):
        start = c * LANES
        if start < near:
            weight = first_ref[:, start : start + group * LANES]
        else:
            weight = last_ref[:, start - near : start - near + group * LANES]
        part = jnp.dot(picked, weight, preferred_element_type=F32)
        for g in range(group):
            piece = part[:, g * LANES : (g + 1) * LANES]
            fold_ref[pl.ds(c + g, kept, stride=pieces + 1), :] = piece
    for r in range(half):
        rows = slice(r * pieces, (r + 1) * pieces)
        start = r * (pieces + 1)
        keep_ref[rows] = fold_ref[start : start + pieces]
        start = (half + r) * (pieces + 1)
        send_ref[rows] = fold_ref[start : start + pieces].astype(BF16)


def state_kernel(
    live_ref,
    mine_ref,
    other_ref,
    mixed_ref,
    step_ref,
    rates_ref,
    state_ref,
    new_state_ref,
    token_ref,
    low_ref,
):
    token_ref[...] = jnp.zeros_like(token_ref)
    blocks = live_ref.shape[0]
    rows_dev = state_ref.shape[0] // blocks
    join_low(mine_ref, other_ref, low_ref)
    in_coefs = low_ref[:, DTR : DTR + NSTATE].T
    step_size = step_ref[...]
    driven = step_size * mixed_ref[...].astype(F32)
    rates = -jnp.exp(rates_ref[...])
    for b in range(blocks):
        for t in range(LIVE_MAX):
            r = b * LIVE_MAX + t
            wide = state_ref[b * rows_dev + t].astype(F32)
            updated = (
                jnp.exp(step_size[r : r + 1, :] * rates) * wide
                + in_coefs[:, r : r + 1] * driven[r : r + 1, :]
            )
            new_state_ref[b * rows_dev + t] = jnp.where(
                t < live_ref[b], updated, wide
            ).astype(BF16)
        for t in range(LIVE_MAX, rows_dev):
            new_state_ref[b * rows_dev + t] = state_ref[b * rows_dev + t]


def sum_kernel(count, skipped, *refs):
    parts, outs = refs[:count], refs[count + skipped :]
    size = outs[0].shape[0]
    for k, out in enumerate(outs):
        rows = slice(k * size, (k + 1) * size)
        total = parts[0][rows]
        for part in parts[1:]:
            total = total + part[rows].astype(F32)
        out[...] = total.astype(out.dtype)


def last_sum_kernel(*refs):
    hidden_ref, parts, out_ref, fold_ref = refs[0], refs[1:-2], refs[-2], refs[-1]
    total = parts[0][...]
    for part in parts[1:]:
        total = total + part[...].astype(F32)
    rows, pieces = spread(total, fold_ref)
    for c in range(pieces):
        span = slice(c * LANES, (c + 1) * LANES)
        wide = hidden_ref[:, span].astype(F32)
        own = wide[:rows] + fold_ref[pl.ds(c, rows, stride=pieces + 1), :]
        out_ref[:, span] = jnp.concatenate([own, wide[rows:]], axis=0).astype(BF16)


def body(
    hidden,
    norm_gain,
    in_weight,
    conv_weight,
    conv_offset,
    coef_weight,
    step_weight,
    step_bias,
    log_rates,
    skip_gain,
    out_weight,
    ssm_state,
    conv_state,
    live_counts,
):
    devices = lax.axis_size("weight")
    rows_dev, width = hidden.shape
    rows = devices * rows_dev
    kept = devices * LIVE_MAX
    channels = in_weight.shape[2]
    low_width = coef_weight.shape[1]
    phases = gather_phases(devices)
    spots = spots_of(order_of(phases))
    scatter = scatter_phases(devices)
    ends = spots_of(order_of(scatter[::-1] + [(1,)])).T
    pieces = width // LANES
    slab = LIVE_MAX * pieces

    weight_shape = pltpu.VMEM(in_weight.shape, BF16)

    def load(share, so_far=None):
        return call(
            functools.partial(load_kernel, share),
            weight_shape,
            (in_weight,),
            far=1,
            scratch=[pltpu.SemaphoreType.DMA((4,))],
            limit=43,
            after=() if so_far is None else (so_far,),
            aliases={} if so_far is None else {1: 0},
        )

    gathered = call(
        norm_kernel,
        pltpu.VMEM((slab, LANES), BF16),
        (hidden, norm_gain.reshape(1, width)),
        far=2,
        scratch=[
            pltpu.VMEM((slab + LIVE_MAX, LANES), F32),
            pltpu.VMEM(hidden.shape, BF16),
            pltpu.VMEM((1, width), F32),
            pltpu.SemaphoreType.DMA((2,)),
        ],
        limit=60,
    )
    done, near_weight = 0.0, None
    for k, phase in enumerate(phases[:-1]):
        until = CORE_SHARE if k == len(phases) - 2 else done + (CORE_SHARE - done) * FIRST_SHARE
        near_weight = load((done, until), near_weight)
        done = until
        gathered = join(
            [gathered] + [swap(gathered, s, devices) for s in phase], (near_weight,)
        )
    near_weight = load((done, 1.0), near_weight)
    folded = [pltpu.VMEM((kept // 2 * (pieces + 1), LANES), F32)]
    half = call(half_kernel, shape((kept // 2, width)), (gathered,), scratch=folded, limit=12)
    normed = call(
        unfold_kernel,
        shape((kept, width), BF16),
        (half, swap(gathered, 1, devices)),
        scratch=folded,
        limit=12,
        after=(near_weight,),
    )
    both = jnp.einsum("rd,dbc->brc", normed, near_weight, preferred_element_type=F32)

    conv_turned = conv_state.transpose(1, 0, 2)
    keep, send, mixed_x = call(
        functools.partial(conv_kernel, rows_dev),
        (
            shape((kept // 2, low_width)),
            shape((kept // 2, low_width)),
            shape((kept, channels), BF16),
        ),
        (
            both,
            spots,
            conv_turned,
            conv_weight,
            conv_offset.reshape(1, channels),
            coef_weight.T,
        ),
        scratch=[pltpu.VMEM((kept, low_width), F32)],
        limit=16,
    )
    gate, alive = call(
        gate_kernel,
        (shape((kept, channels)), shape((kept, LANES))),
        (live_counts, both, spots),
        scalars=1,
    )
    new_conv = call(
        taps_kernel,
        shape((TAPS - 1, rows, channels), BF16),
        (live_counts, both, spots, conv_turned),
        scalars=1,
        scratch=[pltpu.VMEM((rows, LANES), F32)],
    )

    packed_width = low_width + 2 * NSTATE

    def add(*parts, after=()):
        return call(
            functools.partial(add_kernel, len(parts)),
            (shape(parts[0].shape), shape((kept // 2, packed_width), BF16)),
            parts,
            after=after,
        )

    low, packed = add(keep, swap(send, 1, devices), after=(gate,))
    exchanges = sum_phases(devices)
    first_columns = width * FIRST_COLUMNS // 16 if len(exchanges) > 1 else width // 2
    near_out = [
        call(
            functools.partial(columns_kernel, start),
            pltpu.VMEM((channels, count), BF16),
            (out_weight,),
            far=1,
            scratch=[pltpu.SemaphoreType.DMA((4,))],
            limit=50,
        )
        for start, count in ((0, first_columns), (first_columns, width - first_columns))
    ]
    for k, phase in enumerate(exchanges):
        after = (near_out[0],) if k == 0 else (near_out[1],)
        low, packed = add(low, *[swap(packed, s, devices) for s in phase], after=after)
    other = swap(packed, 1, devices)

    size = kept // 2 * pieces
    keep, send, step_size = call(
        readout_kernel,
        (shape((size, LANES)), shape((size, LANES), BF16), shape((kept, channels))),
        (
            low,
            other,
            ends,
            mixed_x,
            gate,
            alive,
            step_weight,
            step_bias.reshape(1, channels),
            log_rates,
            skip_gain.reshape(1, channels),
            ssm_state,
            *near_out,
        ),
        scratch=[
            pltpu.VMEM((kept, low_width), F32),
            pltpu.VMEM((kept, channels), F32),
            pltpu.VMEM((kept * (pieces + 1), LANES), F32),
        ],
        limit=24,
    )
    new_state, token = call(
        state_kernel,
        (shape(ssm_state.shape, BF16), shape((8, LANES))),
        (live_counts, low, other, mixed_x, step_size, log_rates, ssm_state),
        scalars=1,
        scratch=[pltpu.VMEM((kept, low_width), F32)],
        limit=16,
    )

    total = (keep, swap(send, 1, devices))
    for k, phase in enumerate(scatter):
        size //= len(phase) + 1
        parts = call(
            functools.partial(sum_kernel, len(total), 1 if k == 1 else 0),
            (shape((size, LANES)),) + (shape((size, LANES), BF16),) * len(phase),
            total,
            after=(token,) if k == 1 else (),
        )
        total = (parts[0],) + tuple(swap(p, s, devices) for p, s in zip(parts[1:], phase))
    mixed = call(
        last_sum_kernel,
        shape(hidden.shape, BF16),
        (hidden,) + total,
        scratch=[pltpu.VMEM((slab + LIVE_MAX, LANES), F32)],
    )
    return (mixed, new_state, new_conv.transpose(1, 0, 2))


def solution(mesh):
    in_specs = (
        P(("groups", "weight"), None),
        P(),
        P(None, None, "weight"),
        P(None, "weight"),
        P("weight"),
        P("weight", None),
        P(None, "weight"),
        P("weight"),
        P(None, "weight"),
        P("weight"),
        P("weight", None),
        P("groups", None, "weight"),
        P("groups", None, "weight"),
        P("groups"),
    )
    out_specs = (
        P(("groups", "weight"), None),
        P("groups", None, "weight"),
        P("groups", None, "weight"),
    )
    return jax.shard_map(body, mesh=mesh, in_specs=in_specs, out_specs=out_specs, check_vma=False)
```

```python
import functools

import jax
import jax.numpy as jnp
from jax import lax
from jax.experimental import pallas as pl
from jax.experimental.pallas import tpu as pltpu
from jax.sharding import PartitionSpec as P

NSTATE = 16
DTR = 512
LIVE_MAX = 3
TAPS = 4
LANES = 128
MIB = 1024 * 1024
CORE_SHARE = 0.9375
FIRST_SHARE = 0.4
FIRST_COLUMNS = 5
BF16 = jnp.bfloat16
F32 = jnp.float32


def chip_steps(devices):
    steps, high = [], devices
    while high > 2:
        if high >= 8:
            steps.append((high // 4, high // 2))
            high //= 4
        else:
            steps.append((high // 2,))
            high //= 2
    steps = [tuple(step) for step in steps]
    if len(steps[-1]) == 1:
        bits = [bit for step in steps for bit in step]
        bits.sort()
        top = bits.pop()
        steps = [(top,)] + [tuple(bits[k : k + 2]) for k in range(len(bits) - 2, -1, -2)]
    return steps


def gather_phases(devices):
    whole = [step if len(step) == 1 else (sum(step), step[1], step[0]) for step in chip_steps(devices)]
    return whole + [(1,)]


def scatter_phases(devices):
    whole = [step if len(step) == 1 else (step[1], step[0], sum(step)) for step in chip_steps(devices)]
    return whole[::-1]


def sum_phases(devices):
    return [
        (step[0] + 1,) if len(step) == 1 else (step[0] + 1, step[1] + 1, sum(step))
        for step in chip_steps(devices)
    ]


def order_of(phases):
    order = [0]
    for phase in phases:
        order = order + [o ^ s for s in phase for o in order]
    return order


def spots_of(order):
    return jnp.array(
        [[o for o in order for _ in range(LIVE_MAX)], list(range(LIVE_MAX)) * len(order)],
        jnp.int32,
    )


def side(index):
    for shift in (4, 2, 1):
        index = jnp.bitwise_xor(index, lax.shift_right_logical(index, shift))
    return jnp.bitwise_and(index, 1)


def swap(value, shift, devices):
    return lax.ppermute(value, "weight", [(i, i ^ shift) for i in range(devices)])


def silu(v):
    return v / (1.0 + jnp.exp(-v))


def softplus(v):
    return jnp.maximum(v, 0.0) + jnp.log1p(jnp.exp(-jnp.abs(v)))


def vmem(count):
    return [pl.BlockSpec(memory_space=pltpu.VMEM)] * count


def shape(dims, kind=F32):
    return jax.ShapeDtypeStruct(dims, kind)


def call(kernel, outs, operands, scalars=0, far=0, scratch=(), limit=8, after=(), aliases=None):
    many = isinstance(outs, tuple)
    return pl.pallas_call(
        kernel,
        out_shape=outs,
        in_specs=[pl.BlockSpec(memory_space=pltpu.SMEM)] * scalars
        + vmem(len(operands) - scalars - far)
        + [pl.BlockSpec(memory_space=pl.ANY)] * (far + len(after)),
        out_specs=tuple(vmem(len(outs))) if many else vmem(1)[0],
        scratch_shapes=list(scratch),
        input_output_aliases=aliases or {},
        compiler_params=pltpu.CompilerParams(vmem_limit_bytes=limit * MIB),
    )(*operands, *after)


def share_copies(far_ref, near_ref, sems, share):
    rows = far_ref.shape[0]
    start, end = (int(rows * part) // 8 * 8 for part in share)
    count = sems.shape[0]
    size = (end - start) // count
    spans = [pl.ds(start + size * k, size) for k in range(count)]
    return [
        pltpu.make_async_copy(far_ref.at[span], near_ref.at[span], sems.at[k])
        for k, span in enumerate(spans)
    ]


def start_all(copies):
    for copy in copies:
        copy.start()


def wait_all(copies):
    for copy in copies:
        copy.wait()


def fold(wide, fold_ref, folded_ref):
    rows, pieces = wide.shape[0], wide.shape[1] // LANES
    for c in range(pieces):
        fold_ref[pl.ds(c, rows, stride=pieces + 1), :] = wide[:, c * LANES : (c + 1) * LANES]
    for r in range(rows):
        start = r * (pieces + 1)
        folded_ref[r * pieces : (r + 1) * pieces] = fold_ref[start : start + pieces].astype(
            folded_ref.dtype
        )


def spread(folded, fold_ref):
    rows = fold_ref.shape[0] - folded.shape[0]
    pieces = folded.shape[0] // rows
    for r in range(rows):
        start = r * (pieces + 1)
        fold_ref[start : start + pieces] = folded[r * pieces : (r + 1) * pieces].astype(F32)
    return rows, pieces


def norm_kernel(far_hidden_ref, far_gain_ref, out_ref, fold_ref, hidden_ref, gain_ref, sems):
    copies = [
        pltpu.make_async_copy(far_hidden_ref, hidden_ref, sems.at[0]),
        pltpu.make_async_copy(far_gain_ref, gain_ref, sems.at[1]),
    ]
    start_all(copies)
    wait_all(copies)
    wide = hidden_ref[...].astype(F32)[:LIVE_MAX]
    factor = lax.rsqrt(jnp.mean(wide * wide, axis=-1, keepdims=True) + 1e-05)
    fold(wide * factor * gain_ref[...], fold_ref, out_ref)


def join_kernel(count, *refs):
    start = 0
    for ref in refs[:count]:
        refs[-1][start : start + ref.shape[0]] = ref[...]
        start += ref.shape[0]


def join(parts, after=()):
    rows = sum(part.shape[0] for part in parts)
    return call(
        functools.partial(join_kernel, len(parts)),
        shape((rows, parts[0].shape[1]), parts[0].dtype),
        parts,
        after=after,
    )


def half_kernel(mine_ref, out_ref, fold_ref):
    rows, pieces = spread(mine_ref, fold_ref)
    for c in range(pieces):
        out_ref[:, c * LANES : (c + 1) * LANES] = fold_ref[pl.ds(c, rows, stride=pieces + 1), :]


def unfold_kernel(half_ref, other_ref, _, out_ref, fold_ref):
    rows, pieces = spread(other_ref, fold_ref)
    for c in range(pieces):
        span = slice(c * LANES, (c + 1) * LANES)
        other = fold_ref[pl.ds(c, rows, stride=pieces + 1), :]
        out_ref[:, span] = jnp.concatenate([half_ref[:, span], other], axis=0).astype(BF16)


def columns_kernel(start, far_ref, near_ref, sems):
    columns = pl.ds(start, near_ref.shape[1])
    loads = share_copies(far_ref.at[:, columns], near_ref, sems, (0, 1))
    start_all(loads)
    wait_all(loads)


def load_kernel(share, far_ref, *refs):
    near_ref, sems = refs[-2:]
    loads = share_copies(far_ref, near_ref, sems, share)
    start_all(loads)
    wait_all(loads)


def pack(low):
    coefs = low[:, DTR:]
    high = coefs.astype(BF16)
    rest = (coefs - high.astype(F32)).astype(BF16)
    return jnp.concatenate([low[:, :DTR].astype(BF16), high, rest], axis=1)


def unpack(packed):
    wide = packed.astype(F32)
    count = (wide.shape[1] - DTR) // 2
    coefs = wide[:, DTR : DTR + count] + wide[:, DTR + count :]
    return jnp.concatenate([wide[:, :DTR], coefs], axis=1)


def add_kernel(count, *refs):
    total = refs[0][...]
    for ref in refs[1:count]:
        total = total + (ref[...] if ref.dtype == F32 else unpack(ref[...]))
    refs[-2][...] = total
    refs[-1][...] = pack(total)


def places(block, turn, height, span):
    line = lax.broadcasted_iota(jnp.int32, (height, block.shape[1]), 0)
    return jnp.where(line == block * span + turn, 1.0, 0.0)


def fresh_input(both_ref, block, turn, rows, rows_dev):
    return jnp.dot(
        places(block, turn, rows, rows_dev).astype(BF16),
        both_ref[0].astype(BF16),
        preferred_element_type=F32,
    )


def conv_kernel(
    rows_dev,
    both_ref,
    spot_ref,
    conv_ref,
    taps_ref,
    offset_ref,
    coef_ref,
    keep_ref,
    send_ref,
    mixed_ref,
    low_ref,
):
    index = lax.axis_index("weight")
    rows = conv_ref.shape[1]
    kept = mixed_ref.shape[0]
    block = jnp.bitwise_xor(spot_ref[0:1, :], index)
    fresh = fresh_input(both_ref, block, spot_ref[1:2, :], rows, rows_dev)
    states = [conv_ref[k].astype(F32) for k in range(TAPS - 1)] + [fresh]
    total = states[0] * taps_ref[0:1, :]
    for k in range(1, TAPS):
        total = total + states[k] * taps_ref[k : k + 1, :]
    mixed = silu(total + offset_ref[...]).astype(BF16)
    line = lax.broadcasted_iota(jnp.int32, (kept, rows), 0)
    column = lax.broadcasted_iota(jnp.int32, (kept, rows), 1)
    chosen = (line // LIVE_MAX) * rows_dev + line % LIVE_MAX == column
    mixed = jnp.dot(
        jnp.where(chosen, 1.0, 0.0).astype(BF16), mixed, preferred_element_type=F32
    ).astype(BF16)
    mixed_ref[...] = mixed
    low_ref[...] = lax.dot_general(
        mixed, coef_ref[...], (((1,), (1,)), ((), ())), preferred_element_type=F32
    )
    half = keep_ref.shape[0]
    core = side(index)
    keep_ref[...] = low_ref[pl.ds(pl.multiple_of(core * half, 8), half), :]
    send_ref[...] = low_ref[pl.ds(pl.multiple_of((1 - core) * half, 8), half), :]


def gate_kernel(live_ref, both_ref, spot_ref, mixed_ref, gate_ref, alive_ref, x_ref):
    x_ref[...] = mixed_ref[...].astype(F32)
    for b in range(live_ref.shape[0]):
        for t in range(LIVE_MAX):
            r = b * LIVE_MAX + t
            alive_ref[r : r + 1, :] = jnp.full(
                (1, LANES), jnp.where(t < live_ref[b], 1.0, 0.0)
            )
    block = jnp.bitwise_xor(spot_ref[0:1, :], lax.axis_index("weight"))
    gate_ref[...] = jnp.dot(
        places(block, spot_ref[1:2, :], gate_ref.shape[0], LIVE_MAX),
        silu(both_ref[1]),
        precision=lax.Precision.HIGHEST,
        preferred_element_type=F32,
    )


def taps_kernel(live_ref, both_ref, spot_ref, conv_ref, new_conv_ref, alive_ref):
    blocks = live_ref.shape[0]
    rows = conv_ref.shape[1]
    rows_dev = rows // blocks
    block = jnp.bitwise_xor(spot_ref[0:1, :], lax.axis_index("weight"))
    row_iota = lax.broadcasted_iota(jnp.int32, (rows_dev, LANES), 0)
    for b in range(blocks):
        alive_ref[b * rows_dev : (b + 1) * rows_dev, :] = jnp.where(
            row_iota < live_ref[b], 1.0, 0.0
        )
    alive = alive_ref[:, 0:1] > 0.0
    fresh = fresh_input(both_ref, block, spot_ref[1:2, :], rows, rows_dev)
    states = [conv_ref[k].astype(F32) for k in range(TAPS - 1)] + [fresh]
    for k in range(TAPS - 1):
        new_conv_ref[k] = jnp.where(alive, states[k + 1], states[k]).astype(BF16)


def half_rows(which, size):
    return pl.ds(pl.multiple_of(which * size, 8), size)


def join_halves(mine, other, out_ref):
    size = mine.shape[0]
    mine_side = side(lax.axis_index("weight"))
    out_ref[half_rows(mine_side, size), :] = mine
    out_ref[half_rows(1 - mine_side, size), :] = other


def gated_rows(which, low, weights, rows_refs, state_ref, read_ref):
    step_weight_ref, bias_ref, rates_ref, skip_ref = weights
    size = low.shape[0]
    x_wide, gate, alive = (ref[half_rows(which, size), :] for ref in rows_refs)
    blocks = size // LIVE_MAX
    rows_dev = state_ref.shape[0] // (2 * blocks)
    step_size = softplus(
        jnp.dot(low[:, :DTR].astype(BF16), step_weight_ref[...], preferred_element_type=F32)
        + bias_ref[...]
    )
    coefs = low[:, DTR:]
    both_coefs = jnp.sum(coefs[:, :NSTATE] * coefs[:, NSTATE:], axis=1, keepdims=True)
    out_coefs = coefs[:, NSTATE:].T
    rates = -jnp.exp(rates_ref[...])
    first = which * (blocks * rows_dev)
    for b in range(blocks):
        for t in range(LIVE_MAX):
            r = b * LIVE_MAX + t
            wide = state_ref[first + (b * rows_dev + t)].astype(F32)
            decayed = jnp.exp(step_size[r : r + 1, :] * rates) * wide
            read_ref[r : r + 1, :] = jnp.sum(
                out_coefs[:, r : r + 1] * decayed, axis=0, keepdims=True
            )
    readout = read_ref[...] + (both_coefs * step_size + skip_ref[...]) * x_wide
    return step_size, jnp.where(alive[:, 0:1] > 0.0, readout * gate, 0.0)


def own_kernel(
    low_ref,
    x_ref,
    gate_ref,
    alive_ref,
    step_weight_ref,
    bias_ref,
    rates_ref,
    skip_ref,
    state_ref,
    gated_ref,
    step_ref,
    read_ref,
):
    step_ref[...], gated_ref[...] = gated_rows(
        side(lax.axis_index("weight")),
        low_ref[...],
        (step_weight_ref, bias_ref, rates_ref, skip_ref),
        (x_ref, gate_ref, alive_ref),
        state_ref,
        read_ref,
    )


def readout_kernel(
    other_ref,
    x_ref,
    gate_ref,
    alive_ref,
    step_weight_ref,
    bias_ref,
    rates_ref,
    skip_ref,
    state_ref,
    own_ref,
    spot_ref,
    first_ref,
    last_ref,
    keep_ref,
    send_ref,
    step_ref,
    read_ref,
    gated_ref,
    fold_ref,
):
    kept = x_ref.shape[0]
    step_ref[...], gated = gated_rows(
        1 - side(lax.axis_index("weight")),
        unpack(other_ref[...]),
        (step_weight_ref, bias_ref, rates_ref, skip_ref),
        (x_ref, gate_ref, alive_ref),
        state_ref,
        read_ref,
    )
    join_halves(own_ref[...], gated, gated_ref)
    block = jnp.bitwise_xor(spot_ref[:, 0:1], lax.axis_index("weight"))
    column = lax.broadcasted_iota(jnp.int32, (kept, kept), 1)
    pick = jnp.where(column == block * LIVE_MAX + spot_ref[:, 1:2], 1.0, 0.0).astype(BF16)
    picked = jnp.dot(
        pick, gated_ref[...].astype(BF16), preferred_element_type=F32
    ).astype(BF16)
    half = kept // 2
    near = first_ref.shape[1]
    pieces = (near + last_ref.shape[1]) // LANES
    group = 4
    for c in range(0, pieces, group):
        start = c * LANES
        if start < near:
            weight = first_ref[:, start : start + group * LANES]
        else:
            weight = last_ref[:, start - near : start - near + group * LANES]
        part = jnp.dot(picked, weight, preferred_element_type=F32)
        for g in range(group):
            piece = part[:, g * LANES : (g + 1) * LANES]
            fold_ref[pl.ds(c + g, kept, stride=pieces + 1), :] = piece
    for r in range(half):
        rows = slice(r * pieces, (r + 1) * pieces)
        start = r * (pieces + 1)
        keep_ref[rows] = fold_ref[start : start + pieces]
        start = (half + r) * (pieces + 1)
        send_ref[rows] = fold_ref[start : start + pieces].astype(BF16)


def state_kernel(
    live_ref,
    mine_ref,
    other_ref,
    x_ref,
    own_step_ref,
    other_step_ref,
    rates_ref,
    state_ref,
    new_state_ref,
    token_ref,
    low_ref,
    step_ref,
):
    token_ref[...] = jnp.zeros_like(token_ref)
    blocks = live_ref.shape[0]
    rows_dev = state_ref.shape[0] // blocks
    join_halves(mine_ref[...], unpack(other_ref[...]), low_ref)
    join_halves(own_step_ref[...], other_step_ref[...], step_ref)
    in_coefs = low_ref[:, DTR : DTR + NSTATE].T
    step_size = step_ref[...]
    driven = step_size * x_ref[...]
    rates = -jnp.exp(rates_ref[...])
    for b in range(blocks):
        for t in range(LIVE_MAX):
            r = b * LIVE_MAX + t
            wide = state_ref[b * rows_dev + t].astype(F32)
            updated = (
                jnp.exp(step_size[r : r + 1, :] * rates) * wide
                + in_coefs[:, r : r + 1] * driven[r : r + 1, :]
            )
            new_state_ref[b * rows_dev + t] = jnp.where(
                t < live_ref[b], updated, wide
            ).astype(BF16)
        for t in range(LIVE_MAX, rows_dev):
            new_state_ref[b * rows_dev + t] = state_ref[b * rows_dev + t]


def sum_kernel(count, skipped, *refs):
    parts, outs = refs[:count], refs[count + skipped :]
    size = outs[0].shape[0]
    for k, out in enumerate(outs):
        rows = slice(k * size, (k + 1) * size)
        total = parts[0][rows]
        for part in parts[1:]:
            total = total + part[rows].astype(F32)
        out[...] = total.astype(out.dtype)


def last_sum_kernel(*refs):
    hidden_ref, parts, out_ref, fold_ref = refs[0], refs[1:-2], refs[-2], refs[-1]
    total = parts[0][...]
    for part in parts[1:]:
        total = total + part[...].astype(F32)
    rows, pieces = spread(total, fold_ref)
    for c in range(pieces):
        span = slice(c * LANES, (c + 1) * LANES)
        wide = hidden_ref[:, span].astype(F32)
        own = wide[:rows] + fold_ref[pl.ds(c, rows, stride=pieces + 1), :]
        out_ref[:, span] = jnp.concatenate([own, wide[rows:]], axis=0).astype(BF16)


def body(
    hidden,
    norm_gain,
    in_weight,
    conv_weight,
    conv_offset,
    coef_weight,
    step_weight,
    step_bias,
    log_rates,
    skip_gain,
    out_weight,
    ssm_state,
    conv_state,
    live_counts,
):
    devices = lax.axis_size("weight")
    rows_dev, width = hidden.shape
    rows = devices * rows_dev
    kept = devices * LIVE_MAX
    channels = in_weight.shape[2]
    low_width = coef_weight.shape[1]
    phases = gather_phases(devices)
    spots = spots_of(order_of(phases))
    scatter = scatter_phases(devices)
    ends = spots_of(order_of(scatter[::-1] + [(1,)])).T
    pieces = width // LANES
    slab = LIVE_MAX * pieces

    weight_shape = pltpu.VMEM(in_weight.shape, BF16)

    def load(share, so_far=None):
        return call(
            functools.partial(load_kernel, share),
            weight_shape,
            (in_weight,),
            far=1,
            scratch=[pltpu.SemaphoreType.DMA((4,))],
            limit=43,
            after=() if so_far is None else (so_far,),
            aliases={} if so_far is None else {1: 0},
        )

    gathered = call(
        norm_kernel,
        pltpu.VMEM((slab, LANES), BF16),
        (hidden, norm_gain.reshape(1, width)),
        far=2,
        scratch=[
            pltpu.VMEM((slab + LIVE_MAX, LANES), F32),
            pltpu.VMEM(hidden.shape, BF16),
            pltpu.VMEM((1, width), F32),
            pltpu.SemaphoreType.DMA((2,)),
        ],
        limit=60,
    )
    done, near_weight = 0.0, None
    for k, phase in enumerate(phases[:-1]):
        until = CORE_SHARE if k == len(phases) - 2 else done + (CORE_SHARE - done) * FIRST_SHARE
        near_weight = load((done, until), near_weight)
        done = until
        gathered = join(
            [gathered] + [swap(gathered, s, devices) for s in phase], (near_weight,)
        )
    near_weight = load((done, 1.0), near_weight)
    folded = [pltpu.VMEM((kept // 2 * (pieces + 1), LANES), F32)]
    half = call(half_kernel, shape((kept // 2, width)), (gathered,), scratch=folded, limit=12)
    normed = call(
        unfold_kernel,
        shape((kept, width), BF16),
        (half, swap(gathered, 1, devices)),
        scratch=folded,
        limit=12,
        after=(near_weight,),
    )
    both = jnp.einsum("rd,dbc->brc", normed, near_weight, preferred_element_type=F32)

    conv_turned = conv_state.transpose(1, 0, 2)
    keep, send, mixed_x = call(
        functools.partial(conv_kernel, rows_dev),
        (
            shape((kept // 2, low_width)),
            shape((kept // 2, low_width)),
            shape((kept, channels), BF16),
        ),
        (
            both,
            spots,
            conv_turned,
            conv_weight,
            conv_offset.reshape(1, channels),
            coef_weight.T,
        ),
        scratch=[pltpu.VMEM((kept, low_width), F32)],
        limit=16,
    )
    gate, alive, x_wide = call(
        gate_kernel,
        (shape((kept, channels)), shape((kept, LANES)), shape((kept, channels))),
        (live_counts, both, spots, mixed_x),
        scalars=1,
    )
    new_conv = call(
        taps_kernel,
        shape((TAPS - 1, rows, channels), BF16),
        (live_counts, both, spots, conv_turned),
        scalars=1,
        scratch=[pltpu.VMEM((rows, LANES), F32)],
    )

    packed_width = low_width + 2 * NSTATE

    def add(*parts, after=()):
        return call(
            functools.partial(add_kernel, len(parts)),
            (shape(parts[0].shape), shape((kept // 2, packed_width), BF16)),
            parts,
            after=after,
        )

    low, packed = add(keep, swap(send, 1, devices), after=(gate,))
    exchanges = sum_phases(devices)
    first_columns = width * FIRST_COLUMNS // 16 if len(exchanges) > 1 else width // 2
    near_out = [
        call(
            functools.partial(columns_kernel, start),
            pltpu.VMEM((channels, count), BF16),
            (out_weight,),
            far=1,
            scratch=[pltpu.SemaphoreType.DMA((4,))],
            limit=50,
        )
        for start, count in ((0, first_columns), (first_columns, width - first_columns))
    ]
    for k, phase in enumerate(exchanges):
        after = (near_out[0],) if k == 0 else (near_out[1],)
        low, packed = add(low, *[swap(packed, s, devices) for s in phase], after=after)
    other = swap(packed, 1, devices)

    size = kept // 2 * pieces
    rows_of = (x_wide, gate, alive)
    weights = (
        step_weight,
        step_bias.reshape(1, channels),
        log_rates,
        skip_gain.reshape(1, channels),
        ssm_state,
    )
    half_shape = (kept // 2, channels)
    own_gated, own_step = call(
        own_kernel,
        (shape(half_shape), shape(half_shape)),
        (low, *rows_of, *weights),
        scratch=[pltpu.VMEM(half_shape, F32)],
        limit=16,
    )
    keep, send, other_step = call(
        readout_kernel,
        (shape((size, LANES)), shape((size, LANES), BF16), shape(half_shape)),
        (other, *rows_of, *weights, own_gated, ends, *near_out),
        scratch=[
            pltpu.VMEM(half_shape, F32),
            pltpu.VMEM((kept, channels), F32),
            pltpu.VMEM((kept * (pieces + 1), LANES), F32),
        ],
        limit=24,
    )
    new_state, token = call(
        state_kernel,
        (shape(ssm_state.shape, BF16), shape((8, LANES))),
        (live_counts, low, other, x_wide, own_step, other_step, log_rates, ssm_state),
        scalars=1,
        scratch=[
            pltpu.VMEM((kept, low_width), F32),
            pltpu.VMEM((kept, channels), F32),
        ],
        limit=16,
    )

    total = (keep, swap(send, 1, devices))
    for k, phase in enumerate(scatter):
        size //= len(phase) + 1
        parts = call(
            functools.partial(sum_kernel, len(total), 1 if k == 1 else 0),
            (shape((size, LANES)),) + (shape((size, LANES), BF16),) * len(phase),
            total,
            after=(token,) if k == 1 else (),
        )
        total = (parts[0],) + tuple(swap(p, s, devices) for p, s in zip(parts[1:], phase))
    mixed = call(
        last_sum_kernel,
        shape(hidden.shape, BF16),
        (hidden,) + total,
        scratch=[pltpu.VMEM((slab + LIVE_MAX, LANES), F32)],
    )
    return (mixed, new_state, new_conv.transpose(1, 0, 2))


def solution(mesh):
    in_specs = (
        P(("groups", "weight"), None),
        P(),
        P(None, None, "weight"),
        P(None, "weight"),
        P("weight"),
        P("weight", None),
        P(None, "weight"),
        P("weight"),
        P(None, "weight"),
        P("weight"),
        P("weight", None),
        P("groups", None, "weight"),
        P("groups", None, "weight"),
        P("groups"),
    )
    out_specs = (
        P(("groups", "weight"), None),
        P("groups", None, "weight"),
        P("groups", None, "weight"),
    )
    return jax.shard_map(body, mesh=mesh, in_specs=in_specs, out_specs=out_specs, check_vma=False)
```

```python
import functools

import jax
import jax.numpy as jnp
from jax import lax
from jax.experimental import pallas as pl
from jax.experimental.pallas import tpu as pltpu
from jax.sharding import PartitionSpec as P

NSTATE = 16
DTR = 512
LIVE_MAX = 3
TAPS = 4
LANES = 128
MIB = 1024 * 1024
CORE_SHARE = 0.9375
FIRST_SHARE = 0.4
FIRST_COLUMNS = 5
BF16 = jnp.bfloat16
F32 = jnp.float32


def chip_steps(devices):
    steps, high = [], devices
    while high > 2:
        if high >= 8:
            steps.append((high // 4, high // 2))
            high //= 4
        else:
            steps.append((high // 2,))
            high //= 2
    steps = [tuple(step) for step in steps]
    if len(steps[-1]) == 1:
        bits = [bit for step in steps for bit in step]
        bits.sort()
        top = bits.pop()
        steps = [(top,)] + [tuple(bits[k : k + 2]) for k in range(len(bits) - 2, -1, -2)]
    return steps


def gather_phases(devices):
    whole = [step if len(step) == 1 else (sum(step), step[1], step[0]) for step in chip_steps(devices)]
    return whole + [(1,)]


def scatter_phases(devices):
    whole = [step if len(step) == 1 else (step[1], step[0], sum(step)) for step in chip_steps(devices)]
    return whole[::-1]


def sum_phases(devices):
    return [
        (step[0] + 1,) if len(step) == 1 else (step[0] + 1, step[1] + 1, sum(step))
        for step in chip_steps(devices)
    ]


def order_of(phases):
    order = [0]
    for phase in phases:
        order = order + [o ^ s for s in phase for o in order]
    return order


def spots_of(order):
    return jnp.array(
        [[o for o in order for _ in range(LIVE_MAX)], list(range(LIVE_MAX)) * len(order)],
        jnp.int32,
    )


def side(index):
    for shift in (4, 2, 1):
        index = jnp.bitwise_xor(index, lax.shift_right_logical(index, shift))
    return jnp.bitwise_and(index, 1)


def swap(value, shift, devices):
    return lax.ppermute(value, "weight", [(i, i ^ shift) for i in range(devices)])


def silu(v):
    return v / (1.0 + jnp.exp(-v))


def softplus(v):
    return jnp.maximum(v, 0.0) + jnp.log1p(jnp.exp(-jnp.abs(v)))


def vmem(count):
    return [pl.BlockSpec(memory_space=pltpu.VMEM)] * count


def shape(dims, kind=F32):
    return jax.ShapeDtypeStruct(dims, kind)


def call(kernel, outs, operands, scalars=0, far=0, scratch=(), limit=8, after=(), aliases=None):
    many = isinstance(outs, tuple)
    return pl.pallas_call(
        kernel,
        out_shape=outs,
        in_specs=[pl.BlockSpec(memory_space=pltpu.SMEM)] * scalars
        + vmem(len(operands) - scalars - far)
        + [pl.BlockSpec(memory_space=pl.ANY)] * (far + len(after)),
        out_specs=tuple(vmem(len(outs))) if many else vmem(1)[0],
        scratch_shapes=list(scratch),
        input_output_aliases=aliases or {},
        compiler_params=pltpu.CompilerParams(vmem_limit_bytes=limit * MIB),
    )(*operands, *after)


def share_copies(far_ref, near_ref, sems, share):
    rows = far_ref.shape[0]
    start, end = (int(rows * part) // 8 * 8 for part in share)
    count = sems.shape[0]
    size = (end - start) // count
    spans = [pl.ds(start + size * k, size) for k in range(count)]
    return [
        pltpu.make_async_copy(far_ref.at[span], near_ref.at[span], sems.at[k])
        for k, span in enumerate(spans)
    ]


def start_all(copies):
    for copy in copies:
        copy.start()


def wait_all(copies):
    for copy in copies:
        copy.wait()


def fold(wide, fold_ref, folded_ref):
    rows, pieces = wide.shape[0], wide.shape[1] // LANES
    for c in range(pieces):
        fold_ref[pl.ds(c, rows, stride=pieces + 1), :] = wide[:, c * LANES : (c + 1) * LANES]
    for r in range(rows):
        start = r * (pieces + 1)
        folded_ref[r * pieces : (r + 1) * pieces] = fold_ref[start : start + pieces].astype(
            folded_ref.dtype
        )


def spread(folded, fold_ref, rows):
    pieces = folded.shape[0] // rows
    for r in range(rows):
        start = r * (pieces + 1)
        fold_ref[start : start + pieces] = folded[r * pieces : (r + 1) * pieces].astype(F32)
    return pieces


def fold_scratch(rows, pieces):
    return pltpu.VMEM((-(-rows // 8) * 8 * (pieces + 1) + pieces + 1, LANES), F32)


def norm_kernel(far_hidden_ref, far_gain_ref, out_ref, fold_ref, hidden_ref, gain_ref, sems):
    copies = [
        pltpu.make_async_copy(far_hidden_ref, hidden_ref, sems.at[0]),
        pltpu.make_async_copy(far_gain_ref, gain_ref, sems.at[1]),
    ]
    start_all(copies)
    wait_all(copies)
    wide = hidden_ref[...].astype(F32)[:LIVE_MAX]
    factor = lax.rsqrt(jnp.mean(wide * wide, axis=-1, keepdims=True) + 1e-05)
    fold(wide * factor * gain_ref[...], fold_ref, out_ref)


def join_kernel(count, *refs):
    start = 0
    for ref in refs[:count]:
        refs[-1][start : start + ref.shape[0]] = ref[...]
        start += ref.shape[0]


def join(parts, after=()):
    rows = sum(part.shape[0] for part in parts)
    return call(
        functools.partial(join_kernel, len(parts)),
        shape((rows, parts[0].shape[1]), parts[0].dtype),
        parts,
        after=after,
    )


def half_kernel(mine_ref, out_ref, fold_ref):
    rows = out_ref.shape[0]
    pieces = spread(mine_ref, fold_ref, rows)
    for c in range(pieces):
        out_ref[:, c * LANES : (c + 1) * LANES] = fold_ref[pl.ds(c, rows, stride=pieces + 1), :]


def unfold_kernel(half_ref, other_ref, _, out_ref, fold_ref):
    rows = half_ref.shape[0]
    pieces = spread(other_ref, fold_ref, rows)
    for c in range(pieces):
        span = slice(c * LANES, (c + 1) * LANES)
        other = fold_ref[pl.ds(c, rows, stride=pieces + 1), :]
        out_ref[:, span] = jnp.concatenate([half_ref[:, span], other], axis=0).astype(BF16)


def columns_kernel(start, far_ref, near_ref, sems):
    columns = pl.ds(start, near_ref.shape[1])
    loads = share_copies(far_ref.at[:, columns], near_ref, sems, (0, 1))
    start_all(loads)
    wait_all(loads)


def load_kernel(share, far_ref, *refs):
    near_ref, sems = refs[-2:]
    loads = share_copies(far_ref, near_ref, sems, share)
    start_all(loads)
    wait_all(loads)


def pack(low):
    coefs = low[:, DTR:]
    high = coefs.astype(BF16)
    rest = (coefs - high.astype(F32)).astype(BF16)
    return jnp.concatenate([low[:, :DTR].astype(BF16), high, rest], axis=1)


def unpack(packed):
    wide = packed.astype(F32)
    count = (wide.shape[1] - DTR) // 2
    coefs = wide[:, DTR : DTR + count] + wide[:, DTR + count :]
    return jnp.concatenate([wide[:, :DTR], coefs], axis=1)


def add_kernel(count, *refs):
    total = refs[0][...]
    for ref in refs[1:count]:
        total = total + (ref[...] if ref.dtype == F32 else unpack(ref[...]))
    refs[-2][...] = total
    refs[-1][...] = pack(total)


def places(block, turn, height, span):
    line = lax.broadcasted_iota(jnp.int32, (height, block.shape[1]), 0)
    return jnp.where(line == block * span + turn, 1.0, 0.0)


def fresh_input(both_ref, block, turn, rows, rows_dev):
    return jnp.dot(
        places(block, turn, rows, rows_dev).astype(BF16),
        both_ref[0].astype(BF16),
        preferred_element_type=F32,
    )


def conv_kernel(
    rows_dev,
    both_ref,
    spot_ref,
    conv_ref,
    taps_ref,
    offset_ref,
    coef_ref,
    keep_ref,
    send_ref,
    mixed_ref,
    low_ref,
):
    index = lax.axis_index("weight")
    rows = conv_ref.shape[1]
    kept = mixed_ref.shape[0]
    block = jnp.bitwise_xor(spot_ref[0:1, :], index)
    fresh = fresh_input(both_ref, block, spot_ref[1:2, :], rows, rows_dev)
    states = [conv_ref[k].astype(F32) for k in range(TAPS - 1)] + [fresh]
    total = states[0] * taps_ref[0:1, :]
    for k in range(1, TAPS):
        total = total + states[k] * taps_ref[k : k + 1, :]
    mixed = silu(total + offset_ref[...]).astype(BF16)
    line = lax.broadcasted_iota(jnp.int32, (kept, rows), 0)
    column = lax.broadcasted_iota(jnp.int32, (kept, rows), 1)
    chosen = (line // LIVE_MAX) * rows_dev + line % LIVE_MAX == column
    mixed = jnp.dot(
        jnp.where(chosen, 1.0, 0.0).astype(BF16), mixed, preferred_element_type=F32
    ).astype(BF16)
    mixed_ref[...] = mixed
    low_ref[...] = lax.dot_general(
        mixed, coef_ref[...], (((1,), (1,)), ((), ())), preferred_element_type=F32
    )
    half = keep_ref.shape[0]
    core = side(index)
    keep_ref[...] = low_ref[pl.ds(pl.multiple_of(core * half, 8), half), :]
    send_ref[...] = low_ref[pl.ds(pl.multiple_of((1 - core) * half, 8), half), :]


def gate_kernel(live_ref, both_ref, spot_ref, mixed_ref, gate_ref, alive_ref, x_ref):
    x_ref[...] = mixed_ref[...].astype(F32)
    for b in range(live_ref.shape[0]):
        for t in range(LIVE_MAX):
            r = b * LIVE_MAX + t
            alive_ref[r : r + 1, :] = jnp.full(
                (1, LANES), jnp.where(t < live_ref[b], 1.0, 0.0)
            )
    block = jnp.bitwise_xor(spot_ref[0:1, :], lax.axis_index("weight"))
    gate_ref[...] = jnp.dot(
        places(block, spot_ref[1:2, :], gate_ref.shape[0], LIVE_MAX),
        silu(both_ref[1]),
        precision=lax.Precision.HIGHEST,
        preferred_element_type=F32,
    )


def taps_kernel(live_ref, both_ref, spot_ref, conv_ref, new_conv_ref, alive_ref):
    blocks = live_ref.shape[0]
    rows = conv_ref.shape[1]
    rows_dev = rows // blocks
    block = jnp.bitwise_xor(spot_ref[0:1, :], lax.axis_index("weight"))
    row_iota = lax.broadcasted_iota(jnp.int32, (rows_dev, LANES), 0)
    for b in range(blocks):
        alive_ref[b * rows_dev : (b + 1) * rows_dev, :] = jnp.where(
            row_iota < live_ref[b], 1.0, 0.0
        )
    alive = alive_ref[:, 0:1] > 0.0
    fresh = fresh_input(both_ref, block, spot_ref[1:2, :], rows, rows_dev)
    states = [conv_ref[k].astype(F32) for k in range(TAPS - 1)] + [fresh]
    for k in range(TAPS - 1):
        new_conv_ref[k] = jnp.where(alive, states[k + 1], states[k]).astype(BF16)


def half_rows(which, size):
    return pl.ds(pl.multiple_of(which * size, 8), size)


def join_halves(mine, other, out_ref):
    size = mine.shape[0]
    mine_side = side(lax.axis_index("weight"))
    out_ref[half_rows(mine_side, size), :] = mine
    out_ref[half_rows(1 - mine_side, size), :] = other


def gated_rows(which, low, weights, rows_refs, state_ref, read_ref):
    step_weight_ref, bias_ref, rates_ref, skip_ref = weights
    size = low.shape[0]
    x_wide, gate, alive = (ref[half_rows(which, size), :] for ref in rows_refs)
    blocks = size // LIVE_MAX
    rows_dev = state_ref.shape[0] // (2 * blocks)
    step_size = softplus(
        jnp.dot(low[:, :DTR].astype(BF16), step_weight_ref[...], preferred_element_type=F32)
        + bias_ref[...]
    )
    coefs = low[:, DTR:]
    both_coefs = jnp.sum(coefs[:, :NSTATE] * coefs[:, NSTATE:], axis=1, keepdims=True)
    out_coefs = coefs[:, NSTATE:].T
    rates = -jnp.exp(rates_ref[...])
    first = which * (blocks * rows_dev)
    for b in range(blocks):
        for t in range(LIVE_MAX):
            r = b * LIVE_MAX + t
            wide = state_ref[first + (b * rows_dev + t)].astype(F32)
            decayed = jnp.exp(step_size[r : r + 1, :] * rates) * wide
            read_ref[r : r + 1, :] = jnp.sum(
                out_coefs[:, r : r + 1] * decayed, axis=0, keepdims=True
            )
    readout = read_ref[...] + (both_coefs * step_size + skip_ref[...]) * x_wide
    return step_size, jnp.where(alive[:, 0:1] > 0.0, readout * gate, 0.0)


def own_kernel(
    low_ref,
    x_ref,
    gate_ref,
    alive_ref,
    step_weight_ref,
    bias_ref,
    rates_ref,
    skip_ref,
    state_ref,
    gated_ref,
    step_ref,
    read_ref,
):
    step_ref[...], gated_ref[...] = gated_rows(
        side(lax.axis_index("weight")),
        low_ref[...],
        (step_weight_ref, bias_ref, rates_ref, skip_ref),
        (x_ref, gate_ref, alive_ref),
        state_ref,
        read_ref,
    )


def readout_kernel(
    other_ref,
    x_ref,
    gate_ref,
    alive_ref,
    step_weight_ref,
    bias_ref,
    rates_ref,
    skip_ref,
    state_ref,
    own_ref,
    spot_ref,
    first_ref,
    last_ref,
    keep_ref,
    send_ref,
    step_ref,
    read_ref,
    gated_ref,
    fold_ref,
):
    kept = x_ref.shape[0]
    step_ref[...], gated = gated_rows(
        1 - side(lax.axis_index("weight")),
        unpack(other_ref[...]),
        (step_weight_ref, bias_ref, rates_ref, skip_ref),
        (x_ref, gate_ref, alive_ref),
        state_ref,
        read_ref,
    )
    join_halves(own_ref[...], gated, gated_ref)
    block = jnp.bitwise_xor(spot_ref[:, 0:1], lax.axis_index("weight"))
    column = lax.broadcasted_iota(jnp.int32, (kept, kept), 1)
    pick = jnp.where(column == block * LIVE_MAX + spot_ref[:, 1:2], 1.0, 0.0).astype(BF16)
    picked = jnp.dot(
        pick, gated_ref[...].astype(BF16), preferred_element_type=F32
    ).astype(BF16)
    half = kept // 2
    near = first_ref.shape[1]
    pieces = (near + last_ref.shape[1]) // LANES
    group = 4
    for c in range(0, pieces, group):
        start = c * LANES
        if start < near:
            weight = first_ref[:, start : start + group * LANES]
        else:
            weight = last_ref[:, start - near : start - near + group * LANES]
        part = jnp.dot(picked, weight, preferred_element_type=F32)
        for g in range(group):
            piece = part[:, g * LANES : (g + 1) * LANES]
            fold_ref[pl.ds(c + g, kept, stride=pieces + 1), :] = piece
    for r in range(half):
        rows = slice(r * pieces, (r + 1) * pieces)
        start = r * (pieces + 1)
        keep_ref[rows] = fold_ref[start : start + pieces]
        start = (half + r) * (pieces + 1)
        send_ref[rows] = fold_ref[start : start + pieces].astype(BF16)


def state_kernel(
    live_ref,
    mine_ref,
    other_ref,
    x_ref,
    own_step_ref,
    other_step_ref,
    rates_ref,
    state_ref,
    new_state_ref,
    token_ref,
    low_ref,
    step_ref,
):
    token_ref[...] = jnp.zeros_like(token_ref)
    blocks = live_ref.shape[0]
    rows_dev = state_ref.shape[0] // blocks
    join_halves(mine_ref[...], unpack(other_ref[...]), low_ref)
    join_halves(own_step_ref[...], other_step_ref[...], step_ref)
    in_coefs = low_ref[:, DTR : DTR + NSTATE].T
    step_size = step_ref[...]
    driven = step_size * x_ref[...]
    rates = -jnp.exp(rates_ref[...])
    for b in range(blocks):
        for t in range(LIVE_MAX):
            r = b * LIVE_MAX + t
            wide = state_ref[b * rows_dev + t].astype(F32)
            updated = (
                jnp.exp(step_size[r : r + 1, :] * rates) * wide
                + in_coefs[:, r : r + 1] * driven[r : r + 1, :]
            )
            new_state_ref[b * rows_dev + t] = jnp.where(
                t < live_ref[b], updated, wide
            ).astype(BF16)
        for t in range(LIVE_MAX, rows_dev):
            new_state_ref[b * rows_dev + t] = state_ref[b * rows_dev + t]


def sum_kernel(count, skipped, *refs):
    parts, outs = refs[:count], refs[count + skipped :]
    size = outs[0].shape[0]
    for k, out in enumerate(outs):
        rows = slice(k * size, (k + 1) * size)
        total = parts[0][rows]
        for part in parts[1:]:
            total = total + part[rows].astype(F32)
        out[...] = total.astype(out.dtype)


def last_sum_kernel(*refs):
    hidden_ref, parts, out_ref, fold_ref = refs[0], refs[1:-2], refs[-2], refs[-1]
    total = parts[0][...]
    for part in parts[1:]:
        total = total + part[...].astype(F32)
    rows = LIVE_MAX
    pieces = spread(total, fold_ref, rows)
    for c in range(pieces):
        span = slice(c * LANES, (c + 1) * LANES)
        wide = hidden_ref[:, span].astype(F32)
        own = wide[:rows] + fold_ref[pl.ds(c, rows, stride=pieces + 1), :]
        out_ref[:, span] = jnp.concatenate([own, wide[rows:]], axis=0).astype(BF16)


def body(
    hidden,
    norm_gain,
    in_weight,
    conv_weight,
    conv_offset,
    coef_weight,
    step_weight,
    step_bias,
    log_rates,
    skip_gain,
    out_weight,
    ssm_state,
    conv_state,
    live_counts,
):
    devices = lax.axis_size("weight")
    rows_dev, width = hidden.shape
    rows = devices * rows_dev
    kept = devices * LIVE_MAX
    channels = in_weight.shape[2]
    low_width = coef_weight.shape[1]
    phases = gather_phases(devices)
    spots = spots_of(order_of(phases))
    scatter = scatter_phases(devices)
    ends = spots_of(order_of(scatter[::-1] + [(1,)])).T
    pieces = width // LANES
    slab = LIVE_MAX * pieces

    weight_shape = pltpu.VMEM(in_weight.shape, BF16)

    def load(share, so_far=None):
        return call(
            functools.partial(load_kernel, share),
            weight_shape,
            (in_weight,),
            far=1,
            scratch=[pltpu.SemaphoreType.DMA((4,))],
            limit=43,
            after=() if so_far is None else (so_far,),
            aliases={} if so_far is None else {1: 0},
        )

    gathered = call(
        norm_kernel,
        pltpu.VMEM((slab, LANES), BF16),
        (hidden, norm_gain.reshape(1, width)),
        far=2,
        scratch=[
            fold_scratch(LIVE_MAX, pieces),
            pltpu.VMEM(hidden.shape, BF16),
            pltpu.VMEM((1, width), F32),
            pltpu.SemaphoreType.DMA((2,)),
        ],
        limit=60,
    )
    done, near_weight = 0.0, None
    for k, phase in enumerate(phases[:-1]):
        until = CORE_SHARE if k == len(phases) - 2 else done + (CORE_SHARE - done) * FIRST_SHARE
        near_weight = load((done, until), near_weight)
        done = until
        gathered = join(
            [gathered] + [swap(gathered, s, devices) for s in phase], (near_weight,)
        )
    near_weight = load((done, 1.0), near_weight)
    folded = [fold_scratch(kept // 2, pieces)]
    half = call(half_kernel, shape((kept // 2, width)), (gathered,), scratch=folded, limit=12)
    normed = call(
        unfold_kernel,
        shape((kept, width), BF16),
        (half, swap(gathered, 1, devices)),
        scratch=folded,
        limit=12,
        after=(near_weight,),
    )
    both = jnp.einsum("rd,dbc->brc", normed, near_weight, preferred_element_type=F32)

    conv_turned = conv_state.transpose(1, 0, 2)
    keep, send, mixed_x = call(
        functools.partial(conv_kernel, rows_dev),
        (
            shape((kept // 2, low_width)),
            shape((kept // 2, low_width)),
            shape((kept, channels), BF16),
        ),
        (
            both,
            spots,
            conv_turned,
            conv_weight,
            conv_offset.reshape(1, channels),
            coef_weight.T,
        ),
        scratch=[pltpu.VMEM((kept, low_width), F32)],
        limit=16,
    )
    gate, alive, x_wide = call(
        gate_kernel,
        (shape((kept, channels)), shape((kept, LANES)), shape((kept, channels))),
        (live_counts, both, spots, mixed_x),
        scalars=1,
    )
    new_conv = call(
        taps_kernel,
        shape((TAPS - 1, rows, channels), BF16),
        (live_counts, both, spots, conv_turned),
        scalars=1,
        scratch=[pltpu.VMEM((rows, LANES), F32)],
    )

    packed_width = low_width + 2 * NSTATE

    def add(*parts, after=()):
        return call(
            functools.partial(add_kernel, len(parts)),
            (shape(parts[0].shape), shape((kept // 2, packed_width), BF16)),
            parts,
            after=after,
        )

    low, packed = add(keep, swap(send, 1, devices), after=(gate,))
    exchanges = sum_phases(devices)
    first_columns = width * FIRST_COLUMNS // 16 if len(exchanges) > 1 else width // 2
    near_out = [
        call(
            functools.partial(columns_kernel, start),
            pltpu.VMEM((channels, count), BF16),
            (out_weight,),
            far=1,
            scratch=[pltpu.SemaphoreType.DMA((4,))],
            limit=50,
        )
        for start, count in ((0, first_columns), (first_columns, width - first_columns))
    ]
    for k, phase in enumerate(exchanges):
        after = (near_out[0],) if k == 0 else (near_out[1],)
        low, packed = add(low, *[swap(packed, s, devices) for s in phase], after=after)
    other = swap(packed, 1, devices)

    size = kept // 2 * pieces
    rows_of = (x_wide, gate, alive)
    weights = (
        step_weight,
        step_bias.reshape(1, channels),
        log_rates,
        skip_gain.reshape(1, channels),
        ssm_state,
    )
    half_shape = (kept // 2, channels)
    own_gated, own_step = call(
        own_kernel,
        (shape(half_shape), shape(half_shape)),
        (low, *rows_of, *weights),
        scratch=[pltpu.VMEM(half_shape, F32)],
        limit=16,
    )
    keep, send, other_step = call(
        readout_kernel,
        (shape((size, LANES)), shape((size, LANES), BF16), shape(half_shape)),
        (other, *rows_of, *weights, own_gated, ends, *near_out),
        scratch=[
            pltpu.VMEM(half_shape, F32),
            pltpu.VMEM((kept, channels), F32),
            fold_scratch(kept, pieces),
        ],
        limit=24,
    )
    new_state, token = call(
        state_kernel,
        (shape(ssm_state.shape, BF16), shape((8, LANES))),
        (live_counts, low, other, x_wide, own_step, other_step, log_rates, ssm_state),
        scalars=1,
        scratch=[
            pltpu.VMEM((kept, low_width), F32),
            pltpu.VMEM((kept, channels), F32),
        ],
        limit=16,
    )

    total = (keep, swap(send, 1, devices))
    for k, phase in enumerate(scatter):
        size //= len(phase) + 1
        parts = call(
            functools.partial(sum_kernel, len(total), 1 if k == 1 else 0),
            (shape((size, LANES)),) + (shape((size, LANES), BF16),) * len(phase),
            total,
            after=(token,) if k == 1 else (),
        )
        total = (parts[0],) + tuple(swap(p, s, devices) for p, s in zip(parts[1:], phase))
    mixed = call(
        last_sum_kernel,
        shape(hidden.shape, BF16),
        (hidden,) + total,
        scratch=[fold_scratch(LIVE_MAX, pieces)],
    )
    return (mixed, new_state, new_conv.transpose(1, 0, 2))


def solution(mesh):
    in_specs = (
        P(("groups", "weight"), None),
        P(),
        P(None, None, "weight"),
        P(None, "weight"),
        P("weight"),
        P("weight", None),
        P(None, "weight"),
        P("weight"),
        P(None, "weight"),
        P("weight"),
        P("weight", None),
        P("groups", None, "weight"),
        P("groups", None, "weight"),
        P("groups"),
    )
    out_specs = (
        P(("groups", "weight"), None),
        P("groups", None, "weight"),
        P("groups", None, "weight"),
    )
    return jax.shard_map(body, mesh=mesh, in_specs=in_specs, out_specs=out_specs, check_vma=False)
```

```python
import functools

import jax
import jax.numpy as jnp
from jax import lax
from jax.experimental import pallas as pl
from jax.experimental.pallas import tpu as pltpu
from jax.sharding import PartitionSpec as P

NSTATE = 16
DTR = 512
LIVE_MAX = 3
TAPS = 4
LANES = 128
MIB = 1024 * 1024
CORE_SHARE = 0.9375
FIRST_SHARE = 0.4
FIRST_COLUMNS = 5
BF16 = jnp.bfloat16
F32 = jnp.float32


def chip_steps(devices):
    steps, high = [], devices
    while high > 2:
        if high >= 8:
            steps.append((high // 4, high // 2))
            high //= 4
        else:
            steps.append((high // 2,))
            high //= 2
    steps = [tuple(step) for step in steps]
    if len(steps[-1]) == 1:
        bits = [bit for step in steps for bit in step]
        bits.sort()
        top = bits.pop()
        steps = [(top,)] + [tuple(bits[k : k + 2]) for k in range(len(bits) - 2, -1, -2)]
    return steps


def gather_phases(devices):
    whole = [step if len(step) == 1 else (sum(step), step[1], step[0]) for step in chip_steps(devices)]
    return whole + [(1,)]


def scatter_phases(devices):
    whole = [step if len(step) == 1 else (step[1], step[0], sum(step)) for step in chip_steps(devices)]
    return whole[::-1]


def sum_phases(devices):
    return [
        (step[0] + 1,) if len(step) == 1 else (step[0] + 1, step[1] + 1, sum(step))
        for step in chip_steps(devices)
    ]


def order_of(phases):
    order = [0]
    for phase in phases:
        order = order + [o ^ s for s in phase for o in order]
    return order


def spots_of(order):
    return jnp.array(
        [[o for o in order for _ in range(LIVE_MAX)], list(range(LIVE_MAX)) * len(order)],
        jnp.int32,
    )


def side(index):
    for shift in (4, 2, 1):
        index = jnp.bitwise_xor(index, lax.shift_right_logical(index, shift))
    return jnp.bitwise_and(index, 1)


def swap(value, shift, devices):
    return lax.ppermute(value, "weight", [(i, i ^ shift) for i in range(devices)])


def silu(v):
    return v / (1.0 + jnp.exp(-v))


def softplus(v):
    return jnp.maximum(v, 0.0) + jnp.log1p(jnp.exp(-jnp.abs(v)))


def vmem(count):
    return [pl.BlockSpec(memory_space=pltpu.VMEM)] * count


def shape(dims, kind=F32):
    return jax.ShapeDtypeStruct(dims, kind)


def call(kernel, outs, operands, scalars=0, far=0, scratch=(), limit=8, after=(), aliases=None, whole=False):
    many = isinstance(outs, tuple)
    return pl.pallas_call(
        kernel,
        out_shape=outs,
        in_specs=[pl.BlockSpec(memory_space=pltpu.SMEM)] * scalars
        + vmem(len(operands) - scalars - far)
        + [pl.BlockSpec(memory_space=pl.ANY)] * (far + len(after)),
        out_specs=pl.BlockSpec(memory_space=pl.ANY)
        if whole
        else tuple(vmem(len(outs)))
        if many
        else vmem(1)[0],
        scratch_shapes=list(scratch),
        input_output_aliases=aliases or {},
        compiler_params=pltpu.CompilerParams(vmem_limit_bytes=limit * MIB),
    )(*operands, *after)


def share_copies(far_ref, near_ref, sems, share):
    rows = far_ref.shape[0]
    start, end = (int(rows * part) // 8 * 8 for part in share)
    count = sems.shape[0]
    size = (end - start) // count
    spans = [pl.ds(start + size * k, size) for k in range(count)]
    return [
        pltpu.make_async_copy(far_ref.at[span], near_ref.at[span], sems.at[k])
        for k, span in enumerate(spans)
    ]


def start_all(copies):
    for copy in copies:
        copy.start()


def wait_all(copies):
    for copy in copies:
        copy.wait()


def fold(wide, fold_ref, folded_ref):
    rows, pieces = wide.shape[0], wide.shape[1] // LANES
    for c in range(pieces):
        fold_ref[pl.ds(c, rows, stride=pieces + 1), :] = wide[:, c * LANES : (c + 1) * LANES]
    for r in range(rows):
        start = r * (pieces + 1)
        folded_ref[r * pieces : (r + 1) * pieces] = fold_ref[start : start + pieces].astype(
            folded_ref.dtype
        )


def spread(folded, fold_ref, rows):
    pieces = folded.shape[0] // rows
    for r in range(rows):
        start = r * (pieces + 1)
        fold_ref[start : start + pieces] = folded[r * pieces : (r + 1) * pieces].astype(F32)
    return pieces


def fold_scratch(rows, pieces):
    return pltpu.VMEM((-(-rows // 8) * 8 * (pieces + 1) + pieces + 1, LANES), F32)


def norm_kernel(far_hidden_ref, far_gain_ref, out_ref, fold_ref, hidden_ref, gain_ref, sems):
    copies = [
        pltpu.make_async_copy(far_hidden_ref, hidden_ref, sems.at[0]),
        pltpu.make_async_copy(far_gain_ref, gain_ref, sems.at[1]),
    ]
    start_all(copies)
    wait_all(copies)
    wide = hidden_ref[...].astype(F32)[:LIVE_MAX]
    factor = lax.rsqrt(jnp.mean(wide * wide, axis=-1, keepdims=True) + 1e-05)
    fold(wide * factor * gain_ref[...], fold_ref, out_ref)


def join_kernel(count, *refs):
    start = 0
    for ref in refs[:count]:
        refs[-1][start : start + ref.shape[0]] = ref[...]
        start += ref.shape[0]


def join(parts, after=()):
    rows = sum(part.shape[0] for part in parts)
    return call(
        functools.partial(join_kernel, len(parts)),
        shape((rows, parts[0].shape[1]), parts[0].dtype),
        parts,
        after=after,
    )


def half_kernel(mine_ref, out_ref, fold_ref):
    rows = out_ref.shape[0]
    pieces = spread(mine_ref, fold_ref, rows)
    for c in range(pieces):
        out_ref[:, c * LANES : (c + 1) * LANES] = fold_ref[pl.ds(c, rows, stride=pieces + 1), :]


def unfold_kernel(half_ref, other_ref, _, out_ref, fold_ref):
    rows = half_ref.shape[0]
    pieces = spread(other_ref, fold_ref, rows)
    for c in range(pieces):
        span = slice(c * LANES, (c + 1) * LANES)
        other = fold_ref[pl.ds(c, rows, stride=pieces + 1), :]
        out_ref[:, span] = jnp.concatenate([half_ref[:, span], other], axis=0).astype(BF16)


def columns_kernel(start, far_ref, near_ref, sems):
    columns = pl.ds(start, near_ref.shape[1])
    loads = share_copies(far_ref.at[:, columns], near_ref, sems, (0, 1))
    start_all(loads)
    wait_all(loads)


def load_kernel(share, far_ref, *refs):
    near_ref, sems = refs[-2:]
    loads = share_copies(far_ref, near_ref, sems, share)
    start_all(loads)
    wait_all(loads)


def pack(low):
    coefs = low[:, DTR:]
    high = coefs.astype(BF16)
    rest = (coefs - high.astype(F32)).astype(BF16)
    return jnp.concatenate([low[:, :DTR].astype(BF16), high, rest], axis=1)


def unpack(packed):
    wide = packed.astype(F32)
    count = (wide.shape[1] - DTR) // 2
    coefs = wide[:, DTR : DTR + count] + wide[:, DTR + count :]
    return jnp.concatenate([wide[:, :DTR], coefs], axis=1)


def add_kernel(count, *refs):
    total = refs[0][...]
    for ref in refs[1:count]:
        total = total + (ref[...] if ref.dtype == F32 else unpack(ref[...]))
    refs[-2][...] = total
    refs[-1][...] = pack(total)


def places(block, turn, height, span):
    line = lax.broadcasted_iota(jnp.int32, (height, block.shape[1]), 0)
    return jnp.where(line == block * span + turn, 1.0, 0.0)


def fresh_input(both_ref, block, turn, rows, rows_dev):
    return jnp.dot(
        places(block, turn, rows, rows_dev).astype(BF16),
        both_ref[0].astype(BF16),
        preferred_element_type=F32,
    )


def conv_kernel(
    rows_dev,
    both_ref,
    spot_ref,
    conv_ref,
    taps_ref,
    offset_ref,
    coef_ref,
    keep_ref,
    send_ref,
    mixed_ref,
    low_ref,
):
    index = lax.axis_index("weight")
    rows = conv_ref.shape[1]
    kept = mixed_ref.shape[0]
    block = jnp.bitwise_xor(spot_ref[0:1, :], index)
    fresh = fresh_input(both_ref, block, spot_ref[1:2, :], rows, rows_dev)
    states = [conv_ref[k].astype(F32) for k in range(TAPS - 1)] + [fresh]
    total = states[0] * taps_ref[0:1, :]
    for k in range(1, TAPS):
        total = total + states[k] * taps_ref[k : k + 1, :]
    mixed = silu(total + offset_ref[...]).astype(BF16)
    line = lax.broadcasted_iota(jnp.int32, (kept, rows), 0)
    column = lax.broadcasted_iota(jnp.int32, (kept, rows), 1)
    chosen = (line // LIVE_MAX) * rows_dev + line % LIVE_MAX == column
    mixed = jnp.dot(
        jnp.where(chosen, 1.0, 0.0).astype(BF16), mixed, preferred_element_type=F32
    ).astype(BF16)
    mixed_ref[...] = mixed
    low_ref[...] = lax.dot_general(
        mixed, coef_ref[...], (((1,), (1,)), ((), ())), preferred_element_type=F32
    )
    half = keep_ref.shape[0]
    core = side(index)
    keep_ref[...] = low_ref[pl.ds(pl.multiple_of(core * half, 8), half), :]
    send_ref[...] = low_ref[pl.ds(pl.multiple_of((1 - core) * half, 8), half), :]


def gate_kernel(live_ref, both_ref, spot_ref, mixed_ref, gate_ref, alive_ref, x_ref):
    x_ref[...] = mixed_ref[...].astype(F32)
    for b in range(live_ref.shape[0]):
        for t in range(LIVE_MAX):
            r = b * LIVE_MAX + t
            alive_ref[r : r + 1, :] = jnp.full(
                (1, LANES), jnp.where(t < live_ref[b], 1.0, 0.0)
            )
    block = jnp.bitwise_xor(spot_ref[0:1, :], lax.axis_index("weight"))
    gate_ref[...] = jnp.dot(
        places(block, spot_ref[1:2, :], gate_ref.shape[0], LIVE_MAX),
        silu(both_ref[1]),
        precision=lax.Precision.HIGHEST,
        preferred_element_type=F32,
    )


def taps_kernel(live_ref, both_ref, spot_ref, conv_ref, new_conv_ref, alive_ref):
    blocks = live_ref.shape[0]
    rows = conv_ref.shape[1]
    rows_dev = rows // blocks
    block = jnp.bitwise_xor(spot_ref[0:1, :], lax.axis_index("weight"))
    row_iota = lax.broadcasted_iota(jnp.int32, (rows_dev, LANES), 0)
    for b in range(blocks):
        alive_ref[b * rows_dev : (b + 1) * rows_dev, :] = jnp.where(
            row_iota < live_ref[b], 1.0, 0.0
        )
    alive = alive_ref[:, 0:1] > 0.0
    fresh = fresh_input(both_ref, block, spot_ref[1:2, :], rows, rows_dev)
    states = [conv_ref[k].astype(F32) for k in range(TAPS - 1)] + [fresh]
    for k in range(TAPS - 1):
        new_conv_ref[k] = jnp.where(alive, states[k + 1], states[k]).astype(BF16)


def half_rows(which, size):
    return pl.ds(pl.multiple_of(which * size, 8), size)


def join_halves(mine, other, out_ref):
    size = mine.shape[0]
    mine_side = side(lax.axis_index("weight"))
    out_ref[half_rows(mine_side, size), :] = mine
    out_ref[half_rows(1 - mine_side, size), :] = other


def gated_rows(which, low, weights, rows_refs, state_ref, read_ref):
    step_weight_ref, bias_ref, rates_ref, skip_ref = weights
    size = low.shape[0]
    x_wide, gate, alive = (ref[half_rows(which, size), :] for ref in rows_refs)
    blocks = size // LIVE_MAX
    rows_dev = state_ref.shape[0] // (2 * blocks)
    step_size = softplus(
        jnp.dot(low[:, :DTR].astype(BF16), step_weight_ref[...], preferred_element_type=F32)
        + bias_ref[...]
    )
    coefs = low[:, DTR:]
    both_coefs = jnp.sum(coefs[:, :NSTATE] * coefs[:, NSTATE:], axis=1, keepdims=True)
    out_coefs = coefs[:, NSTATE:].T
    rates = -jnp.exp(rates_ref[...])
    first = which * (blocks * rows_dev)
    for b in range(blocks):
        for t in range(LIVE_MAX):
            r = b * LIVE_MAX + t
            wide = state_ref[first + (b * rows_dev + t)].astype(F32)
            decayed = jnp.exp(step_size[r : r + 1, :] * rates) * wide
            read_ref[r : r + 1, :] = jnp.sum(
                out_coefs[:, r : r + 1] * decayed, axis=0, keepdims=True
            )
    readout = read_ref[...] + (both_coefs * step_size + skip_ref[...]) * x_wide
    return step_size, jnp.where(alive[:, 0:1] > 0.0, readout * gate, 0.0)


def own_kernel(
    low_ref,
    x_ref,
    gate_ref,
    alive_ref,
    step_weight_ref,
    bias_ref,
    rates_ref,
    skip_ref,
    state_ref,
    gated_ref,
    step_ref,
    read_ref,
):
    step_ref[...], gated_ref[...] = gated_rows(
        side(lax.axis_index("weight")),
        low_ref[...],
        (step_weight_ref, bias_ref, rates_ref, skip_ref),
        (x_ref, gate_ref, alive_ref),
        state_ref,
        read_ref,
    )


def readout_kernel(
    other_ref,
    x_ref,
    gate_ref,
    alive_ref,
    step_weight_ref,
    bias_ref,
    rates_ref,
    skip_ref,
    state_ref,
    own_ref,
    spot_ref,
    first_ref,
    last_ref,
    keep_ref,
    send_ref,
    step_ref,
    read_ref,
    gated_ref,
    fold_ref,
):
    kept = x_ref.shape[0]
    step_ref[...], gated = gated_rows(
        1 - side(lax.axis_index("weight")),
        unpack(other_ref[...]),
        (step_weight_ref, bias_ref, rates_ref, skip_ref),
        (x_ref, gate_ref, alive_ref),
        state_ref,
        read_ref,
    )
    join_halves(own_ref[...], gated, gated_ref)
    block = jnp.bitwise_xor(spot_ref[:, 0:1], lax.axis_index("weight"))
    column = lax.broadcasted_iota(jnp.int32, (kept, kept), 1)
    pick = jnp.where(column == block * LIVE_MAX + spot_ref[:, 1:2], 1.0, 0.0).astype(BF16)
    picked = jnp.dot(
        pick, gated_ref[...].astype(BF16), preferred_element_type=F32
    ).astype(BF16)
    half = kept // 2
    near = first_ref.shape[1]
    pieces = (near + last_ref.shape[1]) // LANES
    group = 4
    for c in range(0, pieces, group):
        start = c * LANES
        if start < near:
            weight = first_ref[:, start : start + group * LANES]
        else:
            weight = last_ref[:, start - near : start - near + group * LANES]
        part = jnp.dot(picked, weight, preferred_element_type=F32)
        for g in range(group):
            piece = part[:, g * LANES : (g + 1) * LANES]
            fold_ref[pl.ds(c + g, kept, stride=pieces + 1), :] = piece
    for r in range(half):
        rows = slice(r * pieces, (r + 1) * pieces)
        start = r * (pieces + 1)
        keep_ref[rows] = fold_ref[start : start + pieces]
        start = (half + r) * (pieces + 1)
        send_ref[rows] = fold_ref[start : start + pieces].astype(BF16)


def state_kernel(
    live_ref,
    mine_ref,
    other_ref,
    x_ref,
    own_step_ref,
    other_step_ref,
    rates_ref,
    state_ref,
    new_state_ref,
    token_ref,
    low_ref,
    step_ref,
):
    token_ref[...] = jnp.zeros_like(token_ref)
    blocks = live_ref.shape[0]
    rows_dev = state_ref.shape[0] // blocks
    join_halves(mine_ref[...], unpack(other_ref[...]), low_ref)
    join_halves(own_step_ref[...], other_step_ref[...], step_ref)
    in_coefs = low_ref[:, DTR : DTR + NSTATE].T
    step_size = step_ref[...]
    driven = step_size * x_ref[...]
    rates = -jnp.exp(rates_ref[...])
    for b in range(blocks):
        for t in range(LIVE_MAX):
            r = b * LIVE_MAX + t
            wide = state_ref[b * rows_dev + t].astype(F32)
            updated = (
                jnp.exp(step_size[r : r + 1, :] * rates) * wide
                + in_coefs[:, r : r + 1] * driven[r : r + 1, :]
            )
            new_state_ref[b * rows_dev + t] = jnp.where(
                t < live_ref[b], updated, wide
            ).astype(BF16)
        for t in range(LIVE_MAX, rows_dev):
            new_state_ref[b * rows_dev + t] = state_ref[b * rows_dev + t]


def sum_kernel(count, skipped, *refs):
    parts, outs = refs[:count], refs[count + skipped :]
    size = outs[0].shape[0]
    for k, out in enumerate(outs):
        rows = slice(k * size, (k + 1) * size)
        total = parts[0][rows]
        for part in parts[1:]:
            total = total + part[rows].astype(F32)
        out[...] = total.astype(out.dtype)


def last_sum_kernel(*refs):
    hidden_ref, parts, out_ref, fold_ref = refs[0], refs[1:-2], refs[-2], refs[-1]
    total = parts[0][...]
    for part in parts[1:]:
        total = total + part[...].astype(F32)
    rows = LIVE_MAX
    pieces = spread(total, fold_ref, rows)
    for c in range(pieces):
        span = slice(c * LANES, (c + 1) * LANES)
        wide = hidden_ref[:, span].astype(F32)
        own = wide[:rows] + fold_ref[pl.ds(c, rows, stride=pieces + 1), :]
        out_ref[:, span] = jnp.concatenate([own, wide[rows:]], axis=0).astype(BF16)


def body(
    hidden,
    norm_gain,
    in_weight,
    conv_weight,
    conv_offset,
    coef_weight,
    step_weight,
    step_bias,
    log_rates,
    skip_gain,
    out_weight,
    ssm_state,
    conv_state,
    live_counts,
):
    devices = lax.axis_size("weight")
    rows_dev, width = hidden.shape
    rows = devices * rows_dev
    kept = devices * LIVE_MAX
    channels = in_weight.shape[2]
    low_width = coef_weight.shape[1]
    phases = gather_phases(devices)
    spots = spots_of(order_of(phases))
    scatter = scatter_phases(devices)
    ends = spots_of(order_of(scatter[::-1] + [(1,)])).T
    pieces = width // LANES
    slab = LIVE_MAX * pieces

    weight_shape = pltpu.VMEM(in_weight.shape, BF16)

    def load(share, so_far=None):
        return call(
            functools.partial(load_kernel, share),
            weight_shape,
            (in_weight,),
            far=1,
            scratch=[pltpu.SemaphoreType.DMA((4,))],
            limit=43,
            after=() if so_far is None else (so_far,),
            whole=True,
            aliases={} if so_far is None else {1: 0},
        )

    gathered = call(
        norm_kernel,
        pltpu.VMEM((slab, LANES), BF16),
        (hidden, norm_gain.reshape(1, width)),
        far=2,
        scratch=[
            fold_scratch(LIVE_MAX, pieces),
            pltpu.VMEM(hidden.shape, BF16),
            pltpu.VMEM((1, width), F32),
            pltpu.SemaphoreType.DMA((2,)),
        ],
        limit=60,
    )
    done, near_weight = 0.0, None
    for k, phase in enumerate(phases[:-1]):
        until = CORE_SHARE if k == len(phases) - 2 else done + (CORE_SHARE - done) * FIRST_SHARE
        near_weight = load((done, until), near_weight)
        done = until
        gathered = join(
            [gathered] + [swap(gathered, s, devices) for s in phase], (near_weight,)
        )
    near_weight = load((done, 1.0), near_weight)
    folded = [fold_scratch(kept // 2, pieces)]
    half = call(half_kernel, shape((kept // 2, width)), (gathered,), scratch=folded, limit=12)
    normed = call(
        unfold_kernel,
        shape((kept, width), BF16),
        (half, swap(gathered, 1, devices)),
        scratch=folded,
        limit=12,
        after=(near_weight,),
    )
    both = jnp.einsum("rd,dbc->brc", normed, near_weight, preferred_element_type=F32)

    conv_turned = conv_state.transpose(1, 0, 2)
    keep, send, mixed_x = call(
        functools.partial(conv_kernel, rows_dev),
        (
            shape((kept // 2, low_width)),
            shape((kept // 2, low_width)),
            shape((kept, channels), BF16),
        ),
        (
            both,
            spots,
            conv_turned,
            conv_weight,
            conv_offset.reshape(1, channels),
            coef_weight.T,
        ),
        scratch=[pltpu.VMEM((kept, low_width), F32)],
        limit=16,
    )
    gate, alive, x_wide = call(
        gate_kernel,
        (shape((kept, channels)), shape((kept, LANES)), shape((kept, channels))),
        (live_counts, both, spots, mixed_x),
        scalars=1,
    )
    new_conv = call(
        taps_kernel,
        shape((TAPS - 1, rows, channels), BF16),
        (live_counts, both, spots, conv_turned),
        scalars=1,
        scratch=[pltpu.VMEM((rows, LANES), F32)],
    )

    packed_width = low_width + 2 * NSTATE

    def add(*parts, after=()):
        return call(
            functools.partial(add_kernel, len(parts)),
            (shape(parts[0].shape), shape((kept // 2, packed_width), BF16)),
            parts,
            after=after,
        )

    low, packed = add(keep, swap(send, 1, devices), after=(gate,))
    exchanges = sum_phases(devices)
    first_columns = width * FIRST_COLUMNS // 16 if len(exchanges) > 1 else width // 2
    near_out = [
        call(
            functools.partial(columns_kernel, start),
            pltpu.VMEM((channels, count), BF16),
            (out_weight,),
            far=1,
            scratch=[pltpu.SemaphoreType.DMA((4,))],
            limit=50,
            whole=True,
        )
        for start, count in ((0, first_columns), (first_columns, width - first_columns))
    ]
    for k, phase in enumerate(exchanges):
        after = (near_out[0],) if k == 0 else (near_out[1],)
        low, packed = add(low, *[swap(packed, s, devices) for s in phase], after=after)
    other = swap(packed, 1, devices)

    size = kept // 2 * pieces
    rows_of = (x_wide, gate, alive)
    weights = (
        step_weight,
        step_bias.reshape(1, channels),
        log_rates,
        skip_gain.reshape(1, channels),
        ssm_state,
    )
    half_shape = (kept // 2, channels)
    own_gated, own_step = call(
        own_kernel,
        (shape(half_shape), shape(half_shape)),
        (low, *rows_of, *weights),
        scratch=[pltpu.VMEM(half_shape, F32)],
        limit=16,
    )
    keep, send, other_step = call(
        readout_kernel,
        (shape((size, LANES)), shape((size, LANES), BF16), shape(half_shape)),
        (other, *rows_of, *weights, own_gated, ends, *near_out),
        scratch=[
            pltpu.VMEM(half_shape, F32),
            pltpu.VMEM((kept, channels), F32),
            fold_scratch(kept, pieces),
        ],
        limit=24,
    )
    new_state, token = call(
        state_kernel,
        (shape(ssm_state.shape, BF16), shape((8, LANES))),
        (live_counts, low, other, x_wide, own_step, other_step, log_rates, ssm_state),
        scalars=1,
        scratch=[
            pltpu.VMEM((kept, low_width), F32),
            pltpu.VMEM((kept, channels), F32),
        ],
        limit=16,
    )

    total = (keep, swap(send, 1, devices))
    for k, phase in enumerate(scatter):
        size //= len(phase) + 1
        parts = call(
            functools.partial(sum_kernel, len(total), 1 if k == 1 else 0),
            (shape((size, LANES)),) + (shape((size, LANES), BF16),) * len(phase),
            total,
            after=(token,) if k == 1 else (),
        )
        total = (parts[0],) + tuple(swap(p, s, devices) for p, s in zip(parts[1:], phase))
    mixed = call(
        last_sum_kernel,
        shape(hidden.shape, BF16),
        (hidden,) + total,
        scratch=[fold_scratch(LIVE_MAX, pieces)],
    )
    return (mixed, new_state, new_conv.transpose(1, 0, 2))


def solution(mesh):
    in_specs = (
        P(("groups", "weight"), None),
        P(),
        P(None, None, "weight"),
        P(None, "weight"),
        P("weight"),
        P("weight", None),
        P(None, "weight"),
        P("weight"),
        P(None, "weight"),
        P("weight"),
        P("weight", None),
        P("groups", None, "weight"),
        P("groups", None, "weight"),
        P("groups"),
    )
    out_specs = (
        P(("groups", "weight"), None),
        P("groups", None, "weight"),
        P("groups", None, "weight"),
    )
    return jax.shard_map(body, mesh=mesh, in_specs=in_specs, out_specs=out_specs, check_vma=False)
```

```python
import functools

import jax
import jax.numpy as jnp
from jax import lax
from jax.experimental import pallas as pl
from jax.experimental.pallas import tpu as pltpu
from jax.sharding import PartitionSpec as P

NSTATE = 16
DTR = 512
LIVE_MAX = 3
TAPS = 4
LANES = 128
MIB = 1024 * 1024
CORE_SHARE = 0.9375
FIRST_SHARE = 0.4
FIRST_COLUMNS = 5
BF16 = jnp.bfloat16
F32 = jnp.float32


def chip_steps(devices):
    steps, high = [], devices
    while high > 2:
        if high >= 8:
            steps.append((high // 4, high // 2))
            high //= 4
        else:
            steps.append((high // 2,))
            high //= 2
    steps = [tuple(step) for step in steps]
    if len(steps[-1]) == 1:
        bits = [bit for step in steps for bit in step]
        bits.sort()
        top = bits.pop()
        steps = [(top,)] + [tuple(bits[k : k + 2]) for k in range(len(bits) - 2, -1, -2)]
    return steps


def gather_phases(devices):
    whole = [step if len(step) == 1 else (sum(step), step[1], step[0]) for step in chip_steps(devices)]
    return whole + [(1,)]


def scatter_phases(devices):
    whole = [step if len(step) == 1 else (step[1], step[0], sum(step)) for step in chip_steps(devices)]
    return whole[::-1]


def sum_phases(devices):
    return [
        (step[0] + 1,) if len(step) == 1 else (step[0] + 1, step[1] + 1, sum(step))
        for step in chip_steps(devices)
    ]


def order_of(phases):
    order = [0]
    for phase in phases:
        order = order + [o ^ s for s in phase for o in order]
    return order


def spots_of(order):
    return jnp.array(
        [[o for o in order for _ in range(LIVE_MAX)], list(range(LIVE_MAX)) * len(order)],
        jnp.int32,
    )


def side(index):
    for shift in (4, 2, 1):
        index = jnp.bitwise_xor(index, lax.shift_right_logical(index, shift))
    return jnp.bitwise_and(index, 1)


def swap(value, shift, devices):
    return lax.ppermute(value, "weight", [(i, i ^ shift) for i in range(devices)])


def silu(v):
    return v / (1.0 + jnp.exp(-v))


def softplus(v):
    return jnp.maximum(v, 0.0) + jnp.log1p(jnp.exp(-jnp.abs(v)))


def vmem(count):
    return [pl.BlockSpec(memory_space=pltpu.VMEM)] * count


def shape(dims, kind=F32):
    return jax.ShapeDtypeStruct(dims, kind)


def call(kernel, outs, operands, scalars=0, far=0, scratch=(), limit=8, after=(), aliases=None, whole=False):
    many = isinstance(outs, tuple)
    return pl.pallas_call(
        kernel,
        out_shape=outs,
        in_specs=[pl.BlockSpec(memory_space=pltpu.SMEM)] * scalars
        + vmem(len(operands) - scalars - far)
        + [pl.BlockSpec(memory_space=pl.ANY)] * (far + len(after)),
        out_specs=pl.BlockSpec(memory_space=pl.ANY)
        if whole
        else tuple(vmem(len(outs)))
        if many
        else vmem(1)[0],
        scratch_shapes=list(scratch),
        input_output_aliases=aliases or {},
        compiler_params=pltpu.CompilerParams(vmem_limit_bytes=limit * MIB),
    )(*operands, *after)


def share_copies(far_ref, near_ref, sems, share):
    rows = far_ref.shape[0]
    start, end = (int(rows * part) // 8 * 8 for part in share)
    count = sems.shape[0]
    size = (end - start) // count
    spans = [pl.ds(start + size * k, size) for k in range(count)]
    return [
        pltpu.make_async_copy(far_ref.at[span], near_ref.at[span], sems.at[k])
        for k, span in enumerate(spans)
    ]


def start_all(copies):
    for copy in copies:
        copy.start()


def wait_all(copies):
    for copy in copies:
        copy.wait()


def fold(wide, fold_ref, folded_ref):
    rows, pieces = wide.shape[0], wide.shape[1] // LANES
    for c in range(pieces):
        fold_ref[pl.ds(c, rows, stride=pieces + 1), :] = wide[:, c * LANES : (c + 1) * LANES]
    for r in range(rows):
        start = r * (pieces + 1)
        folded_ref[r * pieces : (r + 1) * pieces] = fold_ref[start : start + pieces].astype(
            folded_ref.dtype
        )


def spread(folded, fold_ref, rows):
    pieces = folded.shape[0] // rows
    for r in range(rows):
        start = r * (pieces + 1)
        fold_ref[start : start + pieces] = folded[r * pieces : (r + 1) * pieces].astype(F32)
    return pieces


def fold_scratch(rows, pieces):
    return pltpu.VMEM((-(-rows // 8) * 8 * (pieces + 1) + pieces + 1, LANES), F32)


def norm_kernel(far_hidden_ref, far_gain_ref, out_ref, fold_ref, hidden_ref, gain_ref, sems):
    copies = [
        pltpu.make_async_copy(far_hidden_ref, hidden_ref, sems.at[0]),
        pltpu.make_async_copy(far_gain_ref, gain_ref, sems.at[1]),
    ]
    start_all(copies)
    wait_all(copies)
    wide = hidden_ref[...].astype(F32)[:LIVE_MAX]
    factor = lax.rsqrt(jnp.mean(wide * wide, axis=-1, keepdims=True) + 1e-05)
    fold(wide * factor * gain_ref[...], fold_ref, out_ref)


def join_kernel(count, *refs):
    start = 0
    for ref in refs[:count]:
        refs[-1][start : start + ref.shape[0]] = ref[...]
        start += ref.shape[0]


def join(parts, after=()):
    rows = sum(part.shape[0] for part in parts)
    return call(
        functools.partial(join_kernel, len(parts)),
        shape((rows, parts[0].shape[1]), parts[0].dtype),
        parts,
        after=after,
    )


def half_kernel(mine_ref, out_ref, fold_ref):
    rows = out_ref.shape[0]
    pieces = spread(mine_ref, fold_ref, rows)
    for c in range(pieces):
        out_ref[:, c * LANES : (c + 1) * LANES] = fold_ref[pl.ds(c, rows, stride=pieces + 1), :]


def unfold_kernel(half_ref, other_ref, _, out_ref, fold_ref):
    rows = half_ref.shape[0]
    pieces = spread(other_ref, fold_ref, rows)
    for c in range(pieces):
        span = slice(c * LANES, (c + 1) * LANES)
        other = fold_ref[pl.ds(c, rows, stride=pieces + 1), :]
        out_ref[:, span] = jnp.concatenate([half_ref[:, span], other], axis=0).astype(BF16)


def columns_kernel(start, far_ref, near_ref, sems):
    columns = pl.ds(start, near_ref.shape[1])
    loads = share_copies(far_ref.at[:, columns], near_ref, sems, (0, 1))
    start_all(loads)
    wait_all(loads)


def load_kernel(share, far_ref, *refs):
    near_ref, sems = refs[-2:]
    loads = share_copies(far_ref, near_ref, sems, share)
    start_all(loads)
    wait_all(loads)


def pack(low):
    coefs = low[:, DTR:]
    high = coefs.astype(BF16)
    rest = (coefs - high.astype(F32)).astype(BF16)
    return jnp.concatenate([low[:, :DTR].astype(BF16), high, rest], axis=1)


def unpack(packed):
    wide = packed.astype(F32)
    count = (wide.shape[1] - DTR) // 2
    coefs = wide[:, DTR : DTR + count] + wide[:, DTR + count :]
    return jnp.concatenate([wide[:, :DTR], coefs], axis=1)


def add_kernel(count, *refs):
    total = refs[0][...]
    for ref in refs[1:count]:
        total = total + (ref[...] if ref.dtype == F32 else unpack(ref[...]))
    refs[-2][...] = total
    refs[-1][...] = pack(total)


def places(block, turn, height, span):
    line = lax.broadcasted_iota(jnp.int32, (height, block.shape[1]), 0)
    return jnp.where(line == block * span + turn, 1.0, 0.0)


def fresh_input(both_ref, block, turn, rows, rows_dev):
    return jnp.dot(
        places(block, turn, rows, rows_dev).astype(BF16),
        both_ref[0].astype(BF16),
        preferred_element_type=F32,
    )


def conv_kernel(
    rows_dev,
    both_ref,
    spot_ref,
    conv_ref,
    taps_ref,
    offset_ref,
    coef_ref,
    keep_ref,
    send_ref,
    mixed_ref,
    low_ref,
):
    index = lax.axis_index("weight")
    rows = conv_ref.shape[1]
    kept = mixed_ref.shape[0]
    block = jnp.bitwise_xor(spot_ref[0:1, :], index)
    fresh = fresh_input(both_ref, block, spot_ref[1:2, :], rows, rows_dev)
    states = [conv_ref[k].astype(F32) for k in range(TAPS - 1)] + [fresh]
    total = states[0] * taps_ref[0:1, :]
    for k in range(1, TAPS):
        total = total + states[k] * taps_ref[k : k + 1, :]
    mixed = silu(total + offset_ref[...]).astype(BF16)
    line = lax.broadcasted_iota(jnp.int32, (kept, rows), 0)
    column = lax.broadcasted_iota(jnp.int32, (kept, rows), 1)
    chosen = (line // LIVE_MAX) * rows_dev + line % LIVE_MAX == column
    mixed = jnp.dot(
        jnp.where(chosen, 1.0, 0.0).astype(BF16), mixed, preferred_element_type=F32
    ).astype(BF16)
    mixed_ref[...] = mixed
    low_ref[...] = lax.dot_general(
        mixed, coef_ref[...], (((1,), (1,)), ((), ())), preferred_element_type=F32
    )
    half = keep_ref.shape[0]
    core = side(index)
    keep_ref[...] = low_ref[pl.ds(pl.multiple_of(core * half, 8), half), :]
    send_ref[...] = pack(low_ref[pl.ds(pl.multiple_of((1 - core) * half, 8), half), :])


def gate_kernel(live_ref, both_ref, spot_ref, mixed_ref, gate_ref, alive_ref, x_ref):
    x_ref[...] = mixed_ref[...].astype(F32)
    for b in range(live_ref.shape[0]):
        for t in range(LIVE_MAX):
            r = b * LIVE_MAX + t
            alive_ref[r : r + 1, :] = jnp.full(
                (1, LANES), jnp.where(t < live_ref[b], 1.0, 0.0)
            )
    block = jnp.bitwise_xor(spot_ref[0:1, :], lax.axis_index("weight"))
    gate_ref[...] = jnp.dot(
        places(block, spot_ref[1:2, :], gate_ref.shape[0], LIVE_MAX),
        silu(both_ref[1]),
        precision=lax.Precision.HIGHEST,
        preferred_element_type=F32,
    )


def taps_kernel(live_ref, both_ref, spot_ref, conv_ref, new_conv_ref, alive_ref):
    blocks = live_ref.shape[0]
    rows = conv_ref.shape[1]
    rows_dev = rows // blocks
    block = jnp.bitwise_xor(spot_ref[0:1, :], lax.axis_index("weight"))
    row_iota = lax.broadcasted_iota(jnp.int32, (rows_dev, LANES), 0)
    for b in range(blocks):
        alive_ref[b * rows_dev : (b + 1) * rows_dev, :] = jnp.where(
            row_iota < live_ref[b], 1.0, 0.0
        )
    alive = alive_ref[:, 0:1] > 0.0
    fresh = fresh_input(both_ref, block, spot_ref[1:2, :], rows, rows_dev)
    states = [conv_ref[k].astype(F32) for k in range(TAPS - 1)] + [fresh]
    for k in range(TAPS - 1):
        new_conv_ref[k] = jnp.where(alive, states[k + 1], states[k]).astype(BF16)


def half_rows(which, size):
    return pl.ds(pl.multiple_of(which * size, 8), size)


def join_halves(mine, other, out_ref):
    size = mine.shape[0]
    mine_side = side(lax.axis_index("weight"))
    out_ref[half_rows(mine_side, size), :] = mine
    out_ref[half_rows(1 - mine_side, size), :] = other


def gated_rows(which, low, weights, rows_refs, state_ref, read_ref):
    step_weight_ref, bias_ref, rates_ref, skip_ref = weights
    size = low.shape[0]
    x_wide, gate, alive = (ref[half_rows(which, size), :] for ref in rows_refs)
    blocks = size // LIVE_MAX
    rows_dev = state_ref.shape[0] // (2 * blocks)
    step_size = softplus(
        jnp.dot(low[:, :DTR].astype(BF16), step_weight_ref[...], preferred_element_type=F32)
        + bias_ref[...]
    )
    coefs = low[:, DTR:]
    both_coefs = jnp.sum(coefs[:, :NSTATE] * coefs[:, NSTATE:], axis=1, keepdims=True)
    out_coefs = coefs[:, NSTATE:].T
    rates = -jnp.exp(rates_ref[...])
    first = which * (blocks * rows_dev)
    for b in range(blocks):
        for t in range(LIVE_MAX):
            r = b * LIVE_MAX + t
            wide = state_ref[first + (b * rows_dev + t)].astype(F32)
            decayed = jnp.exp(step_size[r : r + 1, :] * rates) * wide
            read_ref[r : r + 1, :] = jnp.sum(
                out_coefs[:, r : r + 1] * decayed, axis=0, keepdims=True
            )
    readout = read_ref[...] + (both_coefs * step_size + skip_ref[...]) * x_wide
    return step_size, jnp.where(alive[:, 0:1] > 0.0, readout * gate, 0.0)


def own_kernel(
    low_ref,
    x_ref,
    gate_ref,
    alive_ref,
    step_weight_ref,
    bias_ref,
    rates_ref,
    skip_ref,
    state_ref,
    gated_ref,
    step_ref,
    read_ref,
):
    step_ref[...], gated_ref[...] = gated_rows(
        side(lax.axis_index("weight")),
        low_ref[...],
        (step_weight_ref, bias_ref, rates_ref, skip_ref),
        (x_ref, gate_ref, alive_ref),
        state_ref,
        read_ref,
    )


def readout_kernel(
    other_ref,
    x_ref,
    gate_ref,
    alive_ref,
    step_weight_ref,
    bias_ref,
    rates_ref,
    skip_ref,
    state_ref,
    own_ref,
    spot_ref,
    first_ref,
    last_ref,
    keep_ref,
    send_ref,
    step_ref,
    read_ref,
    gated_ref,
    fold_ref,
):
    kept = x_ref.shape[0]
    step_ref[...], gated = gated_rows(
        1 - side(lax.axis_index("weight")),
        unpack(other_ref[...]),
        (step_weight_ref, bias_ref, rates_ref, skip_ref),
        (x_ref, gate_ref, alive_ref),
        state_ref,
        read_ref,
    )
    join_halves(own_ref[...], gated, gated_ref)
    block = jnp.bitwise_xor(spot_ref[:, 0:1], lax.axis_index("weight"))
    column = lax.broadcasted_iota(jnp.int32, (kept, kept), 1)
    pick = jnp.where(column == block * LIVE_MAX + spot_ref[:, 1:2], 1.0, 0.0).astype(BF16)
    picked = jnp.dot(
        pick, gated_ref[...].astype(BF16), preferred_element_type=F32
    ).astype(BF16)
    half = kept // 2
    near = first_ref.shape[1]
    pieces = (near + last_ref.shape[1]) // LANES
    group = 4
    for c in range(0, pieces, group):
        start = c * LANES
        if start < near:
            weight = first_ref[:, start : start + group * LANES]
        else:
            weight = last_ref[:, start - near : start - near + group * LANES]
        part = jnp.dot(picked, weight, preferred_element_type=F32)
        for g in range(group):
            piece = part[:, g * LANES : (g + 1) * LANES]
            fold_ref[pl.ds(c + g, kept, stride=pieces + 1), :] = piece
    for r in range(half):
        rows = slice(r * pieces, (r + 1) * pieces)
        start = r * (pieces + 1)
        keep_ref[rows] = fold_ref[start : start + pieces]
        start = (half + r) * (pieces + 1)
        send_ref[rows] = fold_ref[start : start + pieces].astype(BF16)


def state_kernel(
    live_ref,
    mine_ref,
    other_ref,
    x_ref,
    own_step_ref,
    other_step_ref,
    rates_ref,
    state_ref,
    new_state_ref,
    token_ref,
    low_ref,
    step_ref,
):
    token_ref[...] = jnp.zeros_like(token_ref)
    blocks = live_ref.shape[0]
    rows_dev = state_ref.shape[0] // blocks
    join_halves(mine_ref[...], unpack(other_ref[...]), low_ref)
    join_halves(own_step_ref[...], other_step_ref[...], step_ref)
    in_coefs = low_ref[:, DTR : DTR + NSTATE].T
    step_size = step_ref[...]
    driven = step_size * x_ref[...]
    rates = -jnp.exp(rates_ref[...])
    for b in range(blocks):
        for t in range(LIVE_MAX):
            r = b * LIVE_MAX + t
            wide = state_ref[b * rows_dev + t].astype(F32)
            updated = (
                jnp.exp(step_size[r : r + 1, :] * rates) * wide
                + in_coefs[:, r : r + 1] * driven[r : r + 1, :]
            )
            new_state_ref[b * rows_dev + t] = jnp.where(
                t < live_ref[b], updated, wide
            ).astype(BF16)
        for t in range(LIVE_MAX, rows_dev):
            new_state_ref[b * rows_dev + t] = state_ref[b * rows_dev + t]


def sum_kernel(count, skipped, *refs):
    parts, outs = refs[:count], refs[count + skipped :]
    size = outs[0].shape[0]
    for k, out in enumerate(outs):
        rows = slice(k * size, (k + 1) * size)
        total = parts[0][rows]
        for part in parts[1:]:
            total = total + part[rows].astype(F32)
        out[...] = total.astype(out.dtype)


def last_sum_kernel(*refs):
    hidden_ref, parts, out_ref, fold_ref = refs[0], refs[1:-2], refs[-2], refs[-1]
    total = parts[0][...]
    for part in parts[1:]:
        total = total + part[...].astype(F32)
    rows = LIVE_MAX
    pieces = spread(total, fold_ref, rows)
    for c in range(pieces):
        span = slice(c * LANES, (c + 1) * LANES)
        wide = hidden_ref[:, span].astype(F32)
        own = wide[:rows] + fold_ref[pl.ds(c, rows, stride=pieces + 1), :]
        out_ref[:, span] = jnp.concatenate([own, wide[rows:]], axis=0).astype(BF16)


def body(
    hidden,
    norm_gain,
    in_weight,
    conv_weight,
    conv_offset,
    coef_weight,
    step_weight,
    step_bias,
    log_rates,
    skip_gain,
    out_weight,
    ssm_state,
    conv_state,
    live_counts,
):
    devices = lax.axis_size("weight")
    rows_dev, width = hidden.shape
    rows = devices * rows_dev
    kept = devices * LIVE_MAX
    channels = in_weight.shape[2]
    low_width = coef_weight.shape[1]
    phases = gather_phases(devices)
    spots = spots_of(order_of(phases))
    scatter = scatter_phases(devices)
    ends = spots_of(order_of(scatter[::-1] + [(1,)])).T
    pieces = width // LANES
    slab = LIVE_MAX * pieces

    weight_shape = pltpu.VMEM(in_weight.shape, BF16)

    def load(share, so_far=None):
        return call(
            functools.partial(load_kernel, share),
            weight_shape,
            (in_weight,),
            far=1,
            scratch=[pltpu.SemaphoreType.DMA((4,))],
            limit=43,
            after=() if so_far is None else (so_far,),
            whole=True,
            aliases={} if so_far is None else {1: 0},
        )

    gathered = call(
        norm_kernel,
        pltpu.VMEM((slab, LANES), BF16),
        (hidden, norm_gain.reshape(1, width)),
        far=2,
        scratch=[
            fold_scratch(LIVE_MAX, pieces),
            pltpu.VMEM(hidden.shape, BF16),
            pltpu.VMEM((1, width), F32),
            pltpu.SemaphoreType.DMA((2,)),
        ],
        limit=60,
    )
    done, near_weight = 0.0, None
    for k, phase in enumerate(phases[:-1]):
        until = CORE_SHARE if k == len(phases) - 2 else done + (CORE_SHARE - done) * FIRST_SHARE
        near_weight = load((done, until), near_weight)
        done = until
        gathered = join(
            [gathered] + [swap(gathered, s, devices) for s in phase], (near_weight,)
        )
    near_weight = load((done, 1.0), near_weight)
    folded = [fold_scratch(kept // 2, pieces)]
    half = call(half_kernel, shape((kept // 2, width)), (gathered,), scratch=folded, limit=12)
    normed = call(
        unfold_kernel,
        shape((kept, width), BF16),
        (half, swap(gathered, 1, devices)),
        scratch=folded,
        limit=12,
        after=(near_weight,),
    )
    both = jnp.einsum("rd,dbc->brc", normed, near_weight, preferred_element_type=F32)

    conv_turned = conv_state.transpose(1, 0, 2)
    keep, send, mixed_x = call(
        functools.partial(conv_kernel, rows_dev),
        (
            shape((kept // 2, low_width)),
            shape((kept // 2, low_width + 2 * NSTATE), BF16),
            shape((kept, channels), BF16),
        ),
        (
            both,
            spots,
            conv_turned,
            conv_weight,
            conv_offset.reshape(1, channels),
            coef_weight.T,
        ),
        scratch=[pltpu.VMEM((kept, low_width), F32)],
        limit=16,
    )
    gate, alive, x_wide = call(
        gate_kernel,
        (shape((kept, channels)), shape((kept, LANES)), shape((kept, channels))),
        (live_counts, both, spots, mixed_x),
        scalars=1,
    )
    new_conv = call(
        taps_kernel,
        shape((TAPS - 1, rows, channels), BF16),
        (live_counts, both, spots, conv_turned),
        scalars=1,
        scratch=[pltpu.VMEM((rows, LANES), F32)],
    )

    packed_width = low_width + 2 * NSTATE

    def add(*parts, after=()):
        return call(
            functools.partial(add_kernel, len(parts)),
            (shape(parts[0].shape), shape((kept // 2, packed_width), BF16)),
            parts,
            after=after,
        )

    low, packed = add(keep, swap(send, 1, devices), after=(gate,))
    exchanges = sum_phases(devices)
    first_columns = width * FIRST_COLUMNS // 16 if len(exchanges) > 1 else width // 2
    near_out = [
        call(
            functools.partial(columns_kernel, start),
            pltpu.VMEM((channels, count), BF16),
            (out_weight,),
            far=1,
            scratch=[pltpu.SemaphoreType.DMA((4,))],
            limit=50,
            whole=True,
        )
        for start, count in ((0, first_columns), (first_columns, width - first_columns))
    ]
    for k, phase in enumerate(exchanges):
        after = (near_out[0],) if k == 0 else (near_out[1],)
        low, packed = add(low, *[swap(packed, s, devices) for s in phase], after=after)
    other = swap(packed, 1, devices)

    size = kept // 2 * pieces
    rows_of = (x_wide, gate, alive)
    weights = (
        step_weight,
        step_bias.reshape(1, channels),
        log_rates,
        skip_gain.reshape(1, channels),
        ssm_state,
    )
    half_shape = (kept // 2, channels)
    own_gated, own_step = call(
        own_kernel,
        (shape(half_shape), shape(half_shape)),
        (low, *rows_of, *weights),
        scratch=[pltpu.VMEM(half_shape, F32)],
        limit=16,
    )
    keep, send, other_step = call(
        readout_kernel,
        (shape((size, LANES)), shape((size, LANES), BF16), shape(half_shape)),
        (other, *rows_of, *weights, own_gated, ends, *near_out),
        scratch=[
            pltpu.VMEM(half_shape, F32),
            pltpu.VMEM((kept, channels), F32),
            fold_scratch(kept, pieces),
        ],
        limit=24,
    )
    new_state, token = call(
        state_kernel,
        (shape(ssm_state.shape, BF16), shape((8, LANES))),
        (live_counts, low, other, x_wide, own_step, other_step, log_rates, ssm_state),
        scalars=1,
        scratch=[
            pltpu.VMEM((kept, low_width), F32),
            pltpu.VMEM((kept, channels), F32),
        ],
        limit=16,
    )

    total = (keep, swap(send, 1, devices))
    for k, phase in enumerate(scatter):
        size //= len(phase) + 1
        parts = call(
            functools.partial(sum_kernel, len(total), 1 if k == 1 else 0),
            (shape((size, LANES)),) + (shape((size, LANES), BF16),) * len(phase),
            total,
            after=(token,) if k == 1 else (),
        )
        total = (parts[0],) + tuple(swap(p, s, devices) for p, s in zip(parts[1:], phase))
    mixed = call(
        last_sum_kernel,
        shape(hidden.shape, BF16),
        (hidden,) + total,
        scratch=[fold_scratch(LIVE_MAX, pieces)],
    )
    return (mixed, new_state, new_conv.transpose(1, 0, 2))


def solution(mesh):
    in_specs = (
        P(("groups", "weight"), None),
        P(),
        P(None, None, "weight"),
        P(None, "weight"),
        P("weight"),
        P("weight", None),
        P(None, "weight"),
        P("weight"),
        P(None, "weight"),
        P("weight"),
        P("weight", None),
        P("groups", None, "weight"),
        P("groups", None, "weight"),
        P("groups"),
    )
    out_specs = (
        P(("groups", "weight"), None),
        P("groups", None, "weight"),
        P("groups", None, "weight"),
    )
    return jax.shard_map(body, mesh=mesh, in_specs=in_specs, out_specs=out_specs, check_vma=False)
```
